32 devices in a mesh: tile: 8 (over z, y), band: 4 (over x, core).
Axes of the slice: x: 2, y: 2, z: 4, core: 2. Of those that a mesh axis runs over, the one named last changes fastest.
Arguments:
- points: float32 [8192, 3, 128], P(('tile', 'band')), may hold values from -6 to 6
- normals: float32 [8192, 3, 128], P(('tile', 'band')), may hold values from -4 to 4
- poses: float32 [6, 256], P(None, ('tile', 'band')), may hold values from -4 to 4
- directions: float32 [2, 6, 256], P(None, None, ('tile', 'band')), may hold values from -6 to 6
- local_pairs: int32 [2, 8192], P(None, ('tile', 'band')), may hold values from 0 to 255
- local_maps: int32 [8192, 128], P(('tile', 'band')), may hold values from 0 to 127
- remote_src: int32 [32, 256], P(('tile', 'band')), may hold values from 0 to 255
- remote_maps: int32 [32, 256, 128], P(('tile', 'band')), may hold values from 0 to 127
- remote_dst: int32 [32, 256], P(('tile', 'band')), may hold values from 0 to 255
- counts: int32 [32, 32], P(('tile', 'band')), may hold values from 4 to 8, as said below
Outputs:
- gradient: float32 [6, 256], P(None, ('tile', 'band'))
- hess_products: float32 [2, 6, 256], P(None, None, ('tile', 'band'))
The draws below stay inside these ranges and needn't reach their ends.
Inputs may be any that keep to these rules, and one draw needn't show every extreme that they name: `counts`: in every row some device pair uses all 8 slots.
All inputs are finite; a program needn't handle non-finite values.
Results may differ from the reference program's by a relative error of at most 0.0003.
Values sent between devices are 32-bit elements; how exact they have to be, the bound alone decides.
No kernel may reach another device: no remote copies, remote signals or barrier semaphores. Data moves between devices by JAX's collectives and lax.ppermute only.
A program may use at most 64 MiB of HBM per device.

```python
import jax
import jax.numpy as jnp
from jax import lax

F_DEV = 8
BF = 32
PB = 128
NLOC = 256
CAP = 8
NBL = 256
FRAGS = 256
BLOCKS = 8192
N_TILE = 8
N_BAND = 4


def draw_counts(key, part):
    devices = N_TILE * N_BAND
    key_base, key_full = jax.random.split(key)
    counts_base = jax.random.randint(key_base, (devices, devices), CAP // 2, CAP + 1)
    full_peer = jax.random.randint(key_full, (devices,), 0, devices)
    return jnp.where(jnp.arange(devices)[None, :] == full_peer[:, None], CAP, counts_base).astype(jnp.int32)


def plant(values, stream_key, smallest, largest):
    extent = values.shape
    place = [jax.random.randint(jax.random.fold_in(stream_key, axis), (), 0, extent[axis]) for axis in range(len(extent))]
    values = values.at[tuple(place)].set(smallest)
    longest = extent.index(max(extent))
    place[longest] = (place[longest] + 1) % extent[longest]
    return values.at[tuple(place)].set(largest)


def levels(rng, shape, cuts, smallest, largest):
    gain = 1.0
    for dim, blocks in cuts:
        heights = jax.random.uniform(jax.random.fold_in(jax.random.fold_in(rng, 6), dim), (blocks,), jnp.float32, smallest / len(cuts), largest / len(cuts))
        gain = gain * jnp.repeat(jnp.exp(heights), shape[dim] // blocks).reshape((-1,) + (1,) * (len(shape) - 1 - dim))
    return gain


def scatter_about(stream_key, extent, scale, limit, pieces=(), held_as=jnp.bfloat16):
    entries = jax.random.normal(stream_key, extent, jnp.float32) * scale
    if len(pieces) > 0:
        entries = levels(stream_key, extent, pieces, -0.22, 0.18) * entries
    return jnp.clip(entries, min=-limit, max=limit).astype(held_as)


def setup_inputs(seed: int = 0) -> dict:
    streams_of = jax.random.split(jax.random.key(seed), 11)
    return {
        "points": scatter_about(streams_of[0], (BLOCKS, 3, PB), 1.0, 6.0, ((0, 32),), jnp.float32),
        "normals": scatter_about(streams_of[1], (BLOCKS, 3, PB), 0.6, 4.0, ((0, 32),), jnp.float32),
        "poses": scatter_about(streams_of[2], (6, FRAGS), 0.6, 4.0, ((1, 32),), jnp.float32),
        "directions": scatter_about(streams_of[3], (2, 6, FRAGS), 1.0, 6.0, ((2, 32),), jnp.float32),
        "local_pairs": plant(jax.random.randint(streams_of[4], (2, NLOC * N_TILE * N_BAND), 0, NBL), jax.random.fold_in(streams_of[4], 1), 0, NBL - 1).astype(jnp.int32),
        "local_maps": plant(jax.random.randint(streams_of[5], (NLOC * N_TILE * N_BAND, PB), 0, PB), jax.random.fold_in(streams_of[5], 1), 0, PB - 1).astype(jnp.int32),
        "remote_src": plant(jax.random.randint(streams_of[6], (N_TILE * N_BAND, N_TILE * N_BAND * CAP), 0, NBL), jax.random.fold_in(streams_of[6], 1), 0, NBL - 1).astype(jnp.int32),
        "remote_maps": plant(jax.random.randint(streams_of[7], (N_TILE * N_BAND, N_TILE * N_BAND * CAP, PB), 0, PB), jax.random.fold_in(streams_of[7], 1), 0, PB - 1).astype(jnp.int32),
        "remote_dst": plant(jax.random.randint(streams_of[8], (N_TILE * N_BAND, N_TILE * N_BAND * CAP), 0, NBL), jax.random.fold_in(streams_of[8], 1), 0, NBL - 1).astype(jnp.int32),
        "counts": draw_counts(jax.random.fold_in(streams_of[10], 71), 0),
    }


def rotations(poses):
    half_angle = poses[0:3] * 0.5
    inverse = 1.0 / jnp.sqrt(1.0 + half_angle[0] * half_angle[0] + half_angle[1] * half_angle[1] + half_angle[2] * half_angle[2])
    quat_w = inverse
    quat_x = half_angle[0] * inverse
    quat_y = half_angle[1] * inverse
    quat_z = half_angle[2] * inverse
    rotation = [[1.0 - 2.0 * (quat_y * quat_y + quat_z * quat_z), 2.0 * (quat_x * quat_y - quat_w * quat_z), 2.0 * (quat_x * quat_z + quat_w * quat_y)], [2.0 * (quat_x * quat_y + quat_w * quat_z), 1.0 - 2.0 * (quat_x * quat_x + quat_z * quat_z), 2.0 * (quat_y * quat_z - quat_w * quat_x)], [2.0 * (quat_x * quat_z - quat_w * quat_y), 2.0 * (quat_y * quat_z + quat_w * quat_x), 1.0 - 2.0 * (quat_x * quat_x + quat_y * quat_y)]]
    return (rotation, poses[3:6])

def to_world(points, normals, poses, per_pose):
    rotation, translation = rotations(poses)

    def spread(values):
        return jnp.repeat(values, per_pose)[:, None]
    world_rows = []
    normal_rows = []
    for i in range(3):
        coeffs = [spread(rotation[i][j]) for j in range(3)]
        world_rows.append(coeffs[0] * points[:, 0] + coeffs[1] * points[:, 1] + coeffs[2] * points[:, 2] + spread(translation[i]))
        normal_rows.append(coeffs[0] * normals[:, 0] + coeffs[1] * normals[:, 1] + coeffs[2] * normals[:, 2])
    return (jnp.stack(world_rows, axis=1), jnp.stack(normal_rows, axis=1))

def cross_rows(left, right):
    return [left[:, 1] * right[:, 2] - left[:, 2] * right[:, 1], left[:, 2] * right[:, 0] - left[:, 0] * right[:, 2], left[:, 0] * right[:, 1] - left[:, 1] * right[:, 0]]

def pick_points(world_pts, normal_pts, point_maps):
    index = jnp.broadcast_to(point_maps[:, None, :], world_pts.shape)
    return (jnp.take_along_axis(world_pts, index, axis=2), jnp.take_along_axis(normal_pts, index, axis=2))

def pair_terms(world_a, world_b, normal_b, dirs_a, dirs_b, valid_mask, blocks_frag):
    count = world_a.shape[2]
    offset = world_a - world_b
    residual = (normal_b[:, 0] * offset[:, 0] + normal_b[:, 1] * offset[:, 1] + normal_b[:, 2] * offset[:, 2]) * valid_mask[:, None]
    normal_list = [normal_b[:, 0], normal_b[:, 1], normal_b[:, 2]]
    jac_a = jnp.stack(cross_rows(world_a, normal_b) + normal_list, axis=1)
    jac_b = -jnp.stack(cross_rows(world_b, normal_b) + normal_list, axis=1)
    grad_scale = 1.0 / count
    hess_scale = 1.0 / (count * blocks_frag)
    parts_a = [lax.optimization_barrier(jnp.sum(residual[:, None] * jac_a, axis=2)) * grad_scale]
    parts_b = [lax.optimization_barrier(jnp.sum(residual[:, None] * jac_b, axis=2)) * grad_scale]
    for v in range(2):
        along_dir = (lax.optimization_barrier(jnp.sum(jac_a * dirs_a[:, 6 * v:6 * v + 6, None], axis=1)) + lax.optimization_barrier(jnp.sum(jac_b * dirs_b[:, 6 * v:6 * v + 6, None], axis=1))) * valid_mask[:, None]
        parts_a.append(lax.optimization_barrier(jnp.sum(along_dir[:, None] * jac_a, axis=2)) * hess_scale)
        parts_b.append(lax.optimization_barrier(jnp.sum(along_dir[:, None] * jac_b, axis=2)) * hess_scale)
    return (jnp.concatenate(parts_a, axis=1), jnp.concatenate(parts_b, axis=1))

def reference(points, normals, poses, directions, local_pairs, local_maps, remote_src, remote_maps, remote_dst, counts):
    devices = N_TILE * N_BAND
    blocks_dev = F_DEV * BF
    frag_total = F_DEV * devices
    world_pts, normal_pts = to_world(points, normals, poses, BF)
    frag_dirs = directions.reshape(12, frag_total).T
    slot_iota = jnp.arange(CAP, dtype=jnp.int32)
    peer_iota = jnp.arange(devices, dtype=jnp.int32)
    local_ones = jnp.ones((NLOC,), jnp.float32)

    def step(totals, device):
        block_base = device * blocks_dev
        local_idx = lax.dynamic_slice_in_dim(local_pairs, device * NLOC, NLOC, 1)
        point_maps = lax.dynamic_slice_in_dim(local_maps, device * NLOC, NLOC, 0)
        source = block_base + local_idx[0]
        target = block_base + local_idx[1]
        world_b, normal_b = pick_points(world_pts[target], normal_pts[target], point_maps)
        terms_a, terms_b = pair_terms(world_pts[source], world_b, normal_b, frag_dirs[source // BF], frag_dirs[target // BF], local_ones, BF)
        totals = totals.at[source // BF].add(terms_a).at[target // BF].add(terms_b)
        source = block_base + lax.dynamic_index_in_dim(remote_src, device, 0, keepdims=False)
        point_maps = lax.dynamic_index_in_dim(remote_maps, device, 0, keepdims=False)
        target = (lax.dynamic_slice_in_dim(remote_dst, device * CAP, CAP, 1) + (peer_iota * blocks_dev)[:, None]).reshape(-1)
        used_slots = lax.dynamic_index_in_dim(counts, device, 0, keepdims=False)
        valid_mask = (slot_iota[None, :] < used_slots[:, None]).astype(jnp.float32).reshape(-1)
        world_b, normal_b = pick_points(world_pts[target], normal_pts[target], point_maps)
        terms_a, terms_b = pair_terms(world_pts[source], world_b, normal_b, frag_dirs[source // BF], frag_dirs[target // BF], valid_mask, BF)
        totals = totals.at[source // BF].add(terms_a).at[target // BF].add(terms_b)
        return (totals, None)
    totals, unused = lax.scan(step, jnp.zeros((frag_total, 18), jnp.float32), jnp.arange(devices, dtype=jnp.int32))
    gradient = totals[:, 0:6].T
    hess_products = totals[:, 6:18].T.reshape(2, 6, frag_total)
    return (gradient, hess_products)
```

```python
import functools

import jax
import jax.numpy as jnp
from jax import lax
from jax.experimental import pallas as pl
from jax.experimental.pallas import tpu as pltpu
from jax.sharding import PartitionSpec as P

AXES = ("tile", "band")
SUB = 8
LANE = 128
MSG = 4 * SUB + 1
STAGE = 6 * SUB
GROUP = 16
VMEM_LIMIT = 16 * 1024 * 1024


def iota(axis):
    return lax.broadcasted_iota(jnp.int32, (SUB, LANE), axis)


def pick(values, index):
    values = jnp.broadcast_to(values, (SUB, LANE))
    return jnp.take_along_axis(values, index, axis=1, mode="promise_in_bounds")


def shift_of(size):
    shift = size.bit_length() - 1
    assert 1 << shift == size
    return shift


def rotations(poses):
    half = [poses[i : i + 1, :] * 0.5 for i in range(3)]
    w = 1.0 / jnp.sqrt(1.0 + half[0] * half[0] + half[1] * half[1] + half[2] * half[2])
    x, y, z = half[0] * w, half[1] * w, half[2] * w
    rotation = [
        [1.0 - 2.0 * (y * y + z * z), 2.0 * (x * y - w * z), 2.0 * (x * z + w * y)],
        [2.0 * (x * y + w * z), 1.0 - 2.0 * (x * x + z * z), 2.0 * (y * z - w * x)],
        [2.0 * (x * z - w * y), 2.0 * (y * z + w * x), 1.0 - 2.0 * (x * x + y * y)],
    ]
    return rotation, [poses[i : i + 1, :] for i in range(3, 6)]


def write_world(points, normals, poses, world):
    blocks, frags = points.shape[1], poses.shape[1]
    per_frag = blocks // frags
    stride = world.shape[0] // (3 if normals is None else 6)
    rotation, translation = rotations(poses[...])

    def spread(row, f):
        return jnp.broadcast_to(row[:, f : f + 1], (SUB, LANE))

    for f in range(frags):
        turn = [[spread(rotation[i][j], f) for j in range(3)] for i in range(3)]
        move = [spread(translation[i], f) for i in range(3)]
        for b in range(f * per_frag, (f + 1) * per_frag, SUB):
            x = [points[j, b : b + SUB, :] for j in range(3)]
            for i in range(3):
                world[pl.ds(i * stride + b, SUB), :] = (
                    turn[i][0] * x[0] + turn[i][1] * x[1] + turn[i][2] * x[2] + move[i]
                )
            if normals is not None:
                n = [normals[j, b : b + SUB, :] for j in range(3)]
                for i in range(3):
                    world[pl.ds((3 + i) * stride + b, SUB), :] = (
                        turn[i][0] * n[0] + turn[i][1] * n[1] + turn[i][2] * n[2]
                    )


def write_directions(directions, table):
    frags = directions.shape[2]
    for v in range(2):
        for j in range(6):
            table[6 * v + j : 6 * v + j + 1, 0:frags] = directions[j, v : v + 1, :]


def index_tile(row_ref, first, offset):
    tile = pl.multiple_of(first // LANE * LANE, LANE)
    return pick(row_ref[0:1, pl.ds(tile, LANE)], offset + lax.rem(first, LANE))


def pack_kernel(points, poses, directions, src_s, src_v, maps, counts, out, world, table, used):
    devices = counts.shape[1]
    per_frag = points.shape[1] // poses.shape[1]
    write_world(points, None, poses, world)
    stride = world.shape[0] // 3
    write_directions(directions, table)
    used[0:1, 0:devices] = counts[...]

    def peer(p, carry):
        for s in range(SUB):
            block = src_s[0, p * SUB + s]
            out[pl.ds(p * MSG + s, 3, stride=SUB), :] = world[pl.ds(block, 3, stride=stride), :]
        rows = maps[pl.ds(pl.multiple_of(p * SUB, SUB), SUB), :]
        out[pl.ds(p * MSG + 3 * SUB, SUB), :] = rows.astype(jnp.float32)
        return carry

    lax.fori_loop(0, devices, peer, 0, unroll=4)
    slot = lax.shift_right_logical(iota(1), shift_of(GROUP))
    field = lax.bitwise_and(iota(1), GROUP - 1)
    for q in range(0, devices, SUB):
        block = index_tile(src_v, q * SUB, iota(0) * SUB + slot)
        frag = lax.shift_right_logical(block, shift_of(per_frag))
        limit = pick(used[0:1, :], iota(0) + q)
        extras = jnp.where(slot < limit, 1.0, 0.0)
        for j in range(12):
            extras = jnp.where(field == j, pick(table[j : j + 1, :], frag), extras)
        out[pl.ds(q * MSG + MSG - 1, SUB, stride=MSG), :] = extras


def cross(left, right):
    return [
        left[1] * right[2] - left[2] * right[1],
        left[2] * right[0] - left[0] * right[2],
        left[0] * right[1] - left[1] * right[0],
    ]


def dot3(left, right):
    return left[0] * right[0] + left[1] * right[1] + left[2] * right[2]


def pair_sums(x, y, n, dirs_a, dirs_b):
    p, q = cross(x, n), cross(y, n)
    scalars = [dot3(n, [x[i] - y[i] for i in range(3)])]
    for v in range(2):
        a, b = dirs_a[6 * v : 6 * v + 6], dirs_b[6 * v : 6 * v + 6]
        slide = [a[3 + i] - b[3 + i] for i in range(3)]
        scalars.append(dot3(p, a) - dot3(q, b) + dot3(n, slide))
    lane = iota(1)
    result = jnp.zeros((SUB, LANE), jnp.float32)
    for k, s in enumerate(scalars):
        for c in range(3):
            for at, value in ((6 * k + c, p[c]), (6 * k + 3 + c, n[c]), (18 + 3 * k + c, q[c])):
                total = jnp.sum(s * value, axis=1, keepdims=True)
                result = jnp.where(lane == at, total, result)
    return result


def frag_sums(row_ref, row, sums, per_frag):
    pairs = sums.shape[0]
    frag = lax.shift_right_logical(row_ref[row : row + 1, :], shift_of(per_frag))
    hot = jnp.broadcast_to(frag, (SUB, pairs)) == lax.broadcasted_iota(jnp.int32, (SUB, pairs), 0)
    return jnp.dot(
        hot.astype(jnp.float32),
        sums[...],
        precision=lax.Precision.HIGHEST,
        preferred_element_type=jnp.float32,
    )


def target_side(sums):
    lane = iota(1)
    k = (lane >= 6).astype(jnp.int32) + (lane >= 12).astype(jnp.int32)
    c = lane - 6 * k
    index = jnp.where(c < 3, 18 + 3 * k + c, lane)
    return -pick(sums, jnp.where(lane < 18, index, LANE - 1))


def local_kernel(
    points, normals, poses, directions, pairs_s, pairs_v, maps, dst_s,
    staged, totals, world, table, sources, targets, sums,
):
    per_frag = points.shape[1] // poses.shape[1]
    groups = pairs_s.shape[1] // SUB
    write_world(points, normals, poses, world)
    stride = world.shape[0] // 6
    write_directions(directions, table)

    def stage_remote(g, carry):
        for s in range(SUB):
            block = dst_s[0, g * SUB + s]
            staged[pl.ds(g * STAGE + s, 6, stride=SUB), :] = world[pl.ds(block, 6, stride=stride), :]
        return carry

    lax.fori_loop(0, dst_s.shape[1] // SUB, stage_remote, 0, unroll=4)

    def stage_local(g, carry):
        for s in range(SUB):
            source, target = pairs_s[0, g * SUB + s], pairs_s[1, g * SUB + s]
            sources[pl.ds(g * 3 * SUB + s, 3, stride=SUB), :] = world[pl.ds(source, 3, stride=stride), :]
            targets[pl.ds(g * STAGE + s, 6, stride=SUB), :] = world[pl.ds(target, 6, stride=stride), :]
        return carry

    lax.fori_loop(0, groups, stage_local, 0, unroll=4)

    def group(g, carry):
        first = pl.multiple_of(g * SUB, SUB)
        index = maps[pl.ds(first, SUB), :]
        x = [sources[pl.ds(pl.multiple_of(g * 3 * SUB, SUB) + SUB * i, SUB), :] for i in range(3)]
        yn = [
            pick(targets[pl.ds(pl.multiple_of(g * STAGE, SUB) + SUB * i, SUB), :], index)
            for i in range(6)
        ]
        dirs = []
        for end in range(2):
            block = index_tile(pairs_v.at[end : end + 1], first, iota(0))
            frag = lax.shift_right_logical(block, shift_of(per_frag))
            dirs.append([pick(table[j : j + 1, :], frag) for j in range(12)])
        sums[pl.ds(first, SUB), :] = pair_sums(x, yn[0:3], yn[3:6], dirs[0], dirs[1])
        return carry

    lax.fori_loop(0, groups, group, 0, unroll=2)
    totals[...] = frag_sums(pairs_v, 0, sums, per_frag) + target_side(
        frag_sums(pairs_v, 1, sums, per_frag)
    )


def remote_kernel(arrived, staged, directions, dst_v, totals_in, back, totals, table, sums, *, per_frag):
    devices = arrived.shape[0] // MSG
    write_directions(directions, table)
    slot = lax.shift_right_logical(iota(1), shift_of(GROUP))
    field = lax.bitwise_and(iota(1), GROUP - 1)
    own = slot == iota(0)

    def peer(d, carry):
        base = d * MSG
        first = pl.multiple_of(d * SUB, SUB)
        x = [arrived[pl.ds(base + SUB * i, SUB), :] for i in range(3)]
        index = arrived[pl.ds(base + 3 * SUB, SUB), :].astype(jnp.int32)
        extras = arrived[pl.ds(base + 4 * SUB, 1), :]
        yn = [
            pick(staged[pl.ds(pl.multiple_of(d * STAGE, SUB) + SUB * i, SUB), :], index)
            for i in range(6)
        ]
        dirs_a = [pick(extras, iota(0) * GROUP + j) for j in range(12)]
        valid = pick(extras, iota(0) * GROUP + 12)
        frag = lax.shift_right_logical(index_tile(dst_v, first, iota(0)), shift_of(per_frag))
        dirs_b = [pick(table[j : j + 1, :], frag) for j in range(12)]
        n = [yn[3 + i] * valid for i in range(3)]
        result = pair_sums(x, yn[0:3], n, dirs_a, dirs_b)
        sums[pl.ds(first, SUB), :] = result
        for half in range(2):
            spread = pick(result, field + half * GROUP)
            back[pl.ds(2 * d + half, 1), :] = jnp.sum(
                jnp.where(own, spread, 0.0), axis=0, keepdims=True
            )
        return carry

    lax.fori_loop(0, devices, peer, 0, unroll=2)
    totals[...] = totals_in[...] + target_side(frag_sums(dst_v, 0, sums, per_frag))


def final_kernel(back, totals, src_v, gradient, hess, *, per_frag):
    devices = back.shape[0] // 2
    slot = lax.shift_right_logical(iota(1), shift_of(GROUP))
    sums = [[jnp.zeros((SUB, LANE), jnp.float32) for half in range(2)] for f in range(SUB)]
    for q in range(0, devices, SUB):
        block = index_tile(src_v, q * SUB, iota(0) * SUB + slot)
        frag = lax.shift_right_logical(block, shift_of(per_frag))
        for half in range(2):
            rows = back[pl.ds(2 * q + half, SUB, stride=2), :]
            for f in range(SUB):
                sums[f][half] = sums[f][half] + jnp.where(frag == f, rows, 0.0)
    halves = []
    for half in range(2):
        tile = jnp.zeros((SUB, LANE), jnp.float32)
        for f in range(SUB):
            tile = jnp.where(iota(0) == f, jnp.sum(sums[f][half], axis=0, keepdims=True), tile)
        for step in (64, 32, 16):
            tile = tile + pltpu.roll(tile, step, 1)
        halves.append(tile)
    lane = iota(1)
    total = totals[...] + jnp.where(lane < GROUP, halves[0], jnp.where(lane < 18, halves[1], 0.0))
    total = total.T
    gradient[...] = total[0:6, :] * (1.0 / LANE)
    for v in range(2):
        part = total[6 + 6 * v : 12 + 6 * v, :] * (1.0 / (LANE * per_frag))
        for j in range(6):
            hess[j, v : v + 1, :] = part[j : j + 1, :]


def call(kernel, outs, scratch, spaces, **more):
    return pl.pallas_call(
        kernel,
        out_shape=outs,
        in_specs=[pl.BlockSpec(memory_space=pltpu.SMEM if s else pltpu.VMEM) for s in spaces],
        out_specs=[pl.BlockSpec(memory_space=pltpu.VMEM)] * len(outs),
        scratch_shapes=scratch,
        compiler_params=pltpu.CompilerParams(vmem_limit_bytes=VMEM_LIMIT),
        **more,
    )


def exchange(rows, devices):
    sent = rows.reshape(devices, 1, -1)
    sent = lax.all_to_all(sent, AXES, split_axis=0, concat_axis=0, tiled=True)
    return sent.reshape(rows.shape)


def local(
    points, normals, poses, directions, local_pairs, local_maps,
    remote_src, remote_maps, remote_dst, counts,
):
    devices = lax.axis_size("tile") * lax.axis_size("band")
    blocks, _, count = points.shape
    frags = poses.shape[1]
    slots = remote_src.shape[1]
    pairs = local_pairs.shape[1]
    assert count == LANE and frags == SUB and slots == devices * SUB and devices <= LANE
    per_frag = blocks // frags
    stride = blocks + SUB
    f32 = jnp.float32
    points = points.transpose(1, 0, 2)
    normals = normals.transpose(1, 0, 2)
    directions = directions.transpose(1, 0, 2)

    def array(*shape):
        return jax.ShapeDtypeStruct(shape, f32)

    table = pltpu.VMEM((2 * SUB, LANE), f32)
    (message,) = call(
        pack_kernel,
        [array(devices * MSG, LANE)],
        [pltpu.VMEM((3 * stride, LANE), f32), table, pltpu.VMEM((SUB, LANE), jnp.int32)],
        [0, 0, 0, 1, 0, 0, 0],
    )(points, poses, directions, remote_src, remote_src, remote_maps[0], counts)
    arrived = exchange(message, devices)
    staged, totals = call(
        local_kernel,
        [array(devices * STAGE, LANE), array(SUB, LANE)],
        [
            pltpu.VMEM((6 * stride, LANE), f32),
            table,
            pltpu.VMEM((pairs * 3, LANE), f32),
            pltpu.VMEM((pairs * 6, LANE), f32),
            pltpu.VMEM((pairs, LANE), f32),
        ],
        [0, 0, 0, 0, 1, 0, 0, 1],
        cost_estimate=pl.CostEstimate(
            flops=200 * pairs * LANE, bytes_accessed=4_000_000, transcendentals=0
        ),
    )(points, normals, poses, directions, local_pairs, local_pairs, local_maps, remote_dst)
    back, totals = call(
        functools.partial(remote_kernel, per_frag=per_frag),
        [array(devices * 2, LANE), array(SUB, LANE)],
        [table, pltpu.VMEM((slots, LANE), f32)],
        [0, 0, 0, 0, 0],
    )(arrived, staged, directions, remote_dst, totals)
    back = exchange(back, devices)
    gradient, hess = call(
        functools.partial(final_kernel, per_frag=per_frag),
        [array(6, frags), array(6, 2, frags)],
        [],
        [0, 0, 0],
    )(back, totals, remote_src)
    return (gradient, hess.transpose(1, 0, 2))


def solution(mesh):
    placed = (
        P(AXES, None, None),
        P(AXES, None, None),
        P(None, AXES),
        P(None, None, AXES),
        P(None, AXES),
        P(AXES, None),
        P(AXES, None),
        P(AXES, None, None),
        P(AXES, None),
        P(AXES, None),
    )
    return jax.shard_map(
        local,
        mesh=mesh,
        in_specs=placed,
        out_specs=(P(None, AXES), P(None, None, AXES)),
        check_vma=False,
    )
```

```python
import functools

import jax
import jax.numpy as jnp
from jax import lax
from jax.experimental import pallas as pl
from jax.experimental.pallas import tpu as pltpu
from jax.sharding import PartitionSpec as P

AXES = ("tile", "band")
SUB = 8
LANE = 128
MSG = 4 * SUB + 1
TARGET = 8 * SUB
SOURCE = 9 * SUB
TOGETHER = 4
GROUP = 16
VMEM_LIMIT = 16 * 1024 * 1024


def iota(axis):
    return lax.broadcasted_iota(jnp.int32, (SUB, LANE), axis)


def pick(values, index):
    values = jnp.broadcast_to(values, (SUB, LANE))
    return jnp.take_along_axis(values, index, axis=1, mode="promise_in_bounds")


def shift_of(size):
    shift = size.bit_length() - 1
    assert 1 << shift == size
    return shift


def rotations(poses):
    half = [poses[i : i + 1, :] * 0.5 for i in range(3)]
    w = 1.0 / jnp.sqrt(1.0 + half[0] * half[0] + half[1] * half[1] + half[2] * half[2])
    x, y, z = half[0] * w, half[1] * w, half[2] * w
    rotation = [
        [1.0 - 2.0 * (y * y + z * z), 2.0 * (x * y - w * z), 2.0 * (x * z + w * y)],
        [2.0 * (x * y + w * z), 1.0 - 2.0 * (x * x + z * z), 2.0 * (y * z - w * x)],
        [2.0 * (x * z - w * y), 2.0 * (y * z + w * x), 1.0 - 2.0 * (x * x + y * y)],
    ]
    return rotation, [poses[i : i + 1, :] for i in range(3, 6)]


def cross(left, right):
    return [
        left[1] * right[2] - left[2] * right[1],
        left[2] * right[0] - left[0] * right[2],
        left[0] * right[1] - left[1] * right[0],
    ]


def dot3(left, right):
    return left[0] * right[0] + left[1] * right[1] + left[2] * right[2]


def spread(row, f):
    return jnp.broadcast_to(row[:, f : f + 1], (SUB, LANE))


def write_points(points, poses, world):
    blocks, frags = points.shape[1], poses.shape[1]
    per_frag, stride = blocks // frags, blocks + SUB
    rotation, translation = rotations(poses[...])
    for f in range(frags):
        turn = [[spread(rotation[i][j], f) for j in range(3)] for i in range(3)]
        move = [spread(translation[i], f) for i in range(3)]
        for b in range(f * per_frag, (f + 1) * per_frag, SUB):
            x = [points[j, b : b + SUB, :] for j in range(3)]
            for i in range(3):
                world[pl.ds(i * stride + b, SUB), :] = dot3(turn[i], x) + move[i]


def write_fields(points, normals, poses, directions, world):
    blocks, frags = points.shape[1], poses.shape[1]
    per_frag, stride = blocks // frags, blocks + SUB
    rotation, translation = rotations(poses[...])
    for f in range(frags):
        turn = [[spread(rotation[i][j], f) for j in range(3)] for i in range(3)]
        move = [spread(translation[i], f) for i in range(3)]
        way = [[spread(directions[j, v : v + 1, :], f) for j in range(6)] for v in range(2)]
        for b in range(f * per_frag, (f + 1) * per_frag, SUB):
            x = [points[j, b : b + SUB, :] for j in range(3)]
            m = [normals[j, b : b + SUB, :] for j in range(3)]
            y = [dot3(turn[i], x) + move[i] for i in range(3)]
            n = [dot3(turn[i], m) for i in range(3)]
            speed = []
            for v in range(2):
                swing = cross(way[v][0:3], y)
                speed.append([swing[i] + way[v][3 + i] for i in range(3)])
            along = [dot3(n, speed[v]) for v in range(2)]
            for i, row in enumerate(y + n + along + speed[0] + speed[1]):
                world[pl.ds(i * stride + b, SUB), :] = row


def index_tile(row_ref, first, offset):
    tile = first // LANE * LANE
    return pick(row_ref[0:1, pl.ds(tile, LANE)], offset + first % LANE)


def pack_kernel(
    points_h, poses_h, directions_h, src_h, maps_h, counts_h, out,
    points, poses, directions, src_s, src_v, maps, used, world, table, sems,
):
    devices = counts_h.shape[1]
    per_frag = points.shape[1] // poses.shape[1]
    stride = points.shape[1] + SUB
    pairs = [
        (poses_h, poses), (points_h, points), (src_h, src_s), (maps_h, maps),
        (directions_h, directions), (src_h, src_v), (counts_h, used),
    ]
    copies = [pltpu.make_async_copy(a, b, sems.at[i]) for i, (a, b) in enumerate(pairs)]
    for copy in copies:
        copy.start()
    copies[0].wait()
    copies[1].wait()
    write_points(points, poses, world)
    copies[2].wait()
    copies[3].wait()

    def peer(p, carry):
        for s in range(SUB):
            block = src_s[0, p * SUB + s]
            out[pl.ds(p * MSG + s, 3, stride=SUB), :] = world[pl.ds(block, 3, stride=stride), :]
        rows = maps[pl.ds(pl.multiple_of(p * SUB, SUB), SUB), :]
        out[pl.ds(p * MSG + 3 * SUB, SUB), :] = rows.astype(jnp.float32)
        return carry

    lax.fori_loop(0, devices, peer, 0, unroll=4)
    for copy in copies[4:]:
        copy.wait()
    frags = directions.shape[2]
    for v in range(2):
        for j in range(6):
            table[6 * v + j : 6 * v + j + 1, 0:frags] = directions[j, v : v + 1, :]
    limits = jnp.broadcast_to(used[0:1, :], (SUB, devices))
    peers = lax.broadcasted_iota(jnp.int32, (SUB, devices), 1)
    row = lax.broadcasted_iota(jnp.int32, (SUB, devices), 0)
    slot = lax.shift_right_logical(iota(1), shift_of(GROUP))
    field = lax.bitwise_and(iota(1), GROUP - 1)
    for q in range(0, devices, SUB):
        block = index_tile(src_v, q * SUB, iota(0) * SUB + slot)
        frag = lax.shift_right_logical(block, shift_of(per_frag))
        limit = jnp.sum(
            jnp.where(peers == row + q, limits.astype(jnp.float32), 0.0), axis=1, keepdims=True
        )
        extras = jnp.where(slot.astype(jnp.float32) < limit, 1.0, 0.0)
        for j in range(12):
            extras = jnp.where(field == j, pick(table[j : j + 1, :], frag), extras)
        out[pl.ds(q * MSG + MSG - 1, SUB, stride=MSG), :] = extras


def pair_sums(scalars, p, n, q):
    field = lax.bitwise_and(iota(1), GROUP - 1)
    tiles = [jnp.zeros((SUB, LANE), jnp.float32) for half in range(2)]
    for k, s in enumerate(scalars):
        for c in range(3):
            for at, value in ((6 * k + c, p[c]), (6 * k + 3 + c, n[c]), (18 + 3 * k + c, q[c])):
                total = jnp.sum(s * value, axis=1, keepdims=True)
                half = at // GROUP
                tiles[half] = jnp.where(field == at % GROUP, total, tiles[half])
    return tiles


def frag_sums(row, sums, per_frag):
    pairs = sums.shape[0]
    frag = lax.shift_right_logical(row, shift_of(per_frag))
    hot = jnp.broadcast_to(frag, (SUB, pairs)) == lax.broadcasted_iota(jnp.int32, (SUB, pairs), 0)
    total = jnp.dot(
        hot.astype(jnp.float32),
        sums[...],
        precision=lax.Precision.HIGHEST,
        preferred_element_type=jnp.float32,
    )
    return [total[:, 0:LANE], total[:, LANE:]]


def target_side(sums):
    lane = lax.bitwise_and(iota(1), GROUP - 1)
    k = (lane >= 6).astype(jnp.int32) + (lane >= 12).astype(jnp.int32)
    c = lane - 6 * k
    first = jnp.where(c < 3, pick(sums[1], jnp.minimum(2 + 3 * k + c, GROUP - 1)), sums[0])
    return [-first, -sums[1]]


def local_kernel(
    points, normals, poses, directions, pairs_s, pairs_v, maps, dst_s,
    staged, totals, world, sources, targets, sums,
):
    per_frag = points.shape[1] // poses.shape[1]
    stride = points.shape[1] + SUB
    groups = pairs_s.shape[1] // SUB
    write_fields(points, normals, poses, directions, world)

    def stage_remote(g, carry):
        for s in range(SUB):
            block = dst_s[0, g * SUB + s]
            staged[pl.ds(g * TARGET + s, 8, stride=SUB), :] = world[pl.ds(block, 8, stride=stride), :]
        return carry

    lax.fori_loop(0, dst_s.shape[1] // SUB, stage_remote, 0, unroll=4)

    def stage_local(g, carry):
        for s in range(SUB):
            a, b = pairs_s[0, g * SUB + s], pairs_s[1, g * SUB + s]
            targets[pl.ds(g * TARGET + s, 8, stride=SUB), :] = world[pl.ds(b, 8, stride=stride), :]
            sources[pl.ds(g * SOURCE + s, 3, stride=SUB), :] = world[pl.ds(a, 3, stride=stride), :]
            sources[pl.ds(g * SOURCE + 3 * SUB + s, 6, stride=SUB), :] = world[
                pl.ds(a + 8 * stride, 6, stride=stride), :
            ]
        return carry

    lax.fori_loop(0, groups, stage_local, 0, unroll=4)

    def step(i, carry):
        done = []
        for u in range(TOGETHER):
            g = i * TOGETHER + u
            index = maps[pl.ds(pl.multiple_of(g * SUB, SUB), SUB), :]
            base = pl.multiple_of(g * SOURCE, SUB)
            source = [sources[pl.ds(base + SUB * k, SUB), :] for k in range(9)]
            base = pl.multiple_of(g * TARGET, SUB)
            target = [pick(targets[pl.ds(base + SUB * k, SUB), :], index) for k in range(8)]
            x, y, n = source[0:3], target[0:3], target[3:6]
            scalars = [dot3(n, [x[k] - y[k] for k in range(3)])]
            for v in range(2):
                scalars.append(dot3(n, source[3 + 3 * v : 6 + 3 * v]) - target[6 + v])
            done.append(pair_sums(scalars, cross(x, n), n, cross(y, n)))
        for u in range(TOGETHER):
            first = pl.multiple_of((i * TOGETHER + u) * SUB, SUB)
            for half in range(2):
                sums[pl.ds(first, SUB), half * LANE : (half + 1) * LANE] = done[u][half]
        return carry

    lax.fori_loop(0, groups // TOGETHER, step, 0)
    side_a = frag_sums(pairs_v[0:1, :], sums, per_frag)
    side_b = target_side(frag_sums(pairs_v[1:2, :], sums, per_frag))
    for half in range(2):
        totals[half * SUB : (half + 1) * SUB, :] = side_a[half] + side_b[half]


def remote_kernel(arrived, staged, back, sums):
    devices = arrived.shape[0] // MSG
    own = lax.shift_right_logical(iota(1), shift_of(GROUP)) == iota(0)

    def step(i, carry):
        done = []
        for u in range(TOGETHER):
            d = i * TOGETHER + u
            x = [arrived[pl.ds(d * MSG + SUB * k, SUB), :] for k in range(3)]
            index = arrived[pl.ds(d * MSG + 3 * SUB, SUB), :].astype(jnp.int32)
            extras = arrived[pl.ds(d * MSG + 4 * SUB, 1), :]
            base = pl.multiple_of(d * TARGET, SUB)
            target = [pick(staged[pl.ds(base + SUB * k, SUB), :], index) for k in range(8)]
            way = [pick(extras, iota(0) * GROUP + j) for j in range(13)]
            y, n = target[0:3], target[3:6]
            p = cross(x, n)
            scalars = [dot3(n, [x[k] - y[k] for k in range(3)])]
            for v in range(2):
                a = way[6 * v : 6 * v + 6]
                scalars.append(dot3(p, a[0:3]) + dot3(n, a[3:6]) - target[6 + v])
            scalars = [s * way[12] for s in scalars]
            done.append(pair_sums(scalars, p, n, cross(y, n)))
        rows = [
            [jnp.sum(jnp.where(own, tile, 0.0), axis=0, keepdims=True) for tile in tiles]
            for tiles in done
        ]
        for u in range(TOGETHER):
            d = i * TOGETHER + u
            for half in range(2):
                back[pl.ds(2 * d + half, 1), :] = rows[u][half]
                sums[pl.ds(pl.multiple_of(d * SUB, SUB), SUB), half * LANE : (half + 1) * LANE] = done[
                    u
                ][half]
        return carry

    lax.fori_loop(0, devices // TOGETHER, step, 0)


def total_kernel(sums, dst_v, totals_in, totals, *, per_frag):
    side_b = target_side(frag_sums(dst_v[...], sums, per_frag))
    for half in range(2):
        rows = slice(half * SUB, (half + 1) * SUB)
        totals[rows, :] = totals_in[rows, :] + side_b[half]


def final_kernel(back, totals, src_v, gradient, hess, *, per_frag):
    devices = back.shape[0] // 2
    slot = lax.shift_right_logical(iota(1), shift_of(GROUP))
    sums = [[jnp.zeros((SUB, LANE), jnp.float32) for half in range(2)] for f in range(SUB)]
    for q in range(0, devices, SUB):
        block = index_tile(src_v, q * SUB, iota(0) * SUB + slot)
        frag = lax.shift_right_logical(block, shift_of(per_frag))
        for half in range(2):
            rows = back[pl.ds(2 * q + half, SUB, stride=2), :]
            for f in range(SUB):
                sums[f][half] = sums[f][half] + jnp.where(frag == f, rows, 0.0)
    halves = []
    for half in range(2):
        tile = jnp.zeros((SUB, LANE), jnp.float32)
        for f in range(SUB):
            tile = jnp.where(iota(0) == f, jnp.sum(sums[f][half], axis=0, keepdims=True), tile)
        for step in (64, 32, 16):
            tile = tile + pltpu.roll(tile, step, 1)
        halves.append(tile + totals[half * SUB : (half + 1) * SUB, :])
    total = jnp.where(iota(1) < GROUP, halves[0], halves[1]).T
    gradient[...] = total[0:6, :] * (1.0 / LANE)
    for v in range(2):
        part = total[6 + 6 * v : 12 + 6 * v, :] * (1.0 / (LANE * per_frag))
        for j in range(6):
            hess[j, v : v + 1, :] = part[j : j + 1, :]


def call(kernel, outs, scratch, spaces, **more):
    kinds = {"v": pltpu.VMEM, "s": pltpu.SMEM, "h": pltpu.HBM}
    return pl.pallas_call(
        kernel,
        out_shape=outs,
        in_specs=[pl.BlockSpec(memory_space=kinds[s]) for s in spaces],
        out_specs=[pl.BlockSpec(memory_space=pltpu.VMEM)] * len(outs),
        scratch_shapes=scratch,
        compiler_params=pltpu.CompilerParams(vmem_limit_bytes=VMEM_LIMIT),
        **more,
    )


def exchange(rows, devices):
    sent = rows.reshape(devices, 1, -1)
    sent = lax.all_to_all(sent, AXES, split_axis=0, concat_axis=0, tiled=True)
    return sent.reshape(rows.shape)


def local(
    points, normals, poses, directions, local_pairs, local_maps,
    remote_src, remote_maps, remote_dst, counts,
):
    devices = lax.axis_size("tile") * lax.axis_size("band")
    blocks, _, count = points.shape
    frags = poses.shape[1]
    slots = remote_src.shape[1]
    pairs = local_pairs.shape[1]
    assert count == LANE and frags == SUB and slots == devices * SUB and devices <= LANE
    per_frag = blocks // frags
    stride = blocks + SUB
    f32 = jnp.float32
    points = points.transpose(1, 0, 2)
    normals = normals.transpose(1, 0, 2)
    directions = directions.transpose(1, 0, 2)

    def array(*shape):
        return jax.ShapeDtypeStruct(shape, f32)

    def vmem(*shape, dtype=f32):
        return pltpu.VMEM(shape, dtype)

    (message,) = call(
        pack_kernel,
        [array(devices * MSG, LANE)],
        [
            vmem(3, blocks, LANE),
            vmem(6, frags),
            vmem(6, 2, frags),
            pltpu.SMEM((1, slots), jnp.int32),
            vmem(1, slots, dtype=jnp.int32),
            vmem(slots, LANE, dtype=jnp.int32),
            vmem(1, devices, dtype=jnp.int32),
            vmem(3 * stride, LANE),
            vmem(2 * SUB, LANE),
            pltpu.SemaphoreType.DMA((7,)),
        ],
        "hhhhhh",
    )(points, poses, directions, remote_src, remote_maps[0], counts)
    arrived = exchange(message, devices)
    staged, totals = call(
        local_kernel,
        [array(devices * TARGET, LANE), array(2 * SUB, LANE)],
        [
            vmem(14 * stride, LANE),
            vmem(pairs // SUB * SOURCE, LANE),
            vmem(pairs // SUB * TARGET, LANE),
            vmem(pairs, 2 * LANE),
        ],
        "vvvvsvvs",
        cost_estimate=pl.CostEstimate(
            flops=200 * pairs * LANE, bytes_accessed=4_000_000, transcendentals=0
        ),
    )(points, normals, poses, directions, local_pairs, local_pairs, local_maps, remote_dst)
    back, sums = call(
        remote_kernel, [array(devices * 2, LANE), array(slots, 2 * LANE)], [], "vv"
    )(arrived, staged)
    back = exchange(back, devices)
    (totals,) = call(
        functools.partial(total_kernel, per_frag=per_frag),
        [array(2 * SUB, LANE)],
        [],
        "vvv",
        cost_estimate=pl.CostEstimate(
            flops=2 * SUB * slots * 2 * LANE, bytes_accessed=1_000_000, transcendentals=0
        ),
    )(sums, remote_dst, totals)
    gradient, hess = call(
        functools.partial(final_kernel, per_frag=per_frag),
        [array(6, frags), array(6, 2, frags)],
        [],
        "vvv",
    )(back, totals, remote_src)
    return (gradient, hess.transpose(1, 0, 2))


def solution(mesh):
    placed = (
        P(AXES, None, None),
        P(AXES, None, None),
        P(None, AXES),
        P(None, None, AXES),
        P(None, AXES),
        P(AXES, None),
        P(AXES, None),
        P(AXES, None, None),
        P(AXES, None),
        P(AXES, None),
    )
    return jax.shard_map(
        local,
        mesh=mesh,
        in_specs=placed,
        out_specs=(P(None, AXES), P(None, None, AXES)),
        check_vma=False,
    )
```

```python
import functools

import jax
import jax.numpy as jnp
from jax import lax
from jax.experimental import pallas as pl
from jax.experimental.pallas import tpu as pltpu
from jax.sharding import PartitionSpec as P

AXES = ("tile", "band")
SUB = 8
LANE = 128
MSG = 4 * SUB + 1
TARGET = 8 * SUB
SOURCE = 9 * SUB
TOGETHER = 4
GROUP = 16
VMEM_LIMIT = 16 * 1024 * 1024
PACK_LIMIT = 60 * 1024 * 1024
PEERS = 32


def iota(axis):
    return lax.broadcasted_iota(jnp.int32, (SUB, LANE), axis)


def pick(values, index):
    values = jnp.broadcast_to(values, (SUB, LANE))
    return jnp.take_along_axis(values, index, axis=1, mode="promise_in_bounds")


def shift_of(size):
    shift = size.bit_length() - 1
    assert 1 << shift == size
    return shift


def rotations(poses):
    half = [poses[i : i + 1, :] * 0.5 for i in range(3)]
    w = 1.0 / jnp.sqrt(1.0 + half[0] * half[0] + half[1] * half[1] + half[2] * half[2])
    x, y, z = half[0] * w, half[1] * w, half[2] * w
    rotation = [
        [1.0 - 2.0 * (y * y + z * z), 2.0 * (x * y - w * z), 2.0 * (x * z + w * y)],
        [2.0 * (x * y + w * z), 1.0 - 2.0 * (x * x + z * z), 2.0 * (y * z - w * x)],
        [2.0 * (x * z - w * y), 2.0 * (y * z + w * x), 1.0 - 2.0 * (x * x + y * y)],
    ]
    return rotation, [poses[i : i + 1, :] for i in range(3, 6)]


def cross(left, right):
    return [
        left[1] * right[2] - left[2] * right[1],
        left[2] * right[0] - left[0] * right[2],
        left[0] * right[1] - left[1] * right[0],
    ]


def dot3(left, right):
    return left[0] * right[0] + left[1] * right[1] + left[2] * right[2]


def spread(row, f):
    return jnp.broadcast_to(row[:, f : f + 1], (SUB, LANE))


def splat_rotation(poses, f):
    half = [jnp.full((SUB, LANE), poses[i, f] * 0.5, jnp.float32) for i in range(3)]
    w = 1.0 / jnp.sqrt(1.0 + half[0] * half[0] + half[1] * half[1] + half[2] * half[2])
    x, y, z = half[0] * w, half[1] * w, half[2] * w
    rotation = [
        [1.0 - 2.0 * (y * y + z * z), 2.0 * (x * y - w * z), 2.0 * (x * z + w * y)],
        [2.0 * (x * y + w * z), 1.0 - 2.0 * (x * x + z * z), 2.0 * (y * z - w * x)],
        [2.0 * (x * z - w * y), 2.0 * (y * z + w * x), 1.0 - 2.0 * (x * x + y * y)],
    ]
    return rotation, [jnp.full((SUB, LANE), poses[i, f], jnp.float32) for i in range(3, 6)]


def write_points(points, poses, world):
    blocks, frags = points.shape[1], poses.shape[1]
    per_frag, stride = blocks // frags, blocks + SUB
    for f in range(frags):
        turn, move = splat_rotation(poses, f)
        for b in range(f * per_frag, (f + 1) * per_frag, SUB):
            x = [points[j, b : b + SUB, :] for j in range(3)]
            for i in range(3):
                world[pl.ds(i * stride + b, SUB), :] = dot3(turn[i], x) + move[i]


def write_fields(points, normals, poses, directions, world):
    blocks, frags = points.shape[1], poses.shape[1]
    per_frag, stride = blocks // frags, blocks + SUB
    rotation, translation = rotations(poses[...])
    for f in range(frags):
        turn = [[spread(rotation[i][j], f) for j in range(3)] for i in range(3)]
        move = [spread(translation[i], f) for i in range(3)]
        way = [[spread(directions[j, v : v + 1, :], f) for j in range(6)] for v in range(2)]
        for b in range(f * per_frag, (f + 1) * per_frag, SUB):
            x = [points[j, b : b + SUB, :] for j in range(3)]
            m = [normals[j, b : b + SUB, :] for j in range(3)]
            y = [dot3(turn[i], x) + move[i] for i in range(3)]
            n = [dot3(turn[i], m) for i in range(3)]
            speed = []
            for v in range(2):
                swing = cross(way[v][0:3], y)
                speed.append([swing[i] + way[v][3 + i] for i in range(3)])
            along = [dot3(n, speed[v]) for v in range(2)]
            for i, row in enumerate(y + n + along + speed[0] + speed[1]):
                world[pl.ds(i * stride + b, SUB), :] = row


def index_tile(row_ref, first, offset):
    tile = first // LANE * LANE
    return pick(row_ref[0:1, pl.ds(tile, LANE)], offset + first % LANE)


def pack_kernel(
    points_h, poses_h, directions_h, src_h, maps_h, counts_h, out_h,
    points, poses, directions, src_s, src_v, maps, used, world, table, out, sems, out_sems,
):
    devices = counts_h.shape[1]
    per_frag = points.shape[1] // poses.shape[1]
    stride = points.shape[1] + SUB
    pairs = [
        (directions_h, directions), (src_h, src_v), (counts_h, used), (poses_h, poses),
        (points_h, points), (src_h, src_s), (maps_h, maps),
    ]
    copies = [pltpu.make_async_copy(a, b, sems.at[i]) for i, (a, b) in enumerate(pairs)]
    for copy in copies:
        copy.start()
    for copy in copies[0:3]:
        copy.wait()
    frags = directions.shape[2]
    for v in range(2):
        for j in range(6):
            table[6 * v + j : 6 * v + j + 1, 0:frags] = directions[j, v : v + 1, :]
    limits = jnp.broadcast_to(used[0:1, :], (SUB, devices)).astype(jnp.float32)
    peers = lax.broadcasted_iota(jnp.int32, (SUB, devices), 1)
    row = lax.broadcasted_iota(jnp.int32, (SUB, devices), 0)
    slot = lax.shift_right_logical(iota(1), shift_of(GROUP))
    field = lax.bitwise_and(iota(1), GROUP - 1)
    for q in range(0, devices, SUB):
        block = index_tile(src_v, q * SUB, iota(0) * SUB + slot)
        frag = lax.shift_right_logical(block, shift_of(per_frag))
        limit = jnp.sum(jnp.where(peers == row + q, limits, 0.0), axis=1, keepdims=True)
        extras = jnp.where(slot.astype(jnp.float32) < limit, 1.0, 0.0)
        for j in range(12):
            extras = jnp.where(field == j, pick(table[j : j + 1, :], frag), extras)
        out[pl.ds(q * MSG + MSG - 1, SUB, stride=MSG), :] = extras
    for copy in copies[3:]:
        copy.wait()
    write_points(points, poses, world)

    def peer(p):
        for s in range(SUB):
            block = src_s[0, p * SUB + s]
            out[pl.ds(p * MSG + s, 3, stride=SUB), :] = world[pl.ds(block, 3, stride=stride), :]
        rows = maps[pl.ds(pl.multiple_of(p * SUB, SUB), SUB), :]
        out[pl.ds(p * MSG + 3 * SUB, SUB), :] = rows.astype(jnp.float32)

    def piece(i):
        rows = pl.ds(pl.multiple_of(i * SUB * MSG, SUB), SUB * MSG)
        return pltpu.make_async_copy(out.at[rows], out_h.at[rows], out_sems.at[i])

    def pack(i, carry):
        for u in range(SUB):
            peer(i * SUB + u)
        piece(i).start()
        return carry

    lax.fori_loop(0, devices // SUB, pack, 0)
    for i in range(devices // SUB):
        piece(i).wait()


def pair_sums(scalars, p, n, q):
    field = lax.bitwise_and(iota(1), GROUP - 1)
    tiles = [jnp.zeros((SUB, LANE), jnp.float32) for half in range(2)]
    for k, s in enumerate(scalars):
        for c in range(3):
            for at, value in ((6 * k + c, p[c]), (6 * k + 3 + c, n[c]), (18 + 3 * k + c, q[c])):
                total = jnp.sum(s * value, axis=1, keepdims=True)
                half = at // GROUP
                tiles[half] = jnp.where(field == at % GROUP, total, tiles[half])
    return tiles


def frag_sums(row, sums, per_frag):
    pairs = sums.shape[0]
    frag = lax.shift_right_logical(row, shift_of(per_frag))
    hot = jnp.broadcast_to(frag, (SUB, pairs)) == lax.broadcasted_iota(jnp.int32, (SUB, pairs), 0)
    total = jnp.dot(
        hot.astype(jnp.float32),
        sums[...],
        precision=lax.Precision.HIGHEST,
        preferred_element_type=jnp.float32,
    )
    return [total[:, 0:LANE], total[:, LANE:]]


def target_side(sums):
    lane = lax.bitwise_and(iota(1), GROUP - 1)
    k = (lane >= 6).astype(jnp.int32) + (lane >= 12).astype(jnp.int32)
    c = lane - 6 * k
    first = jnp.where(c < 3, pick(sums[1], jnp.minimum(2 + 3 * k + c, GROUP - 1)), sums[0])
    return [-first, -sums[1]]


def local_kernel(
    points, normals, poses, directions, pairs_s, pairs_v, maps, dst_s,
    staged, totals, world, sources, targets, sums,
):
    per_frag = points.shape[1] // poses.shape[1]
    stride = points.shape[1] + SUB
    groups = pairs_s.shape[1] // SUB
    write_fields(points, normals, poses, directions, world)

    def stage_remote(g, carry):
        for s in range(SUB):
            block = dst_s[0, g * SUB + s]
            staged[pl.ds(g * TARGET + s, 8, stride=SUB), :] = world[pl.ds(block, 8, stride=stride), :]
        return carry

    lax.fori_loop(0, dst_s.shape[1] // SUB, stage_remote, 0, unroll=4)

    def stage_local(g, carry):
        for s in range(SUB):
            a, b = pairs_s[0, g * SUB + s], pairs_s[1, g * SUB + s]
            targets[pl.ds(g * TARGET + s, 8, stride=SUB), :] = world[pl.ds(b, 8, stride=stride), :]
            sources[pl.ds(g * SOURCE + s, 3, stride=SUB), :] = world[pl.ds(a, 3, stride=stride), :]
            sources[pl.ds(g * SOURCE + 3 * SUB + s, 6, stride=SUB), :] = world[
                pl.ds(a + 8 * stride, 6, stride=stride), :
            ]
        return carry

    lax.fori_loop(0, groups, stage_local, 0, unroll=4)

    def step(i, carry):
        done = []
        for u in range(TOGETHER):
            g = i * TOGETHER + u
            index = maps[pl.ds(pl.multiple_of(g * SUB, SUB), SUB), :]
            base = pl.multiple_of(g * SOURCE, SUB)
            source = [sources[pl.ds(base + SUB * k, SUB), :] for k in range(9)]
            base = pl.multiple_of(g * TARGET, SUB)
            target = [pick(targets[pl.ds(base + SUB * k, SUB), :], index) for k in range(8)]
            x, y, n = source[0:3], target[0:3], target[3:6]
            scalars = [dot3(n, [x[k] - y[k] for k in range(3)])]
            for v in range(2):
                scalars.append(dot3(n, source[3 + 3 * v : 6 + 3 * v]) - target[6 + v])
            done.append(pair_sums(scalars, cross(x, n), n, cross(y, n)))
        for u in range(TOGETHER):
            first = pl.multiple_of((i * TOGETHER + u) * SUB, SUB)
            for half in range(2):
                sums[pl.ds(first, SUB), half * LANE : (half + 1) * LANE] = done[u][half]
        return carry

    lax.fori_loop(0, groups // TOGETHER, step, 0)
    side_a = frag_sums(pairs_v[0:1, :], sums, per_frag)
    side_b = target_side(frag_sums(pairs_v[1:2, :], sums, per_frag))
    for half in range(2):
        totals[half * SUB : (half + 1) * SUB, :] = side_a[half] + side_b[half]


def halves_of(values):
    high = values.astype(jnp.bfloat16)
    return high, (values - high.astype(jnp.float32)).astype(jnp.bfloat16)


def remote_kernel(arrived, staged, back, sums, parts, turned, coeffs, index, partial):
    bf16, f32 = jnp.bfloat16, jnp.float32
    pairs = parts.shape[0]
    peers = pairs // SUB
    nums = lax.dot_general

    def wide(shape, axis):
        return lax.broadcasted_iota(jnp.int32, shape, axis)

    points2 = lax.bitwise_and(wide((LANE, 2 * LANE), 1), LANE - 1)
    same = (points2 == wide((LANE, 2 * LANE), 0)).astype(f32).astype(bf16)
    fields2 = lax.bitwise_and(wide((GROUP, 2 * LANE), 1), GROUP - 1)
    gather = (fields2 == wide((GROUP, 2 * LANE), 0)).astype(f32).astype(bf16)
    own = lax.shift_right_logical(iota(1), shift_of(GROUP)) == iota(0)
    partial[27 * SUB :, :] = jnp.zeros((partial.shape[0] - 27 * SUB, LANE), f32)

    def block(c, carry):
        first = c * peers

        def turn(i, left, at):
            for u in range(0, peers, 2):
                both = jnp.concatenate([at(u), at(u + 1)], axis=0)
                high, low = halves_of(both)
                parts[u * SUB : (u + 2) * SUB, i * 2 * LANE : i * 2 * LANE + LANE] = high
                parts[u * SUB : (u + 2) * SUB, i * 2 * LANE + LANE : (i + 1) * 2 * LANE] = low
            return nums(
                left,
                parts[:, i * 2 * LANE : (i + 1) * 2 * LANE],
                (((1,), (1,)), ((), ())),
                preferred_element_type=f32,
            )

        for u in range(peers):
            row = (first + u) * MSG + 3 * SUB
            index[u * SUB : (u + 1) * SUB, :] = arrived[pl.ds(row, SUB), :].astype(jnp.int32)

        def extras(u):
            row = arrived[pl.ds((first + u) * MSG + 4 * SUB, 1), :]
            return jnp.where(own, jnp.broadcast_to(row, (SUB, LANE)), 0.0)

        def target(k):
            def at(u):
                base = pl.multiple_of((first + u) * TARGET, SUB)
                return pick(staged[pl.ds(base + SUB * k, SUB), :], index[u * SUB : (u + 1) * SUB, :])

            return at

        def source(k):
            return lambda u: arrived[pl.ds((first + u) * MSG + SUB * k, SUB), :]

        coeffs[...] = turn(11, gather, extras)
        for k in range(8):
            turned[k * LANE : (k + 1) * LANE, :] = turn(k, same, target(k))
        for k in range(3):
            turned[(8 + k) * LANE : (9 + k) * LANE, :] = turn(8 + k, same, source(k))
        for t in range(0, pairs, LANE):
            lanes = slice(t, t + LANE)

            def add(i, totals):
                start = pl.multiple_of(i * SUB, SUB)
                field = [turned[pl.ds(start + k * LANE, SUB), lanes] for k in range(11)]
                way = [coeffs[j : j + 1, lanes] for j in range(12)]
                y, n, x = field[0:3], field[3:6], field[8:11]
                p, q = cross(x, n), cross(y, n)
                scalars = [dot3(n, [x[k] - y[k] for k in range(3)])]
                for v in range(2):
                    a = way[6 * v : 6 * v + 6]
                    scalars.append(dot3(p, a[0:3]) + dot3(n, a[3:6]) - field[6 + v])
                terms = []
                for s in scalars:
                    terms += [s * value for value in p + n]
                for s in scalars:
                    terms += [s * value for value in q]
                return tuple(total + term for total, term in zip(totals, terms))

            zero = jnp.zeros((SUB, LANE), f32)
            totals = lax.fori_loop(0, LANE // SUB, add, (zero,) * 27, unroll=4)
            for j in range(27):
                partial[j * SUB : (j + 1) * SUB, :] = totals[j]
            total = partial[pl.ds(0, 4 * SUB, stride=SUB), :]
            for s in range(1, SUB):
                total = total + partial[pl.ds(s, 4 * SUB, stride=SUB), :]
            at = pl.multiple_of(c * pairs, LANE) + t
            sums[:, pl.ds(at, LANE)] = total * coeffs[12:13, lanes]
        start = pl.multiple_of(c * pairs, LANE)
        high, low = halves_of(sums[:, pl.ds(start, pairs)])
        entry = wide((8 * SUB, 2 * LANE), 1)
        entry = lax.bitwise_and(entry, GROUP - 1) + GROUP * lax.shift_right_logical(entry, 7)
        place = (lax.bitwise_and(wide((8 * SUB, 2 * LANE), 0), 4 * SUB - 1) == entry).astype(f32)
        rows = nums(
            jnp.concatenate([high, low], axis=0),
            place.astype(bf16),
            (((0,), (0,)), ((), ())),
            preferred_element_type=f32,
        )
        slot = lax.bitwise_and(wide((pairs, 2 * LANE), 0), SUB - 1)
        lane = lax.bitwise_and(wide((pairs, 2 * LANE), 1), LANE - 1)
        high, low = halves_of(jnp.where(lax.shift_right_logical(lane, 4) == slot, rows, 0.0))
        mine = lax.shift_right_logical(wide((peers, pairs), 1), 3) == wide((peers, pairs), 0)
        mine = mine.astype(f32).astype(bf16)
        rows = jnp.dot(mine, high, preferred_element_type=f32) + jnp.dot(
            mine, low, preferred_element_type=f32
        )
        for half in range(2):
            back[pl.ds(2 * first + half, peers, stride=2), :] = rows[
                :, half * LANE : (half + 1) * LANE
            ]
        return carry

    lax.fori_loop(0, sums.shape[1] // pairs, block, 0)


def total_kernel(sums, dst_v, totals, *, per_frag):
    pairs = sums.shape[1]
    frag = lax.shift_right_logical(dst_v[...], shift_of(per_frag))
    hot = jnp.broadcast_to(frag, (SUB, pairs)) == lax.broadcasted_iota(jnp.int32, (SUB, pairs), 0)
    total = -lax.dot_general(
        sums[...],
        hot.astype(jnp.float32),
        (((1,), (1,)), ((), ())),
        precision=lax.Precision.HIGHEST,
        preferred_element_type=jnp.float32,
    )
    for k in range(3):
        totals[6 * k : 6 * k + 3, :] = total[18 + 3 * k : 21 + 3 * k, :]
        totals[6 * k + 3 : 6 * k + 6, :] = total[6 * k + 3 : 6 * k + 6, :]


def final_kernel(back, totals, extra, src_v, gradient, hess, *, per_frag):
    devices = back.shape[0] // 2
    slot = lax.shift_right_logical(iota(1), shift_of(GROUP))
    sums = [[jnp.zeros((SUB, LANE), jnp.float32) for half in range(2)] for f in range(SUB)]
    for q in range(0, devices, SUB):
        block = index_tile(src_v, q * SUB, iota(0) * SUB + slot)
        frag = lax.shift_right_logical(block, shift_of(per_frag))
        for half in range(2):
            rows = back[pl.ds(2 * q + half, SUB, stride=2), :]
            for f in range(SUB):
                sums[f][half] = sums[f][half] + jnp.where(frag == f, rows, 0.0)
    halves = []
    for half in range(2):
        tile = jnp.zeros((SUB, LANE), jnp.float32)
        for f in range(SUB):
            tile = jnp.where(iota(0) == f, jnp.sum(sums[f][half], axis=0, keepdims=True), tile)
        for step in (64, 32, 16):
            tile = tile + pltpu.roll(tile, step, 1)
        halves.append(tile + totals[half * SUB : (half + 1) * SUB, :])
    total = jnp.where(iota(1) < GROUP, halves[0], halves[1]).T[0:18, :] + extra[...]
    gradient[...] = total[0:6, :] * (1.0 / LANE)
    for v in range(2):
        part = total[6 + 6 * v : 12 + 6 * v, :] * (1.0 / (LANE * per_frag))
        for j in range(6):
            hess[j, v : v + 1, :] = part[j : j + 1, :]


def call(kernel, outs, scratch, spaces, limit=VMEM_LIMIT, out_space="v", **more):
    kinds = {"v": pltpu.VMEM, "s": pltpu.SMEM, "h": pltpu.HBM}
    return pl.pallas_call(
        kernel,
        out_shape=outs,
        in_specs=[pl.BlockSpec(memory_space=kinds[s]) for s in spaces],
        out_specs=[pl.BlockSpec(memory_space=kinds[out_space])] * len(outs),
        scratch_shapes=scratch,
        compiler_params=pltpu.CompilerParams(vmem_limit_bytes=limit),
        **more,
    )


def exchange(rows, devices):
    sent = rows.reshape(devices, 1, -1)
    sent = lax.all_to_all(sent, AXES, split_axis=0, concat_axis=0, tiled=True)
    return sent.reshape(rows.shape)


def local(
    points, normals, poses, directions, local_pairs, local_maps,
    remote_src, remote_maps, remote_dst, counts,
):
    devices = lax.axis_size("tile") * lax.axis_size("band")
    blocks, _, count = points.shape
    frags = poses.shape[1]
    slots = remote_src.shape[1]
    pairs = local_pairs.shape[1]
    assert count == LANE and frags == SUB and slots == devices * SUB and devices % PEERS == 0
    per_frag = blocks // frags
    stride = blocks + SUB
    f32 = jnp.float32
    points = points.transpose(1, 0, 2)
    normals = normals.transpose(1, 0, 2)
    directions = directions.transpose(1, 0, 2)

    def array(*shape):
        return jax.ShapeDtypeStruct(shape, f32)

    def vmem(*shape, dtype=f32):
        return pltpu.VMEM(shape, dtype)

    (message,) = call(
        pack_kernel,
        [array(devices * MSG, LANE)],
        [
            vmem(3, blocks, LANE),
            pltpu.SMEM((6, frags), f32),
            vmem(6, 2, frags),
            pltpu.SMEM((1, slots), jnp.int32),
            vmem(1, slots, dtype=jnp.int32),
            vmem(slots, LANE, dtype=jnp.int32),
            vmem(1, devices, dtype=jnp.int32),
            vmem(3 * stride, LANE),
            vmem(2 * SUB, LANE),
            vmem(devices * MSG, LANE),
            pltpu.SemaphoreType.DMA((7,)),
            pltpu.SemaphoreType.DMA((devices // SUB,)),
        ],
        "hhhhhh",
        limit=PACK_LIMIT,
        out_space="h",
    )(points, poses, directions, remote_src, remote_maps[0], counts)
    arrived = exchange(message, devices)
    staged, totals = call(
        local_kernel,
        [array(devices * TARGET, LANE), array(2 * SUB, LANE)],
        [
            vmem(14 * stride, LANE),
            vmem(pairs // SUB * SOURCE, LANE),
            vmem(pairs // SUB * TARGET, LANE),
            vmem(pairs, 2 * LANE),
        ],
        "vvvvsvvs",
        cost_estimate=pl.CostEstimate(
            flops=200 * pairs * LANE, bytes_accessed=4_000_000, transcendentals=0
        ),
    )(points, normals, poses, directions, local_pairs, local_pairs, local_maps, remote_dst)
    part = PEERS * SUB
    back, sums = call(
        remote_kernel,
        [array(devices * 2, LANE), array(4 * SUB, slots)],
        [
            vmem(part, 12 * 2 * LANE, dtype=jnp.bfloat16),
            vmem(11 * LANE, part),
            vmem(GROUP, part),
            vmem(part, LANE, dtype=jnp.int32),
            vmem(4 * SUB * SUB, LANE),
        ],
        "vv",
    )(arrived, staged)
    back = exchange(back, devices)
    (extra,) = call(
        functools.partial(total_kernel, per_frag=per_frag),
        [array(18, frags)],
        [],
        "vv",
        cost_estimate=pl.CostEstimate(
            flops=2 * SUB * slots * 2 * LANE, bytes_accessed=1_000_000, transcendentals=0
        ),
    )(sums, remote_dst)
    gradient, hess = call(
        functools.partial(final_kernel, per_frag=per_frag),
        [array(6, frags), array(6, 2, frags)],
        [],
        "vvvv",
    )(back, totals, extra, remote_src)
    return (gradient, hess.transpose(1, 0, 2))


def solution(mesh):
    placed = (
        P(AXES, None, None),
        P(AXES, None, None),
        P(None, AXES),
        P(None, None, AXES),
        P(None, AXES),
        P(AXES, None),
        P(AXES, None),
        P(AXES, None, None),
        P(AXES, None),
        P(AXES, None),
    )
    return jax.shard_map(
        local,
        mesh=mesh,
        in_specs=placed,
        out_specs=(P(None, AXES), P(None, None, AXES)),
        check_vma=False,
    )
```

```python
import functools

import jax
import jax.numpy as jnp
from jax import lax
from jax.experimental import pallas as pl
from jax.experimental.pallas import tpu as pltpu
from jax.sharding import PartitionSpec as P

AXES = ("tile", "band")
SUB = 8
LANE = 128
MSG = 4 * SUB + 1
TARGET = 8 * SUB
SOURCE = 9 * SUB
TOGETHER = 4
GROUP = 16
VMEM_LIMIT = 16 * 1024 * 1024
PACK_LIMIT = 56 * 1024 * 1024
PEERS = 32


def iota(axis):
    return lax.broadcasted_iota(jnp.int32, (SUB, LANE), axis)


def pick(values, index):
    values = jnp.broadcast_to(values, (SUB, LANE))
    return jnp.take_along_axis(values, index, axis=1, mode="promise_in_bounds")


def shift_of(size):
    shift = size.bit_length() - 1
    assert 1 << shift == size
    return shift


def rotations(poses):
    half = [poses[i : i + 1, :] * 0.5 for i in range(3)]
    w = 1.0 / jnp.sqrt(1.0 + half[0] * half[0] + half[1] * half[1] + half[2] * half[2])
    x, y, z = half[0] * w, half[1] * w, half[2] * w
    rotation = [
        [1.0 - 2.0 * (y * y + z * z), 2.0 * (x * y - w * z), 2.0 * (x * z + w * y)],
        [2.0 * (x * y + w * z), 1.0 - 2.0 * (x * x + z * z), 2.0 * (y * z - w * x)],
        [2.0 * (x * z - w * y), 2.0 * (y * z + w * x), 1.0 - 2.0 * (x * x + y * y)],
    ]
    return rotation, [poses[i : i + 1, :] for i in range(3, 6)]


def cross(left, right):
    return [
        left[1] * right[2] - left[2] * right[1],
        left[2] * right[0] - left[0] * right[2],
        left[0] * right[1] - left[1] * right[0],
    ]


def dot3(left, right):
    return left[0] * right[0] + left[1] * right[1] + left[2] * right[2]


def spread(row, f):
    return jnp.broadcast_to(row[:, f : f + 1], (SUB, LANE))


def splat_rotation(poses, f):
    half = [jnp.full((SUB, LANE), poses[i, f] * 0.5, jnp.float32) for i in range(3)]
    w = 1.0 / jnp.sqrt(1.0 + half[0] * half[0] + half[1] * half[1] + half[2] * half[2])
    x, y, z = half[0] * w, half[1] * w, half[2] * w
    rotation = [
        [1.0 - 2.0 * (y * y + z * z), 2.0 * (x * y - w * z), 2.0 * (x * z + w * y)],
        [2.0 * (x * y + w * z), 1.0 - 2.0 * (x * x + z * z), 2.0 * (y * z - w * x)],
        [2.0 * (x * z - w * y), 2.0 * (y * z + w * x), 1.0 - 2.0 * (x * x + y * y)],
    ]
    return rotation, [jnp.full((SUB, LANE), poses[i, f], jnp.float32) for i in range(3, 6)]


def write_points(points, poses, world):
    blocks, frags = points.shape[1], poses.shape[1]
    per_frag, stride = blocks // frags, blocks + SUB
    for f in range(frags):
        turn, move = splat_rotation(poses, f)
        for b in range(f * per_frag, (f + 1) * per_frag, SUB):
            x = [points[j, b : b + SUB, :] for j in range(3)]
            for i in range(3):
                world[pl.ds(i * stride + b, SUB), :] = dot3(turn[i], x) + move[i]


def write_fields(points, normals, poses, directions, world):
    blocks, frags = points.shape[1], poses.shape[1]
    per_frag, stride = blocks // frags, blocks + SUB
    rotation, translation = rotations(poses[...])
    for f in range(frags):
        turn = [[spread(rotation[i][j], f) for j in range(3)] for i in range(3)]
        move = [spread(translation[i], f) for i in range(3)]
        way = [[spread(directions[j, v : v + 1, :], f) for j in range(6)] for v in range(2)]
        for b in range(f * per_frag, (f + 1) * per_frag, SUB):
            x = [points[j, b : b + SUB, :] for j in range(3)]
            m = [normals[j, b : b + SUB, :] for j in range(3)]
            y = [dot3(turn[i], x) + move[i] for i in range(3)]
            n = [dot3(turn[i], m) for i in range(3)]
            speed = []
            for v in range(2):
                swing = cross(way[v][0:3], y)
                speed.append([swing[i] + way[v][3 + i] for i in range(3)])
            along = [dot3(n, speed[v]) for v in range(2)]
            for i, row in enumerate(y + n + along + speed[0] + speed[1]):
                world[pl.ds(i * stride + b, SUB), :] = row


def index_tile(row_ref, first, offset):
    tile = first // LANE * LANE
    return pick(row_ref[0:1, pl.ds(tile, LANE)], offset + first % LANE)


def pack_kernel(
    points_h, poses_h, directions_h, src_h, maps_h, counts_h, out,
    points, poses, directions, src_s, src_v, maps, used, world, table, sems,
):
    devices = counts_h.shape[1]
    per_frag = points.shape[1] // poses.shape[1]
    stride = points.shape[1] + SUB
    pairs = [
        (directions_h, directions), (src_h, src_v), (counts_h, used), (poses_h, poses),
        (points_h, points), (src_h, src_s), (maps_h, maps),
    ]
    copies = [pltpu.make_async_copy(a, b, sems.at[i]) for i, (a, b) in enumerate(pairs)]
    for copy in copies:
        copy.start()
    for copy in copies[0:3]:
        copy.wait()
    frags = directions.shape[2]
    for v in range(2):
        for j in range(6):
            table[6 * v + j : 6 * v + j + 1, 0:frags] = directions[j, v : v + 1, :]
    limits = jnp.broadcast_to(used[0:1, :], (SUB, devices)).astype(jnp.float32)
    peers = lax.broadcasted_iota(jnp.int32, (SUB, devices), 1)
    row = lax.broadcasted_iota(jnp.int32, (SUB, devices), 0)
    slot = lax.shift_right_logical(iota(1), shift_of(GROUP))
    field = lax.bitwise_and(iota(1), GROUP - 1)
    for q in range(0, devices, SUB):
        block = index_tile(src_v, q * SUB, iota(0) * SUB + slot)
        frag = lax.shift_right_logical(block, shift_of(per_frag))
        limit = jnp.sum(jnp.where(peers == row + q, limits, 0.0), axis=1, keepdims=True)
        extras = jnp.where(slot.astype(jnp.float32) < limit, 1.0, 0.0)
        for j in range(12):
            extras = jnp.where(field == j, pick(table[j : j + 1, :], frag), extras)
        out[pl.ds(q * MSG + MSG - 1, SUB, stride=MSG), :] = extras
    for copy in copies[3:]:
        copy.wait()
    write_points(points, poses, world)

    def peer(p):
        for s in range(SUB):
            block = src_s[0, p * SUB + s]
            out[pl.ds(p * MSG + s, 3, stride=SUB), :] = world[pl.ds(block, 3, stride=stride), :]
        rows = maps[pl.ds(pl.multiple_of(p * SUB, SUB), SUB), :]
        out[pl.ds(p * MSG + 3 * SUB, SUB), :] = rows.astype(jnp.float32)

    def pack(i, carry):
        for u in range(SUB):
            peer(i * SUB + u)
        return carry

    lax.fori_loop(0, devices // SUB, pack, 0)


def pair_sums(scalars, p, n, q):
    field = lax.bitwise_and(iota(1), GROUP - 1)
    tiles = [jnp.zeros((SUB, LANE), jnp.float32) for half in range(2)]
    for k, s in enumerate(scalars):
        for c in range(3):
            for at, value in ((6 * k + c, p[c]), (6 * k + 3 + c, n[c]), (18 + 3 * k + c, q[c])):
                total = jnp.sum(s * value, axis=1, keepdims=True)
                half = at // GROUP
                tiles[half] = jnp.where(field == at % GROUP, total, tiles[half])
    return tiles


def frag_sums(row, sums, per_frag):
    pairs = sums.shape[0]
    frag = lax.shift_right_logical(row, shift_of(per_frag))
    hot = jnp.broadcast_to(frag, (SUB, pairs)) == lax.broadcasted_iota(jnp.int32, (SUB, pairs), 0)
    total = jnp.dot(
        hot.astype(jnp.float32),
        sums[...],
        precision=lax.Precision.HIGHEST,
        preferred_element_type=jnp.float32,
    )
    return [total[:, 0:LANE], total[:, LANE:]]


def target_side(sums):
    lane = lax.bitwise_and(iota(1), GROUP - 1)
    k = (lane >= 6).astype(jnp.int32) + (lane >= 12).astype(jnp.int32)
    c = lane - 6 * k
    first = jnp.where(c < 3, pick(sums[1], jnp.minimum(2 + 3 * k + c, GROUP - 1)), sums[0])
    return [-first, -sums[1]]


def local_kernel(
    points, normals, poses, directions, pairs_s, pairs_v, maps, dst_s,
    staged, totals, world, sources, targets, sums,
):
    per_frag = points.shape[1] // poses.shape[1]
    stride = points.shape[1] + SUB
    groups = pairs_s.shape[1] // SUB
    write_fields(points, normals, poses, directions, world)

    def stage_remote(g, carry):
        for s in range(SUB):
            block = dst_s[0, g * SUB + s]
            staged[pl.ds(g * TARGET + s, 8, stride=SUB), :] = world[pl.ds(block, 8, stride=stride), :]
        return carry

    lax.fori_loop(0, dst_s.shape[1] // SUB, stage_remote, 0, unroll=4)

    def stage_local(g, carry):
        for s in range(SUB):
            a, b = pairs_s[0, g * SUB + s], pairs_s[1, g * SUB + s]
            targets[pl.ds(g * TARGET + s, 8, stride=SUB), :] = world[pl.ds(b, 8, stride=stride), :]
            sources[pl.ds(g * SOURCE + s, 3, stride=SUB), :] = world[pl.ds(a, 3, stride=stride), :]
            sources[pl.ds(g * SOURCE + 3 * SUB + s, 6, stride=SUB), :] = world[
                pl.ds(a + 8 * stride, 6, stride=stride), :
            ]
        return carry

    lax.fori_loop(0, groups, stage_local, 0, unroll=4)

    def step(i, carry):
        done = []
        for u in range(TOGETHER):
            g = i * TOGETHER + u
            index = maps[pl.ds(pl.multiple_of(g * SUB, SUB), SUB), :]
            base = pl.multiple_of(g * SOURCE, SUB)
            source = [sources[pl.ds(base + SUB * k, SUB), :] for k in range(9)]
            base = pl.multiple_of(g * TARGET, SUB)
            target = [pick(targets[pl.ds(base + SUB * k, SUB), :], index) for k in range(8)]
            x, y, n = source[0:3], target[0:3], target[3:6]
            scalars = [dot3(n, [x[k] - y[k] for k in range(3)])]
            for v in range(2):
                scalars.append(dot3(n, source[3 + 3 * v : 6 + 3 * v]) - target[6 + v])
            done.append(pair_sums(scalars, cross(x, n), n, cross(y, n)))
        for u in range(TOGETHER):
            first = pl.multiple_of((i * TOGETHER + u) * SUB, SUB)
            for half in range(2):
                sums[pl.ds(first, SUB), half * LANE : (half + 1) * LANE] = done[u][half]
        return carry

    lax.fori_loop(0, groups // TOGETHER, step, 0)
    side_a = frag_sums(pairs_v[0:1, :], sums, per_frag)
    side_b = target_side(frag_sums(pairs_v[1:2, :], sums, per_frag))
    for half in range(2):
        totals[half * SUB : (half + 1) * SUB, :] = side_a[half] + side_b[half]


def halves_of(values):
    high = values.astype(jnp.bfloat16)
    return high, (values - high.astype(jnp.float32)).astype(jnp.bfloat16)


def remote_kernel(arrived, staged, back, sums, parts, turned, coeffs, index, partial):
    bf16, f32 = jnp.bfloat16, jnp.float32
    pairs = parts.shape[0]
    peers = pairs // SUB
    nums = lax.dot_general

    def wide(shape, axis):
        return lax.broadcasted_iota(jnp.int32, shape, axis)

    points2 = lax.bitwise_and(wide((LANE, 2 * LANE), 1), LANE - 1)
    same = (points2 == wide((LANE, 2 * LANE), 0)).astype(f32).astype(bf16)
    fields2 = lax.bitwise_and(wide((GROUP, 2 * LANE), 1), GROUP - 1)
    gather = (fields2 == wide((GROUP, 2 * LANE), 0)).astype(f32).astype(bf16)
    own = lax.shift_right_logical(iota(1), shift_of(GROUP)) == iota(0)
    partial[27 * SUB :, :] = jnp.zeros((partial.shape[0] - 27 * SUB, LANE), f32)

    def block(c, carry):
        first = c * peers

        def turn(i, left, at):
            for u in range(0, peers, 2):
                both = jnp.concatenate([at(u), at(u + 1)], axis=0)
                high, low = halves_of(both)
                parts[u * SUB : (u + 2) * SUB, i * 2 * LANE : i * 2 * LANE + LANE] = high
                parts[u * SUB : (u + 2) * SUB, i * 2 * LANE + LANE : (i + 1) * 2 * LANE] = low
            return nums(
                left,
                parts[:, i * 2 * LANE : (i + 1) * 2 * LANE],
                (((1,), (1,)), ((), ())),
                preferred_element_type=f32,
            )

        for u in range(peers):
            row = (first + u) * MSG + 3 * SUB
            index[u * SUB : (u + 1) * SUB, :] = arrived[pl.ds(row, SUB), :].astype(jnp.int32)

        def extras(u):
            row = arrived[pl.ds((first + u) * MSG + 4 * SUB, 1), :]
            return jnp.where(own, jnp.broadcast_to(row, (SUB, LANE)), 0.0)

        def target(k):
            def at(u):
                base = pl.multiple_of((first + u) * TARGET, SUB)
                return pick(staged[pl.ds(base + SUB * k, SUB), :], index[u * SUB : (u + 1) * SUB, :])

            return at

        def source(k):
            return lambda u: arrived[pl.ds((first + u) * MSG + SUB * k, SUB), :]

        coeffs[...] = turn(11, gather, extras)
        for k in range(8):
            turned[k * LANE : (k + 1) * LANE, :] = turn(k, same, target(k))
        for k in range(3):
            turned[(8 + k) * LANE : (9 + k) * LANE, :] = turn(8 + k, same, source(k))
        for t in range(0, pairs, LANE):
            lanes = slice(t, t + LANE)

            def add(i, totals):
                start = pl.multiple_of(i * SUB, SUB)
                field = [turned[pl.ds(start + k * LANE, SUB), lanes] for k in range(11)]
                way = [coeffs[j : j + 1, lanes] for j in range(12)]
                y, n, x = field[0:3], field[3:6], field[8:11]
                p, q = cross(x, n), cross(y, n)
                scalars = [dot3(n, [x[k] - y[k] for k in range(3)])]
                for v in range(2):
                    a = way[6 * v : 6 * v + 6]
                    scalars.append(dot3(p, a[0:3]) + dot3(n, a[3:6]) - field[6 + v])
                terms = []
                for s in scalars:
                    terms += [s * value for value in p + n]
                for s in scalars:
                    terms += [s * value for value in q]
                return tuple(total + term for total, term in zip(totals, terms))

            zero = jnp.zeros((SUB, LANE), f32)
            totals = lax.fori_loop(0, LANE // SUB, add, (zero,) * 27, unroll=4)
            for j in range(27):
                partial[j * SUB : (j + 1) * SUB, :] = totals[j]
            total = partial[pl.ds(0, 4 * SUB, stride=SUB), :]
            for s in range(1, SUB):
                total = total + partial[pl.ds(s, 4 * SUB, stride=SUB), :]
            at = pl.multiple_of(c * pairs, LANE) + t
            sums[:, pl.ds(at, LANE)] = total * coeffs[12:13, lanes]
        start = pl.multiple_of(c * pairs, LANE)
        high, low = halves_of(sums[:, pl.ds(start, pairs)])
        entry = wide((8 * SUB, 2 * LANE), 1)
        entry = lax.bitwise_and(entry, GROUP - 1) + GROUP * lax.shift_right_logical(entry, 7)
        place = (lax.bitwise_and(wide((8 * SUB, 2 * LANE), 0), 4 * SUB - 1) == entry).astype(f32)
        rows = nums(
            jnp.concatenate([high, low], axis=0),
            place.astype(bf16),
            (((0,), (0,)), ((), ())),
            preferred_element_type=f32,
        )
        slot = lax.bitwise_and(wide((pairs, 2 * LANE), 0), SUB - 1)
        lane = lax.bitwise_and(wide((pairs, 2 * LANE), 1), LANE - 1)
        high, low = halves_of(jnp.where(lax.shift_right_logical(lane, 4) == slot, rows, 0.0))
        mine = lax.shift_right_logical(wide((peers, pairs), 1), 3) == wide((peers, pairs), 0)
        mine = mine.astype(f32).astype(bf16)
        rows = jnp.dot(mine, high, preferred_element_type=f32) + jnp.dot(
            mine, low, preferred_element_type=f32
        )
        for half in range(2):
            back[pl.ds(2 * first + half, peers, stride=2), :] = rows[
                :, half * LANE : (half + 1) * LANE
            ]
        return carry

    lax.fori_loop(0, sums.shape[1] // pairs, block, 0)


def total_kernel(sums, dst_v, src_v, totals, frags, *, per_frag):
    slot = lax.shift_right_logical(iota(1), shift_of(GROUP))
    for q in range(0, frags.shape[0], SUB):
        block = index_tile(src_v, q * SUB, iota(0) * SUB + slot)
        frags[q : q + SUB, :] = lax.shift_right_logical(block, shift_of(per_frag))
    pairs = sums.shape[1]
    frag = lax.shift_right_logical(dst_v[...], shift_of(per_frag))
    hot = jnp.broadcast_to(frag, (SUB, pairs)) == lax.broadcasted_iota(jnp.int32, (SUB, pairs), 0)
    total = -lax.dot_general(
        sums[...],
        hot.astype(jnp.float32),
        (((1,), (1,)), ((), ())),
        precision=lax.Precision.HIGHEST,
        preferred_element_type=jnp.float32,
    )
    for k in range(3):
        totals[6 * k : 6 * k + 3, :] = total[18 + 3 * k : 21 + 3 * k, :]
        totals[6 * k + 3 : 6 * k + 6, :] = total[6 * k + 3 : 6 * k + 6, :]


def final_kernel(back, totals, extra, frags, gradient, hess, *, per_frag):
    devices = back.shape[0] // 2
    sums = [[jnp.zeros((SUB, LANE), jnp.float32) for half in range(2)] for f in range(SUB)]
    for q in range(0, devices, SUB):
        frag = frags[q : q + SUB, :]
        for half in range(2):
            rows = back[pl.ds(2 * q + half, SUB, stride=2), :]
            for f in range(SUB):
                sums[f][half] = sums[f][half] + jnp.where(frag == f, rows, 0.0)
    halves = []
    for half in range(2):
        tile = jnp.zeros((SUB, LANE), jnp.float32)
        for f in range(SUB):
            tile = jnp.where(iota(0) == f, jnp.sum(sums[f][half], axis=0, keepdims=True), tile)
        for step in (64, 32, 16):
            tile = tile + pltpu.roll(tile, step, 1)
        halves.append(tile + totals[half * SUB : (half + 1) * SUB, :])
    total = jnp.where(iota(1) < GROUP, halves[0], halves[1]).T[0:18, :] + extra[...]
    gradient[...] = total[0:6, :] * (1.0 / LANE)
    for v in range(2):
        part = total[6 + 6 * v : 12 + 6 * v, :] * (1.0 / (LANE * per_frag))
        for j in range(6):
            hess[j, v : v + 1, :] = part[j : j + 1, :]


def call(kernel, outs, scratch, spaces, limit=VMEM_LIMIT, **more):
    kinds = {"v": pltpu.VMEM, "s": pltpu.SMEM, "h": pltpu.HBM}
    return pl.pallas_call(
        kernel,
        out_shape=outs,
        in_specs=[pl.BlockSpec(memory_space=kinds[s]) for s in spaces],
        out_specs=[pl.BlockSpec(memory_space=pltpu.VMEM)] * len(outs),
        scratch_shapes=scratch,
        compiler_params=pltpu.CompilerParams(vmem_limit_bytes=limit),
        **more,
    )


def in_hbm(values):
    return pltpu.with_memory_space_constraint(values, pltpu.HBM)


def exchange(rows, devices):
    sent = rows.reshape(devices, 1, -1)
    sent = lax.all_to_all(sent, AXES, split_axis=0, concat_axis=0, tiled=True)
    return sent.reshape(rows.shape)


def local(
    points, normals, poses, directions, local_pairs, local_maps,
    remote_src, remote_maps, remote_dst, counts,
):
    devices = lax.axis_size("tile") * lax.axis_size("band")
    blocks, _, count = points.shape
    frags = poses.shape[1]
    slots = remote_src.shape[1]
    pairs = local_pairs.shape[1]
    assert count == LANE and frags == SUB and slots == devices * SUB and devices % PEERS == 0
    per_frag = blocks // frags
    stride = blocks + SUB
    f32 = jnp.float32
    points = points.transpose(1, 0, 2)
    normals = normals.transpose(1, 0, 2)
    directions = directions.transpose(1, 0, 2)

    def array(*shape):
        return jax.ShapeDtypeStruct(shape, f32)

    def vmem(*shape, dtype=f32):
        return pltpu.VMEM(shape, dtype)

    (message,) = call(
        pack_kernel,
        [pltpu.VMEM((devices * MSG, LANE), f32)],
        [
            vmem(3, blocks, LANE),
            pltpu.SMEM((6, frags), f32),
            vmem(6, 2, frags),
            pltpu.SMEM((1, slots), jnp.int32),
            vmem(1, slots, dtype=jnp.int32),
            vmem(slots, LANE, dtype=jnp.int32),
            vmem(1, devices, dtype=jnp.int32),
            vmem(3 * stride, LANE),
            vmem(2 * SUB, LANE),
            pltpu.SemaphoreType.DMA((7,)),
        ],
        "hhhhhh",
        limit=PACK_LIMIT,
    )(*[in_hbm(x) for x in (points, poses, directions, remote_src, remote_maps[0], counts)])
    arrived = exchange(message, devices)
    staged, totals = call(
        local_kernel,
        [array(devices * TARGET, LANE), array(2 * SUB, LANE)],
        [
            vmem(14 * stride, LANE),
            vmem(pairs // SUB * SOURCE, LANE),
            vmem(pairs // SUB * TARGET, LANE),
            vmem(pairs, 2 * LANE),
        ],
        "vvvvsvvs",
        cost_estimate=pl.CostEstimate(
            flops=200 * pairs * LANE, bytes_accessed=4_000_000, transcendentals=0
        ),
    )(points, normals, poses, directions, local_pairs, local_pairs, local_maps, remote_dst)
    part = PEERS * SUB
    back, sums = call(
        remote_kernel,
        [array(devices * 2, LANE), array(4 * SUB, slots)],
        [
            vmem(part, 12 * 2 * LANE, dtype=jnp.bfloat16),
            vmem(11 * LANE, part),
            vmem(GROUP, part),
            vmem(part, LANE, dtype=jnp.int32),
            vmem(4 * SUB * SUB, LANE),
        ],
        "vv",
    )(arrived, staged)
    back = exchange(back, devices)
    extra, table = call(
        functools.partial(total_kernel, per_frag=per_frag),
        [array(18, frags), jax.ShapeDtypeStruct((devices, LANE), jnp.int32)],
        [],
        "vvv",
        cost_estimate=pl.CostEstimate(
            flops=2 * SUB * slots * 2 * LANE, bytes_accessed=1_000_000, transcendentals=0
        ),
    )(sums, remote_dst, remote_src)
    gradient, hess = call(
        functools.partial(final_kernel, per_frag=per_frag),
        [array(6, frags), array(6, 2, frags)],
        [],
        "vvvv",
    )(back, totals, extra, table)
    return (gradient, hess.transpose(1, 0, 2))


def solution(mesh):
    placed = (
        P(AXES, None, None),
        P(AXES, None, None),
        P(None, AXES),
        P(None, None, AXES),
        P(None, AXES),
        P(AXES, None),
        P(AXES, None),
        P(AXES, None, None),
        P(AXES, None),
        P(AXES, None),
    )
    return jax.shard_map(
        local,
        mesh=mesh,
        in_specs=placed,
        out_specs=(P(None, AXES), P(None, None, AXES)),
        check_vma=False,
    )
```

```python
import functools

import jax
import jax.numpy as jnp
from jax import lax
from jax.experimental import pallas as pl
from jax.experimental.pallas import tpu as pltpu
from jax.sharding import PartitionSpec as P

AXES = ("tile", "band")
SUB = 8
LANE = 128
MSG = 4 * SUB + 1
TARGET = 8 * SUB
SOURCE = 9 * SUB
TOGETHER = 4
GROUP = 16
VMEM_LIMIT = 16 * 1024 * 1024
PACK_LIMIT = 56 * 1024 * 1024
PEERS = 32


def iota(axis):
    return lax.broadcasted_iota(jnp.int32, (SUB, LANE), axis)


def pick(values, index):
    values = jnp.broadcast_to(values, (SUB, LANE))
    return jnp.take_along_axis(values, index, axis=1, mode="promise_in_bounds")


def shift_of(size):
    shift = size.bit_length() - 1
    assert 1 << shift == size
    return shift


def rotations(poses):
    half = [poses[i : i + 1, :] * 0.5 for i in range(3)]
    w = 1.0 / jnp.sqrt(1.0 + half[0] * half[0] + half[1] * half[1] + half[2] * half[2])
    x, y, z = half[0] * w, half[1] * w, half[2] * w
    rotation = [
        [1.0 - 2.0 * (y * y + z * z), 2.0 * (x * y - w * z), 2.0 * (x * z + w * y)],
        [2.0 * (x * y + w * z), 1.0 - 2.0 * (x * x + z * z), 2.0 * (y * z - w * x)],
        [2.0 * (x * z - w * y), 2.0 * (y * z + w * x), 1.0 - 2.0 * (x * x + y * y)],
    ]
    return rotation, [poses[i : i + 1, :] for i in range(3, 6)]


def cross(left, right):
    return [
        left[1] * right[2] - left[2] * right[1],
        left[2] * right[0] - left[0] * right[2],
        left[0] * right[1] - left[1] * right[0],
    ]


def dot3(left, right):
    return left[0] * right[0] + left[1] * right[1] + left[2] * right[2]


def spread(row, f):
    return jnp.broadcast_to(row[:, f : f + 1], (SUB, LANE))


def splat_rotation(poses, f):
    half = [jnp.full((SUB, LANE), poses[i, f] * 0.5, jnp.float32) for i in range(3)]
    w = 1.0 / jnp.sqrt(1.0 + half[0] * half[0] + half[1] * half[1] + half[2] * half[2])
    x, y, z = half[0] * w, half[1] * w, half[2] * w
    rotation = [
        [1.0 - 2.0 * (y * y + z * z), 2.0 * (x * y - w * z), 2.0 * (x * z + w * y)],
        [2.0 * (x * y + w * z), 1.0 - 2.0 * (x * x + z * z), 2.0 * (y * z - w * x)],
        [2.0 * (x * z - w * y), 2.0 * (y * z + w * x), 1.0 - 2.0 * (x * x + y * y)],
    ]
    return rotation, [jnp.full((SUB, LANE), poses[i, f], jnp.float32) for i in range(3, 6)]


def write_points(points, poses, world):
    blocks, frags = points.shape[1], poses.shape[1]
    per_frag, stride = blocks // frags, blocks + SUB
    for f in range(frags):
        turn, move = splat_rotation(poses, f)
        for b in range(f * per_frag, (f + 1) * per_frag, SUB):
            x = [points[j, b : b + SUB, :] for j in range(3)]
            for i in range(3):
                world[pl.ds(i * stride + b, SUB), :] = dot3(turn[i], x) + move[i]


def write_fields(points, normals, poses, directions, world):
    blocks, frags = points.shape[1], poses.shape[1]
    per_frag, stride = blocks // frags, blocks + SUB
    rotation, translation = rotations(poses[...])
    for f in range(frags):
        turn = [[spread(rotation[i][j], f) for j in range(3)] for i in range(3)]
        move = [spread(translation[i], f) for i in range(3)]
        way = [[spread(directions[j, v : v + 1, :], f) for j in range(6)] for v in range(2)]
        for b in range(f * per_frag, (f + 1) * per_frag, SUB):
            x = [points[j, b : b + SUB, :] for j in range(3)]
            m = [normals[j, b : b + SUB, :] for j in range(3)]
            y = [dot3(turn[i], x) + move[i] for i in range(3)]
            n = [dot3(turn[i], m) for i in range(3)]
            speed = []
            for v in range(2):
                swing = cross(way[v][0:3], y)
                speed.append([swing[i] + way[v][3 + i] for i in range(3)])
            along = [dot3(n, speed[v]) for v in range(2)]
            for i, row in enumerate(y + n + along + speed[0] + speed[1]):
                world[pl.ds(i * stride + b, SUB), :] = row


def index_tile(row_ref, first, offset):
    tile = first // LANE * LANE
    return pick(row_ref[0:1, pl.ds(tile, LANE)], offset + first % LANE)


def pack_kernel(
    points_h, poses_h, directions_h, src_h, maps_h, counts_h, out,
    points, poses, directions, src_s, src_v, maps, used, world, table, sems,
):
    devices = counts_h.shape[1]
    per_frag = points.shape[1] // poses.shape[1]
    stride = points.shape[1] + SUB
    pairs = [
        (directions_h, directions), (src_h, src_v), (counts_h, used), (poses_h, poses),
        (points_h, points), (src_h, src_s), (maps_h, maps),
    ]
    copies = [pltpu.make_async_copy(a, b, sems.at[i]) for i, (a, b) in enumerate(pairs)]
    for copy in copies:
        copy.start()
    for copy in copies[0:3]:
        copy.wait()
    frags = directions.shape[2]
    for v in range(2):
        for j in range(6):
            table[6 * v + j : 6 * v + j + 1, 0:frags] = directions[j, v : v + 1, :]
    limits = jnp.broadcast_to(used[0:1, :], (SUB, devices)).astype(jnp.float32)
    peers = lax.broadcasted_iota(jnp.int32, (SUB, devices), 1)
    row = lax.broadcasted_iota(jnp.int32, (SUB, devices), 0)
    slot = lax.shift_right_logical(iota(1), shift_of(GROUP))
    field = lax.bitwise_and(iota(1), GROUP - 1)
    for q in range(0, devices, SUB):
        block = index_tile(src_v, q * SUB, iota(0) * SUB + slot)
        frag = lax.shift_right_logical(block, shift_of(per_frag))
        limit = jnp.sum(jnp.where(peers == row + q, limits, 0.0), axis=1, keepdims=True)
        extras = jnp.where(slot.astype(jnp.float32) < limit, 1.0, 0.0)
        for j in range(12):
            extras = jnp.where(field == j, pick(table[j : j + 1, :], frag), extras)
        extras = jnp.where(field == 13, frag.astype(jnp.float32), extras)
        out[pl.ds(q * MSG + MSG - 1, SUB, stride=MSG), :] = extras
    for copy in copies[3:]:
        copy.wait()
    write_points(points, poses, world)

    def peer(p):
        for s in range(SUB):
            block = src_s[0, p * SUB + s]
            out[pl.ds(p * MSG + s, 3, stride=SUB), :] = world[pl.ds(block, 3, stride=stride), :]
        rows = maps[pl.ds(pl.multiple_of(p * SUB, SUB), SUB), :]
        out[pl.ds(p * MSG + 3 * SUB, SUB), :] = rows.astype(jnp.float32)

    def pack(i, carry):
        for u in range(SUB):
            peer(i * SUB + u)
        return carry

    lax.fori_loop(0, devices // SUB, pack, 0)


def pair_sums(scalars, p, n, q):
    field = lax.bitwise_and(iota(1), GROUP - 1)
    tiles = [jnp.zeros((SUB, LANE), jnp.float32) for half in range(2)]
    for k, s in enumerate(scalars):
        for c in range(3):
            for at, value in ((6 * k + c, p[c]), (6 * k + 3 + c, n[c]), (18 + 3 * k + c, q[c])):
                total = jnp.sum(s * value, axis=1, keepdims=True)
                half = at // GROUP
                tiles[half] = jnp.where(field == at % GROUP, total, tiles[half])
    return tiles


def frag_sums(row, sums, per_frag):
    pairs = sums.shape[0]
    frag = lax.shift_right_logical(row, shift_of(per_frag))
    hot = jnp.broadcast_to(frag, (SUB, pairs)) == lax.broadcasted_iota(jnp.int32, (SUB, pairs), 0)
    total = jnp.dot(
        hot.astype(jnp.float32),
        sums[...],
        precision=lax.Precision.HIGHEST,
        preferred_element_type=jnp.float32,
    )
    return [total[:, 0:LANE], total[:, LANE:]]


def target_side(sums):
    lane = lax.bitwise_and(iota(1), GROUP - 1)
    k = (lane >= 6).astype(jnp.int32) + (lane >= 12).astype(jnp.int32)
    c = lane - 6 * k
    first = jnp.where(c < 3, pick(sums[1], jnp.minimum(2 + 3 * k + c, GROUP - 1)), sums[0])
    return [-first, -sums[1]]


def local_kernel(
    points, normals, poses, directions, pairs_s, pairs_v, maps, dst_s,
    staged, totals, world, sources, targets, sums,
):
    per_frag = points.shape[1] // poses.shape[1]
    stride = points.shape[1] + SUB
    groups = pairs_s.shape[1] // SUB
    write_fields(points, normals, poses, directions, world)

    def stage_remote(g, carry):
        for s in range(SUB):
            block = dst_s[0, g * SUB + s]
            staged[pl.ds(g * TARGET + s, 8, stride=SUB), :] = world[pl.ds(block, 8, stride=stride), :]
        return carry

    lax.fori_loop(0, dst_s.shape[1] // SUB, stage_remote, 0, unroll=4)

    def stage_local(g, carry):
        for s in range(SUB):
            a, b = pairs_s[0, g * SUB + s], pairs_s[1, g * SUB + s]
            targets[pl.ds(g * TARGET + s, 8, stride=SUB), :] = world[pl.ds(b, 8, stride=stride), :]
            sources[pl.ds(g * SOURCE + s, 3, stride=SUB), :] = world[pl.ds(a, 3, stride=stride), :]
            sources[pl.ds(g * SOURCE + 3 * SUB + s, 6, stride=SUB), :] = world[
                pl.ds(a + 8 * stride, 6, stride=stride), :
            ]
        return carry

    lax.fori_loop(0, groups, stage_local, 0, unroll=4)

    def step(i, carry):
        done = []
        for u in range(TOGETHER):
            g = i * TOGETHER + u
            index = maps[pl.ds(pl.multiple_of(g * SUB, SUB), SUB), :]
            base = pl.multiple_of(g * SOURCE, SUB)
            source = [sources[pl.ds(base + SUB * k, SUB), :] for k in range(9)]
            base = pl.multiple_of(g * TARGET, SUB)
            target = [pick(targets[pl.ds(base + SUB * k, SUB), :], index) for k in range(8)]
            x, y, n = source[0:3], target[0:3], target[3:6]
            scalars = [dot3(n, [x[k] - y[k] for k in range(3)])]
            for v in range(2):
                scalars.append(dot3(n, source[3 + 3 * v : 6 + 3 * v]) - target[6 + v])
            done.append(pair_sums(scalars, cross(x, n), n, cross(y, n)))
        for u in range(TOGETHER):
            first = pl.multiple_of((i * TOGETHER + u) * SUB, SUB)
            for half in range(2):
                sums[pl.ds(first, SUB), half * LANE : (half + 1) * LANE] = done[u][half]
        return carry

    lax.fori_loop(0, groups // TOGETHER, step, 0)
    side_a = frag_sums(pairs_v[0:1, :], sums, per_frag)
    side_b = target_side(frag_sums(pairs_v[1:2, :], sums, per_frag))
    for half in range(2):
        totals[half * SUB : (half + 1) * SUB, :] = side_a[half] + side_b[half]


def halves_of(values):
    high = values.astype(jnp.bfloat16)
    return high, (values - high.astype(jnp.float32)).astype(jnp.bfloat16)


def remote_kernel(arrived, staged, back, sums, parts, turned, coeffs, index, partial, frags):
    bf16, f32 = jnp.bfloat16, jnp.float32
    pairs = parts.shape[0]
    peers = pairs // SUB
    nums = lax.dot_general

    def wide(shape, axis):
        return lax.broadcasted_iota(jnp.int32, shape, axis)

    points2 = lax.bitwise_and(wide((LANE, 2 * LANE), 1), LANE - 1)
    same = (points2 == wide((LANE, 2 * LANE), 0)).astype(f32).astype(bf16)
    fields2 = lax.bitwise_and(wide((GROUP, 2 * LANE), 1), GROUP - 1)
    gather = (fields2 == wide((GROUP, 2 * LANE), 0)).astype(f32).astype(bf16)
    own = lax.shift_right_logical(iota(1), shift_of(GROUP)) == iota(0)
    partial[27 * SUB :, :] = jnp.zeros((partial.shape[0] - 27 * SUB, LANE), f32)

    def block(c, carry):
        first = c * peers

        def turn(i, left, at):
            for u in range(0, peers, 2):
                both = jnp.concatenate([at(u), at(u + 1)], axis=0)
                high, low = halves_of(both)
                parts[u * SUB : (u + 2) * SUB, i * 2 * LANE : i * 2 * LANE + LANE] = high
                parts[u * SUB : (u + 2) * SUB, i * 2 * LANE + LANE : (i + 1) * 2 * LANE] = low
            return nums(
                left,
                parts[:, i * 2 * LANE : (i + 1) * 2 * LANE],
                (((1,), (1,)), ((), ())),
                preferred_element_type=f32,
            )

        for u in range(peers):
            row = (first + u) * MSG + 3 * SUB
            index[u * SUB : (u + 1) * SUB, :] = arrived[pl.ds(row, SUB), :].astype(jnp.int32)

        def extras(u):
            row = arrived[pl.ds((first + u) * MSG + 4 * SUB, 1), :]
            frags[u * SUB : (u + 1) * SUB, :] = pick(row, iota(0) * GROUP + 13)
            return jnp.where(own, jnp.broadcast_to(row, (SUB, LANE)), 0.0)

        def target(k):
            def at(u):
                base = pl.multiple_of((first + u) * TARGET, SUB)
                return pick(staged[pl.ds(base + SUB * k, SUB), :], index[u * SUB : (u + 1) * SUB, :])

            return at

        def source(k):
            return lambda u: arrived[pl.ds((first + u) * MSG + SUB * k, SUB), :]

        coeffs[...] = turn(11, gather, extras)
        for k in range(8):
            turned[k * LANE : (k + 1) * LANE, :] = turn(k, same, target(k))
        for k in range(3):
            turned[(8 + k) * LANE : (9 + k) * LANE, :] = turn(8 + k, same, source(k))
        for t in range(0, pairs, LANE):
            lanes = slice(t, t + LANE)

            def add(i, totals):
                start = pl.multiple_of(i * SUB, SUB)
                field = [turned[pl.ds(start + k * LANE, SUB), lanes] for k in range(11)]
                way = [coeffs[j : j + 1, lanes] for j in range(12)]
                y, n, x = field[0:3], field[3:6], field[8:11]
                p, q = cross(x, n), cross(y, n)
                scalars = [dot3(n, [x[k] - y[k] for k in range(3)])]
                for v in range(2):
                    a = way[6 * v : 6 * v + 6]
                    scalars.append(dot3(p, a[0:3]) + dot3(n, a[3:6]) - field[6 + v])
                terms = []
                for s in scalars:
                    terms += [s * value for value in p + n]
                for s in scalars:
                    terms += [s * value for value in q]
                return tuple(total + term for total, term in zip(totals, terms))

            zero = jnp.zeros((SUB, LANE), f32)
            totals = lax.fori_loop(0, LANE // SUB, add, (zero,) * 27, unroll=4)
            for j in range(27):
                partial[j * SUB : (j + 1) * SUB, :] = totals[j]
            total = partial[pl.ds(0, 4 * SUB, stride=SUB), :]
            for s in range(1, SUB):
                total = total + partial[pl.ds(s, 4 * SUB, stride=SUB), :]
            at = pl.multiple_of(c * pairs, LANE) + t
            sums[:, pl.ds(at, LANE)] = total * coeffs[12:13, lanes]
        start = pl.multiple_of(c * pairs, LANE)
        high, low = halves_of(sums[:, pl.ds(start, pairs)])
        entry = wide((8 * SUB, 2 * LANE), 1)
        entry = lax.bitwise_and(entry, GROUP - 1) + GROUP * lax.shift_right_logical(entry, 7)
        place = (lax.bitwise_and(wide((8 * SUB, 2 * LANE), 0), 4 * SUB - 1) == entry).astype(f32)
        rows = nums(
            jnp.concatenate([high, low], axis=0),
            place.astype(bf16),
            (((0,), (0,)), ((), ())),
            preferred_element_type=f32,
        )
        frag = jnp.concatenate([frags[...], frags[...]], axis=1)
        lane = lax.bitwise_and(wide((pairs, 2 * LANE), 1), LANE - 1)
        place = lax.shift_right_logical(lane, 4).astype(f32) == frag
        high, low = halves_of(jnp.where(place, rows, 0.0))
        mine = lax.shift_right_logical(wide((peers, pairs), 1), 3) == wide((peers, pairs), 0)
        mine = mine.astype(f32).astype(bf16)
        rows = jnp.dot(mine, high, preferred_element_type=f32) + jnp.dot(
            mine, low, preferred_element_type=f32
        )
        for half in range(2):
            back[pl.ds(2 * first + half, peers, stride=2), :] = rows[
                :, half * LANE : (half + 1) * LANE
            ]
        return carry

    lax.fori_loop(0, sums.shape[1] // pairs, block, 0)


def total_kernel(sums, dst_v, totals, *, per_frag):
    pairs = sums.shape[1]
    frag = lax.shift_right_logical(dst_v[...], shift_of(per_frag))
    hot = jnp.broadcast_to(frag, (SUB, pairs)) == lax.broadcasted_iota(jnp.int32, (SUB, pairs), 0)
    total = -lax.dot_general(
        sums[...],
        hot.astype(jnp.float32),
        (((1,), (1,)), ((), ())),
        precision=lax.Precision.HIGHEST,
        preferred_element_type=jnp.float32,
    )
    for k in range(3):
        totals[6 * k : 6 * k + 3, :] = total[18 + 3 * k : 21 + 3 * k, :]
        totals[6 * k + 3 : 6 * k + 6, :] = total[6 * k + 3 : 6 * k + 6, :]


def final_kernel(back, totals, extra, gradient, hess, *, per_frag):
    index = iota(0) * GROUP + lax.bitwise_and(iota(1), GROUP - 1)
    halves = [
        pick(back[half : half + 1, :], index) + totals[half * SUB : (half + 1) * SUB, :]
        for half in range(2)
    ]
    total = jnp.where(iota(1) < GROUP, halves[0], halves[1]).T[0:18, :] + extra[...]
    gradient[...] = total[0:6, :] * (1.0 / LANE)
    for v in range(2):
        part = total[6 + 6 * v : 12 + 6 * v, :] * (1.0 / (LANE * per_frag))
        for j in range(6):
            hess[j, v : v + 1, :] = part[j : j + 1, :]


def call(kernel, outs, scratch, spaces, limit=VMEM_LIMIT, **more):
    kinds = {"v": pltpu.VMEM, "s": pltpu.SMEM, "h": pltpu.HBM}
    return pl.pallas_call(
        kernel,
        out_shape=outs,
        in_specs=[pl.BlockSpec(memory_space=kinds[s]) for s in spaces],
        out_specs=[pl.BlockSpec(memory_space=pltpu.VMEM)] * len(outs),
        scratch_shapes=scratch,
        compiler_params=pltpu.CompilerParams(vmem_limit_bytes=limit),
        **more,
    )


def in_hbm(values):
    return pltpu.with_memory_space_constraint(values, pltpu.HBM)


def exchange(rows, devices):
    sent = rows.reshape(devices, 1, -1)
    sent = lax.all_to_all(sent, AXES, split_axis=0, concat_axis=0, tiled=True)
    return sent.reshape(rows.shape)


def local(
    points, normals, poses, directions, local_pairs, local_maps,
    remote_src, remote_maps, remote_dst, counts,
):
    devices = lax.axis_size("tile") * lax.axis_size("band")
    blocks, _, count = points.shape
    frags = poses.shape[1]
    slots = remote_src.shape[1]
    pairs = local_pairs.shape[1]
    assert count == LANE and frags == SUB and slots == devices * SUB and devices % PEERS == 0
    per_frag = blocks // frags
    stride = blocks + SUB
    f32 = jnp.float32
    points = points.transpose(1, 0, 2)
    normals = normals.transpose(1, 0, 2)
    directions = directions.transpose(1, 0, 2)

    def array(*shape):
        return jax.ShapeDtypeStruct(shape, f32)

    def vmem(*shape, dtype=f32):
        return pltpu.VMEM(shape, dtype)

    (message,) = call(
        pack_kernel,
        [pltpu.VMEM((devices * MSG, LANE), f32)],
        [
            vmem(3, blocks, LANE),
            pltpu.SMEM((6, frags), f32),
            vmem(6, 2, frags),
            pltpu.SMEM((1, slots), jnp.int32),
            vmem(1, slots, dtype=jnp.int32),
            vmem(slots, LANE, dtype=jnp.int32),
            vmem(1, devices, dtype=jnp.int32),
            vmem(3 * stride, LANE),
            vmem(2 * SUB, LANE),
            pltpu.SemaphoreType.DMA((7,)),
        ],
        "hhhhhh",
        limit=PACK_LIMIT,
    )(*[in_hbm(x) for x in (points, poses, directions, remote_src, remote_maps[0], counts)])
    arrived = exchange(message, devices)
    staged, totals = call(
        local_kernel,
        [array(devices * TARGET, LANE), array(2 * SUB, LANE)],
        [
            vmem(14 * stride, LANE),
            vmem(pairs // SUB * SOURCE, LANE),
            vmem(pairs // SUB * TARGET, LANE),
            vmem(pairs, 2 * LANE),
        ],
        "vvvvsvvs",
        cost_estimate=pl.CostEstimate(
            flops=200 * pairs * LANE, bytes_accessed=4_000_000, transcendentals=0
        ),
    )(points, normals, poses, directions, local_pairs, local_pairs, local_maps, remote_dst)
    part = PEERS * SUB
    back, sums = call(
        remote_kernel,
        [array(devices * 2, LANE), array(4 * SUB, slots)],
        [
            vmem(part, 12 * 2 * LANE, dtype=jnp.bfloat16),
            vmem(11 * LANE, part),
            vmem(GROUP, part),
            vmem(part, LANE, dtype=jnp.int32),
            vmem(4 * SUB * SUB, LANE),
            vmem(part, LANE),
        ],
        "vv",
    )(arrived, staged)
    back = back.reshape(devices, 1, 2 * LANE)
    back = lax.psum_scatter(back, AXES, scatter_dimension=0, tiled=True).reshape(2, LANE)
    (extra,) = call(
        functools.partial(total_kernel, per_frag=per_frag),
        [array(18, frags)],
        [],
        "vv",
        cost_estimate=pl.CostEstimate(
            flops=2 * SUB * slots * 2 * LANE, bytes_accessed=1_000_000, transcendentals=0
        ),
    )(sums, remote_dst)
    gradient, hess = call(
        functools.partial(final_kernel, per_frag=per_frag),
        [array(6, frags), array(6, 2, frags)],
        [],
        "vvv",
    )(back, totals, extra)
    return (gradient, hess.transpose(1, 0, 2))


def solution(mesh):
    placed = (
        P(AXES, None, None),
        P(AXES, None, None),
        P(None, AXES),
        P(None, None, AXES),
        P(None, AXES),
        P(AXES, None),
        P(AXES, None),
        P(AXES, None, None),
        P(AXES, None),
        P(AXES, None),
    )
    return jax.shard_map(
        local,
        mesh=mesh,
        in_specs=placed,
        out_specs=(P(None, AXES), P(None, None, AXES)),
        check_vma=False,
    )
```

```python
import functools

import jax
import jax.numpy as jnp
from jax import lax
from jax.experimental import pallas as pl
from jax.experimental.pallas import tpu as pltpu
from jax.sharding import PartitionSpec as P

AXES = ("tile", "band")
SUB = 8
LANE = 128
MSG = 4 * SUB + 1
TARGET = 6 * SUB
SOURCE = 3 * SUB
ROWS = 32
GROUP = 16
VMEM_LIMIT = 16 * 1024 * 1024
PACK_LIMIT = 56 * 1024 * 1024
PEERS = 32


def iota(axis):
    return lax.broadcasted_iota(jnp.int32, (SUB, LANE), axis)


def pick(values, index):
    values = jnp.broadcast_to(values, (SUB, LANE))
    return jnp.take_along_axis(values, index, axis=1, mode="promise_in_bounds")


def shift_of(size):
    shift = size.bit_length() - 1
    assert 1 << shift == size
    return shift


def cross(left, right):
    return [
        left[1] * right[2] - left[2] * right[1],
        left[2] * right[0] - left[0] * right[2],
        left[0] * right[1] - left[1] * right[0],
    ]


def dot3(left, right):
    return left[0] * right[0] + left[1] * right[1] + left[2] * right[2]


def splat_rotation(poses, f):
    half = [jnp.full((SUB, LANE), poses[i, f] * 0.5, jnp.float32) for i in range(3)]
    w = 1.0 / jnp.sqrt(1.0 + half[0] * half[0] + half[1] * half[1] + half[2] * half[2])
    x, y, z = half[0] * w, half[1] * w, half[2] * w
    rotation = [
        [1.0 - 2.0 * (y * y + z * z), 2.0 * (x * y - w * z), 2.0 * (x * z + w * y)],
        [2.0 * (x * y + w * z), 1.0 - 2.0 * (x * x + z * z), 2.0 * (y * z - w * x)],
        [2.0 * (x * z - w * y), 2.0 * (y * z + w * x), 1.0 - 2.0 * (x * x + y * y)],
    ]
    return rotation, [jnp.full((SUB, LANE), poses[i, f], jnp.float32) for i in range(3, 6)]


def write_world(fields, poses, world):
    blocks, frags = fields[0].shape[1], poses.shape[1]
    per_frag, stride = blocks // frags, blocks + SUB
    for f in range(frags):
        turn, move = splat_rotation(poses, f)
        for b in range(f * per_frag, (f + 1) * per_frag, SUB):
            for at, field in enumerate(fields):
                x = [field[j, b : b + SUB, :] for j in range(3)]
                for i in range(3):
                    row = dot3(turn[i], x)
                    world[pl.ds((3 * at + i) * stride + b, SUB), :] = row + move[i] if at == 0 else row


def write_directions(directions, table):
    frags = directions.shape[2]
    for v in range(2):
        for j in range(6):
            table[6 * v + j : 6 * v + j + 1, 0:frags] = directions[j, v : v + 1, :]


def index_tile(row_ref, first, offset):
    tile = first // LANE * LANE
    return pick(row_ref[0:1, pl.ds(tile, LANE)], offset + first % LANE)


def pack_kernel(
    points_h, poses_h, directions_h, src_h, maps_h, counts_h, out_h,
    points, poses, directions, src_s, src_v, maps, used, world, table, out, sems, out_sems,
):
    devices = counts_h.shape[1]
    per_frag = points.shape[1] // poses.shape[1]
    stride = points.shape[1] + SUB
    pairs = [
        (directions_h, directions), (src_h, src_v), (counts_h, used), (poses_h, poses),
        (points_h, points), (src_h, src_s), (maps_h, maps),
    ]
    copies = [pltpu.make_async_copy(a, b, sems.at[i]) for i, (a, b) in enumerate(pairs)]
    for copy in copies:
        copy.start()
    for copy in copies[0:3]:
        copy.wait()
    write_directions(directions, table)
    limits = jnp.broadcast_to(used[0:1, :], (SUB, devices)).astype(jnp.float32)
    peers = lax.broadcasted_iota(jnp.int32, (SUB, devices), 1)
    row = lax.broadcasted_iota(jnp.int32, (SUB, devices), 0)
    slot = lax.shift_right_logical(iota(1), shift_of(GROUP))
    field = lax.bitwise_and(iota(1), GROUP - 1)
    for q in range(0, devices, SUB):
        block = index_tile(src_v, q * SUB, iota(0) * SUB + slot)
        frag = lax.shift_right_logical(block, shift_of(per_frag))
        limit = jnp.sum(jnp.where(peers == row + q, limits, 0.0), axis=1, keepdims=True)
        extras = jnp.where(slot.astype(jnp.float32) < limit, 1.0, 0.0)
        for j in range(12):
            extras = jnp.where(field == j, pick(table[j : j + 1, :], frag), extras)
        extras = jnp.where(field == 13, frag.astype(jnp.float32), extras)
        out[pl.ds(q * MSG + MSG - 1, SUB, stride=MSG), :] = extras
    for copy in copies[3:]:
        copy.wait()
    write_world([points], poses, world)

    def peer(p):
        for s in range(SUB):
            block = src_s[0, p * SUB + s]
            out[pl.ds(p * MSG + s, 3, stride=SUB), :] = world[pl.ds(block, 3, stride=stride), :]
        rows = maps[pl.ds(pl.multiple_of(p * SUB, SUB), SUB), :]
        out[pl.ds(p * MSG + 3 * SUB, SUB), :] = rows.astype(jnp.float32)

    def piece(i):
        rows = pl.ds(pl.multiple_of(i * SUB * MSG, SUB), SUB * MSG)
        return pltpu.make_async_copy(out.at[rows], out_h.at[rows], out_sems.at[i])

    def pack(i, carry):
        for u in range(SUB):
            peer(i * SUB + u)
        piece(i).start()
        return carry

    lax.fori_loop(0, devices // SUB, pack, 0)
    for i in range(devices // SUB):
        piece(i).wait()


def halves_of(values):
    high = values.astype(jnp.bfloat16)
    return high, (values - high.astype(jnp.float32)).astype(jnp.bfloat16)


def turn(at, left, parts, i):
    columns = i * 2 * LANE
    for u in range(0, parts.shape[0] // SUB, 2):
        high, low = halves_of(jnp.concatenate([at(u), at(u + 1)], axis=0))
        parts[u * SUB : (u + 2) * SUB, columns : columns + LANE] = high
        parts[u * SUB : (u + 2) * SUB, columns + LANE : columns + 2 * LANE] = low
    return lax.dot_general(
        left,
        parts[:, columns : columns + 2 * LANE],
        (((1,), (1,)), ((), ())),
        preferred_element_type=jnp.float32,
    )


def turn_fields(source, target, index, same, parts, turned):
    for k in range(6):

        def at(u, k=k):
            return pick(target(u, k), index(u))

        turned[k * LANE : (k + 1) * LANE, :] = turn(at, same, parts, k)
    for k in range(3):
        turned[(6 + k) * LANE : (7 + k) * LANE, :] = turn(
            lambda u, k=k: source(u, k), same, parts, 6 + k
        )


def join_directions(side_a, side_b, joined):
    joined[0:12, :] = side_a[0:12, :]
    for v in range(2):
        joined[6 * v + 3 : 6 * v + 6, :] = side_a[6 * v + 3 : 6 * v + 6, :] - side_b[6 * v + 3 : 6 * v + 6, :]
        joined[12 + 3 * v : 15 + 3 * v, :] = side_b[6 * v : 6 * v + 3, :]


def point_sums(turned, joined, partial, lanes):
    def add(i, totals):
        start = pl.multiple_of(i * SUB, SUB)
        field = [turned[pl.ds(start + k * LANE, SUB), lanes] for k in range(9)]
        way = [joined[j : j + 1, lanes] for j in range(18)]
        y, n, x = field[0:3], field[3:6], field[6:9]
        p, q = cross(x, n), cross(y, n)
        scalars = [dot3(n, [x[k] - y[k] for k in range(3)])]
        for v in range(2):
            a, b = way[6 * v : 6 * v + 6], way[12 + 3 * v : 15 + 3 * v]
            scalars.append(dot3(p, a[0:3]) + dot3(n, a[3:6]) - dot3(q, b))
        terms = []
        for s in scalars:
            terms += [s * value for value in p + n]
        for s in scalars:
            terms += [s * value for value in q]
        return tuple(total + term for total, term in zip(totals, terms))

    zero = jnp.zeros((SUB, LANE), jnp.float32)
    totals = lax.fori_loop(0, LANE // SUB, add, (zero,) * 27, unroll=4)
    for j in range(27):
        partial[j * SUB : (j + 1) * SUB, :] = totals[j]
    for j in range(27, ROWS):
        partial[j * SUB : (j + 1) * SUB, :] = zero
    total = partial[pl.ds(0, ROWS, stride=SUB), :]
    for s in range(1, SUB):
        total = total + partial[pl.ds(s, ROWS, stride=SUB), :]
    return total


def frag_of(row, per_frag):
    return lax.shift_right_logical(row, shift_of(per_frag))


def look_up(table, frag, out):
    for at in range(0, frag.shape[1], LANE):
        index = jnp.broadcast_to(frag[:, at : at + LANE], (SUB, LANE))
        for j in range(0, 2 * SUB, SUB):
            out[j : j + SUB, at : at + LANE] = pick(table[j : j + SUB, :], index)


def by_frag(sums, frag):
    pairs = sums.shape[1]
    hot = jnp.broadcast_to(frag, (SUB, pairs)) == lax.broadcasted_iota(jnp.int32, (SUB, pairs), 0)
    return lax.dot_general(
        sums[...],
        hot.astype(jnp.float32),
        (((1,), (1,)), ((), ())),
        precision=lax.Precision.HIGHEST,
        preferred_element_type=jnp.float32,
    )


def target_side(total):
    rows = []
    for k in range(3):
        rows += [total[18 + 3 * k : 21 + 3 * k, :], total[6 * k + 3 : 6 * k + 6, :]]
    return -jnp.concatenate(rows, axis=0)


def constants(same, gather, place, mine):
    def wide(ref, axis):
        return lax.broadcasted_iota(jnp.int32, ref.shape, axis)

    def put(ref, hit):
        ref[...] = hit.astype(jnp.float32).astype(jnp.bfloat16)

    put(same, lax.bitwise_and(wide(same, 1), LANE - 1) == wide(same, 0))
    put(gather, lax.bitwise_and(wide(gather, 1), GROUP - 1) == wide(gather, 0))
    entry = lax.bitwise_and(wide(place, 1), GROUP - 1) + GROUP * lax.shift_right_logical(
        wide(place, 1), shift_of(LANE)
    )
    put(place, lax.bitwise_and(wide(place, 0), ROWS - 1) == entry)
    put(mine, lax.shift_right_logical(wide(mine, 1), shift_of(SUB)) == wide(mine, 0))


def local_kernel(
    points, normals, poses, directions, pairs_s, pairs_v, maps, dst_s, dst_v,
    staged, remote_b, totals, same, gather, place, mine,
    world, table, sources, targets, sums, side_a, side_b, joined, parts, turned, partial,
):
    per_frag = points.shape[1] // poses.shape[1]
    stride = points.shape[1] + SUB
    constants(same, gather, place, mine)
    table[...] = jnp.zeros_like(table)
    write_directions(directions, table)
    look_up(table, frag_of(dst_v[...], per_frag), remote_b)
    frag_a, frag_b = frag_of(pairs_v[0:1, :], per_frag), frag_of(pairs_v[1:2, :], per_frag)
    look_up(table, frag_a, side_a)
    look_up(table, frag_b, side_b)
    join_directions(side_a, side_b, joined)
    write_world([points, normals], poses, world)

    def stage_remote(g, carry):
        for s in range(SUB):
            block = dst_s[0, g * SUB + s]
            staged[pl.ds(g * TARGET + s, 6, stride=SUB), :] = world[pl.ds(block, 6, stride=stride), :]
        return carry

    lax.fori_loop(0, dst_s.shape[1] // SUB, stage_remote, 0, unroll=4)

    def stage_local(g, carry):
        for s in range(SUB):
            a, b = pairs_s[0, g * SUB + s], pairs_s[1, g * SUB + s]
            targets[pl.ds(g * TARGET + s, 6, stride=SUB), :] = world[pl.ds(b, 6, stride=stride), :]
            sources[pl.ds(g * SOURCE + s, 3, stride=SUB), :] = world[pl.ds(a, 3, stride=stride), :]
        return carry

    lax.fori_loop(0, pairs_s.shape[1] // SUB, stage_local, 0, unroll=4)
    turn_fields(
        lambda u, k: sources[u * SOURCE + k * SUB : u * SOURCE + (k + 1) * SUB, :],
        lambda u, k: targets[u * TARGET + k * SUB : u * TARGET + (k + 1) * SUB, :],
        lambda u: maps[u * SUB : (u + 1) * SUB, :],
        same[...],
        parts,
        turned,
    )
    for t in range(0, sums.shape[1], LANE):
        sums[:, t : t + LANE] = point_sums(turned, joined, partial, slice(t, t + LANE))
    totals[...] = by_frag(sums, frag_a)[0:18, :] + target_side(by_frag(sums, frag_b))


def remote_kernel(
    arrived, staged, remote_b, same, gather, place, mine,
    back, sums, side_a, joined, frags, index, parts, turned, partial,
):
    f32 = jnp.float32
    pairs = parts.shape[0]
    peers = pairs // SUB
    own = lax.shift_right_logical(iota(1), shift_of(GROUP)) == iota(0)

    def block(c, carry):
        first = c * peers
        lanes = pl.ds(pl.multiple_of(c * pairs, LANE), pairs)
        for u in range(peers):
            row = (first + u) * MSG + 3 * SUB
            index[u * SUB : (u + 1) * SUB, :] = arrived[pl.ds(row, SUB), :].astype(jnp.int32)

        def extras(u):
            row = arrived[pl.ds((first + u) * MSG + 4 * SUB, 1), :]
            frags[u * SUB : (u + 1) * SUB, :] = pick(row, iota(0) * GROUP + 13)
            return jnp.where(own, jnp.broadcast_to(row, (SUB, LANE)), 0.0)

        side_a[...] = turn(extras, gather[...], parts, 9)
        join_directions(side_a, remote_b.at[:, lanes], joined)
        turn_fields(
            lambda u, k: arrived[pl.ds((first + u) * MSG + SUB * k, SUB), :],
            lambda u, k: staged[
                pl.ds(pl.multiple_of((first + u) * TARGET, SUB) + SUB * k, SUB), :
            ],
            lambda u: index[u * SUB : (u + 1) * SUB, :],
            same[...],
            parts,
            turned,
        )
        for t in range(0, pairs, LANE):
            total = point_sums(turned, joined, partial, slice(t, t + LANE))
            at = pl.multiple_of(c * pairs, LANE) + t
            sums[:, pl.ds(at, LANE)] = total * side_a[12:13, t : t + LANE]
        rows = lax.dot_general(
            jnp.concatenate(halves_of(sums[:, lanes]), axis=0),
            place[...],
            (((0,), (0,)), ((), ())),
            preferred_element_type=f32,
        )
        slot = lax.shift_right_logical(iota(1), shift_of(GROUP)).astype(f32)[0:1, :]
        hit = frags[...] == jnp.broadcast_to(slot, (pairs, LANE))
        for half in range(2):
            part = jnp.where(hit, rows[:, half * LANE : (half + 1) * LANE], 0.0)
            high, low = halves_of(part)
            back[pl.ds(2 * first + half, peers, stride=2), :] = jnp.dot(
                mine[...], high, preferred_element_type=f32
            ) + jnp.dot(mine[...], low, preferred_element_type=f32)
        return carry

    lax.fori_loop(0, sums.shape[1] // pairs, block, 0)


def total_kernel(sums, dst_v, local_totals, totals, *, per_frag):
    totals[...] = local_totals[...] + target_side(by_frag(sums, frag_of(dst_v[...], per_frag)))


def final_kernel(back, totals, gradient, hess, *, per_frag):
    devices = back.shape[0] // 2
    index = iota(0) * GROUP + lax.bitwise_and(iota(1), GROUP - 1)
    halves = []
    for half in range(2):
        tile = back[pl.ds(half, SUB, stride=2), :]
        for q in range(SUB, devices, SUB):
            tile = tile + back[pl.ds(2 * q + half, SUB, stride=2), :]
        halves.append(pick(jnp.sum(tile, axis=0, keepdims=True), index))
    total = jnp.where(iota(1) < GROUP, halves[0], halves[1]).T[0:18, :] + totals[...]
    gradient[...] = total[0:6, :] * (1.0 / LANE)
    for v in range(2):
        part = total[6 + 6 * v : 12 + 6 * v, :] * (1.0 / (LANE * per_frag))
        for j in range(6):
            hess[j, v : v + 1, :] = part[j : j + 1, :]


def call(kernel, outs, scratch, spaces, limit=VMEM_LIMIT, out_space="v", **more):
    kinds = {"v": pltpu.VMEM, "s": pltpu.SMEM, "h": pltpu.HBM}
    return pl.pallas_call(
        kernel,
        out_shape=outs,
        in_specs=[pl.BlockSpec(memory_space=kinds[s]) for s in spaces],
        out_specs=[pl.BlockSpec(memory_space=kinds[out_space])] * len(outs),
        scratch_shapes=scratch,
        compiler_params=pltpu.CompilerParams(vmem_limit_bytes=limit),
        **more,
    )


def in_hbm(values):
    return pltpu.with_memory_space_constraint(values, pltpu.HBM)


def exchange(rows, devices):
    sent = rows.reshape(devices, 1, -1)
    sent = lax.all_to_all(sent, AXES, split_axis=0, concat_axis=0, tiled=True)
    return sent.reshape(rows.shape)


def local(
    points, normals, poses, directions, local_pairs, local_maps,
    remote_src, remote_maps, remote_dst, counts,
):
    devices = lax.axis_size("tile") * lax.axis_size("band")
    blocks, _, count = points.shape
    frags = poses.shape[1]
    slots = remote_src.shape[1]
    pairs = local_pairs.shape[1]
    assert count == LANE and frags == SUB and slots == devices * SUB and devices % PEERS == 0
    per_frag = blocks // frags
    stride = blocks + SUB
    f32 = jnp.float32
    points = points.transpose(1, 0, 2)
    normals = normals.transpose(1, 0, 2)
    directions = directions.transpose(1, 0, 2)

    def array(*shape, dtype=f32):
        return jax.ShapeDtypeStruct(shape, dtype)

    def vmem(*shape, dtype=f32):
        return pltpu.VMEM(shape, dtype)

    i32, bf16 = jnp.int32, jnp.bfloat16
    part = PEERS * SUB
    (message,) = call(
        pack_kernel,
        [array(devices * MSG, LANE)],
        [
            vmem(3, blocks, LANE),
            pltpu.SMEM((6, frags), f32),
            vmem(6, 2, frags),
            pltpu.SMEM((1, slots), i32),
            vmem(1, slots, dtype=i32),
            vmem(slots, LANE, dtype=i32),
            vmem(1, devices, dtype=i32),
            vmem(3 * stride, LANE),
            vmem(2 * SUB, LANE),
            vmem(devices * MSG, LANE),
            pltpu.SemaphoreType.DMA((7,)),
            pltpu.SemaphoreType.DMA((devices // SUB,)),
        ],
        "hhhhhh",
        limit=PACK_LIMIT,
        out_space="h",
    )(*[in_hbm(x) for x in (points, poses, directions, remote_src, remote_maps[0], counts)])
    arrived = exchange(message, devices)
    staged, remote_b, totals, same, gather, place, mine = call(
        local_kernel,
        [
            array(devices * TARGET, LANE),
            array(2 * SUB, slots),
            array(18, frags),
            array(LANE, 2 * LANE, dtype=bf16),
            array(GROUP, 2 * LANE, dtype=bf16),
            array(2 * ROWS, 2 * LANE, dtype=bf16),
            array(PEERS, part, dtype=bf16),
        ],
        [
            vmem(6 * stride, LANE),
            vmem(2 * SUB, LANE),
            vmem(pairs // SUB * SOURCE, LANE),
            vmem(pairs // SUB * TARGET, LANE),
            vmem(ROWS, pairs),
            vmem(2 * SUB, pairs),
            vmem(2 * SUB, pairs),
            vmem(3 * SUB, pairs),
            vmem(pairs, 9 * 2 * LANE, dtype=bf16),
            vmem(9 * LANE, pairs),
            vmem(ROWS * SUB, LANE),
        ],
        "vvsvsvvsv",
        cost_estimate=pl.CostEstimate(
            flops=200 * pairs * LANE, bytes_accessed=4_000_000, transcendentals=0
        ),
    )(
        points, normals, poses, directions, local_pairs, local_pairs, local_maps,
        remote_dst, remote_dst,
    )
    back, sums = call(
        remote_kernel,
        [array(devices * 2, LANE), array(ROWS, slots)],
        [
            vmem(2 * SUB, part),
            vmem(3 * SUB, part),
            vmem(part, LANE),
            vmem(part, LANE, dtype=i32),
            vmem(part, 10 * 2 * LANE, dtype=bf16),
            vmem(9 * LANE, part),
            vmem(ROWS * SUB, LANE),
        ],
        "vvvvvvv",
    )(arrived, staged, remote_b, same, gather, place, mine)
    back = exchange(back, devices)
    (totals,) = call(
        functools.partial(total_kernel, per_frag=per_frag),
        [array(18, frags)],
        [],
        "vvv",
        cost_estimate=pl.CostEstimate(
            flops=2 * SUB * slots * 2 * LANE, bytes_accessed=1_000_000, transcendentals=0
        ),
    )(sums, remote_dst, totals)
    gradient, hess = call(
        functools.partial(final_kernel, per_frag=per_frag),
        [array(6, frags), array(6, 2, frags)],
        [],
        "vv",
    )(back, totals)
    return (gradient, hess.transpose(1, 0, 2))


def solution(mesh):
    placed = (
        P(AXES, None, None),
        P(AXES, None, None),
        P(None, AXES),
        P(None, None, AXES),
        P(None, AXES),
        P(AXES, None),
        P(AXES, None),
        P(AXES, None, None),
        P(AXES, None),
        P(AXES, None),
    )
    return jax.shard_map(
        local,
        mesh=mesh,
        in_specs=placed,
        out_specs=(P(None, AXES), P(None, None, AXES)),
        check_vma=False,
    )
```

```python
import functools

import jax
import jax.numpy as jnp
from jax import lax
from jax.experimental import pallas as pl
from jax.experimental.pallas import tpu as pltpu
from jax.sharding import PartitionSpec as P

AXES = ("tile", "band")
SUB = 8
LANE = 128
MSG = 4 * SUB + 1
TARGET = 6 * SUB
SOURCE = 3 * SUB
ROWS = 32
GROUP = 16
VMEM_LIMIT = 16 * 1024 * 1024
PACK_LIMIT = 56 * 1024 * 1024
PEERS = 32


def iota(axis):
    return lax.broadcasted_iota(jnp.int32, (SUB, LANE), axis)


def pick(values, index):
    values = jnp.broadcast_to(values, (SUB, LANE))
    return jnp.take_along_axis(values, index, axis=1, mode="promise_in_bounds")


def shift_of(size):
    shift = size.bit_length() - 1
    assert 1 << shift == size
    return shift


def cross(left, right):
    return [
        left[1] * right[2] - left[2] * right[1],
        left[2] * right[0] - left[0] * right[2],
        left[0] * right[1] - left[1] * right[0],
    ]


def dot3(left, right):
    return left[0] * right[0] + left[1] * right[1] + left[2] * right[2]


def splat_rotation(poses, f):
    half = [jnp.full((SUB, LANE), poses[i, f] * 0.5, jnp.float32) for i in range(3)]
    w = 1.0 / jnp.sqrt(1.0 + half[0] * half[0] + half[1] * half[1] + half[2] * half[2])
    x, y, z = half[0] * w, half[1] * w, half[2] * w
    rotation = [
        [1.0 - 2.0 * (y * y + z * z), 2.0 * (x * y - w * z), 2.0 * (x * z + w * y)],
        [2.0 * (x * y + w * z), 1.0 - 2.0 * (x * x + z * z), 2.0 * (y * z - w * x)],
        [2.0 * (x * z - w * y), 2.0 * (y * z + w * x), 1.0 - 2.0 * (x * x + y * y)],
    ]
    return rotation, [jnp.full((SUB, LANE), poses[i, f], jnp.float32) for i in range(3, 6)]


def write_world(fields, poses, world):
    blocks, frags = fields[0].shape[1], poses.shape[1]
    per_frag, stride = blocks // frags, blocks + SUB
    for f in range(frags):
        turn, move = splat_rotation(poses, f)
        for b in range(f * per_frag, (f + 1) * per_frag, SUB):
            for at, field in enumerate(fields):
                x = [field[j, b : b + SUB, :] for j in range(3)]
                for i in range(3):
                    row = dot3(turn[i], x)
                    world[pl.ds((3 * at + i) * stride + b, SUB), :] = row + move[i] if at == 0 else row


def write_directions(directions, table):
    frags = directions.shape[2]
    for v in range(2):
        for j in range(6):
            table[6 * v + j : 6 * v + j + 1, 0:frags] = directions[j, v : v + 1, :]


def index_tile(row_ref, first, offset):
    tile = first // LANE * LANE
    return pick(row_ref[0:1, pl.ds(tile, LANE)], offset + first % LANE)


def pack_kernel(
    points_h, poses_h, directions_h, src_h, maps_h, counts_h, out_h,
    points, poses, directions, src_s, src_v, maps, used, world, table, out, sems, out_sems,
):
    devices = counts_h.shape[1]
    per_frag = points.shape[1] // poses.shape[1]
    stride = points.shape[1] + SUB
    pairs = [
        (directions_h, directions), (src_h, src_v), (counts_h, used), (poses_h, poses),
        (points_h, points), (src_h, src_s), (maps_h, maps),
    ]
    copies = [pltpu.make_async_copy(a, b, sems.at[i]) for i, (a, b) in enumerate(pairs)]
    for copy in copies:
        copy.start()
    for copy in copies[0:3]:
        copy.wait()
    write_directions(directions, table)
    limits = jnp.broadcast_to(used[0:1, :], (SUB, devices)).astype(jnp.float32)
    peers = lax.broadcasted_iota(jnp.int32, (SUB, devices), 1)
    row = lax.broadcasted_iota(jnp.int32, (SUB, devices), 0)
    slot = lax.shift_right_logical(iota(1), shift_of(GROUP))
    field = lax.bitwise_and(iota(1), GROUP - 1)
    for q in range(0, devices, SUB):
        block = index_tile(src_v, q * SUB, iota(0) * SUB + slot)
        frag = lax.shift_right_logical(block, shift_of(per_frag))
        limit = jnp.sum(jnp.where(peers == row + q, limits, 0.0), axis=1, keepdims=True)
        extras = jnp.where(slot.astype(jnp.float32) < limit, 1.0, 0.0)
        for j in range(12):
            extras = jnp.where(field == j, pick(table[j : j + 1, :], frag), extras)
        extras = jnp.where(field == 13, frag.astype(jnp.float32), extras)
        out[pl.ds(q * MSG + MSG - 1, SUB, stride=MSG), :] = extras
    for copy in copies[3:]:
        copy.wait()
    write_world([points], poses, world)

    def peer(p):
        for s in range(SUB):
            block = src_s[0, p * SUB + s]
            out[pl.ds(p * MSG + s, 3, stride=SUB), :] = world[pl.ds(block, 3, stride=stride), :]
        rows = maps[pl.ds(pl.multiple_of(p * SUB, SUB), SUB), :]
        out[pl.ds(p * MSG + 3 * SUB, SUB), :] = rows.astype(jnp.float32)

    def piece(i):
        rows = pl.ds(pl.multiple_of(i * SUB * MSG, SUB), SUB * MSG)
        return pltpu.make_async_copy(out.at[rows], out_h.at[rows], out_sems.at[i])

    def pack(i, carry):
        for u in range(SUB):
            peer(i * SUB + u)
        piece(i).start()
        return carry

    lax.fori_loop(0, devices // SUB, pack, 0)
    for i in range(devices // SUB):
        piece(i).wait()


def halves_of(values):
    high = values.astype(jnp.bfloat16)
    return high, (values - high.astype(jnp.float32)).astype(jnp.bfloat16)


def turn(at, left, parts, i):
    columns = i * 2 * LANE
    for u in range(0, parts.shape[0] // SUB, 2):
        high, low = halves_of(jnp.concatenate([at(u), at(u + 1)], axis=0))
        parts[u * SUB : (u + 2) * SUB, columns : columns + LANE] = high
        parts[u * SUB : (u + 2) * SUB, columns + LANE : columns + 2 * LANE] = low
    return lax.dot_general(
        left,
        parts[:, columns : columns + 2 * LANE],
        (((1,), (1,)), ((), ())),
        preferred_element_type=jnp.float32,
    )


def turn_fields(source, target, index, same, parts, turned):
    for k in range(6):

        def at(u, k=k):
            return pick(target(u, k), index(u))

        turned[k * LANE : (k + 1) * LANE, :] = turn(at, same, parts, k)
    for k in range(3):
        turned[(6 + k) * LANE : (7 + k) * LANE, :] = turn(
            lambda u, k=k: source(u, k), same, parts, 6 + k
        )


def join_directions(side_a, side_b, joined):
    joined[0:12, :] = side_a[0:12, :]
    for v in range(2):
        joined[6 * v + 3 : 6 * v + 6, :] = side_a[6 * v + 3 : 6 * v + 6, :] - side_b[6 * v + 3 : 6 * v + 6, :]
        joined[12 + 3 * v : 15 + 3 * v, :] = side_b[6 * v : 6 * v + 3, :]


def point_sums(turned, joined, partial, lanes):
    def add(i, totals):
        start = pl.multiple_of(i * SUB, SUB)
        field = [turned[pl.ds(start + k * LANE, SUB), lanes] for k in range(9)]
        way = [joined[j : j + 1, lanes] for j in range(18)]
        y, n, x = field[0:3], field[3:6], field[6:9]
        p, q = cross(x, n), cross(y, n)
        scalars = [dot3(n, [x[k] - y[k] for k in range(3)])]
        for v in range(2):
            a, b = way[6 * v : 6 * v + 6], way[12 + 3 * v : 15 + 3 * v]
            scalars.append(dot3(p, a[0:3]) + dot3(n, a[3:6]) - dot3(q, b))
        terms = []
        for s in scalars:
            terms += [s * value for value in p + n]
        for s in scalars:
            terms += [s * value for value in q]
        return tuple(total + term for total, term in zip(totals, terms))

    zero = jnp.zeros((SUB, LANE), jnp.float32)
    totals = lax.fori_loop(0, LANE // SUB, add, (zero,) * 27, unroll=4)
    for j in range(27):
        partial[j * SUB : (j + 1) * SUB, :] = totals[j]
    for j in range(27, ROWS):
        partial[j * SUB : (j + 1) * SUB, :] = zero
    total = partial[pl.ds(0, ROWS, stride=SUB), :]
    for s in range(1, SUB):
        total = total + partial[pl.ds(s, ROWS, stride=SUB), :]
    return total


def frag_of(row, per_frag):
    return lax.shift_right_logical(row, shift_of(per_frag))


def look_up(table, frag, out):
    for at in range(0, frag.shape[1], LANE):
        index = jnp.broadcast_to(frag[:, at : at + LANE], (SUB, LANE))
        for j in range(0, 2 * SUB, SUB):
            out[j : j + SUB, at : at + LANE] = pick(table[j : j + SUB, :], index)


def by_frag(sums, frag):
    pairs = sums.shape[1]
    hot = jnp.broadcast_to(frag, (SUB, pairs)) == lax.broadcasted_iota(jnp.int32, (SUB, pairs), 0)
    return lax.dot_general(
        sums[...],
        hot.astype(jnp.float32),
        (((1,), (1,)), ((), ())),
        precision=lax.Precision.HIGHEST,
        preferred_element_type=jnp.float32,
    )


def target_side(total):
    rows = []
    for k in range(3):
        rows += [total[18 + 3 * k : 21 + 3 * k, :], total[6 * k + 3 : 6 * k + 6, :]]
    return -jnp.concatenate(rows, axis=0)


def constants(same, gather, place, mine):
    def wide(ref, axis):
        return lax.broadcasted_iota(jnp.int32, ref.shape, axis)

    def put(ref, hit):
        ref[...] = hit.astype(jnp.float32).astype(jnp.bfloat16)

    put(same, lax.bitwise_and(wide(same, 1), LANE - 1) == wide(same, 0))
    put(gather, lax.bitwise_and(wide(gather, 1), GROUP - 1) == wide(gather, 0))
    entry = lax.bitwise_and(wide(place, 1), GROUP - 1) + GROUP * lax.shift_right_logical(
        wide(place, 1), shift_of(LANE)
    )
    put(place, lax.bitwise_and(wide(place, 0), ROWS - 1) == entry)
    put(mine, lax.shift_right_logical(wide(mine, 1), shift_of(SUB)) == wide(mine, 0))


def local_kernel(
    points, normals, poses, directions, pairs_s, pairs_v, maps, dst_s, dst_v,
    staged, remote_b, totals, same, gather, place, mine,
    world, table, sources, targets, sums, side_a, side_b, joined, parts, turned, partial,
):
    per_frag = points.shape[1] // poses.shape[1]
    stride = points.shape[1] + SUB
    constants(same, gather, place, mine)
    table[...] = jnp.zeros_like(table)
    write_directions(directions, table)
    look_up(table, frag_of(dst_v[...], per_frag), remote_b)
    frag_a, frag_b = frag_of(pairs_v[0:1, :], per_frag), frag_of(pairs_v[1:2, :], per_frag)
    look_up(table, frag_a, side_a)
    look_up(table, frag_b, side_b)
    join_directions(side_a, side_b, joined)
    write_world([points, normals], poses, world)

    def stage_remote(g, carry):
        for s in range(SUB):
            block = dst_s[0, g * SUB + s]
            staged[pl.ds(g * TARGET + s, 6, stride=SUB), :] = world[pl.ds(block, 6, stride=stride), :]
        return carry

    lax.fori_loop(0, dst_s.shape[1] // SUB, stage_remote, 0, unroll=4)

    def stage_local(g, carry):
        for s in range(SUB):
            a, b = pairs_s[0, g * SUB + s], pairs_s[1, g * SUB + s]
            targets[pl.ds(g * TARGET + s, 6, stride=SUB), :] = world[pl.ds(b, 6, stride=stride), :]
            sources[pl.ds(g * SOURCE + s, 3, stride=SUB), :] = world[pl.ds(a, 3, stride=stride), :]
        return carry

    lax.fori_loop(0, pairs_s.shape[1] // SUB, stage_local, 0, unroll=4)
    turn_fields(
        lambda u, k: sources[u * SOURCE + k * SUB : u * SOURCE + (k + 1) * SUB, :],
        lambda u, k: targets[u * TARGET + k * SUB : u * TARGET + (k + 1) * SUB, :],
        lambda u: maps[u * SUB : (u + 1) * SUB, :],
        same[...],
        parts,
        turned,
    )
    for t in range(0, sums.shape[1], LANE):
        sums[:, t : t + LANE] = point_sums(turned, joined, partial, slice(t, t + LANE))
    totals[...] = by_frag(sums, frag_a)[0:18, :] + target_side(by_frag(sums, frag_b))


def remote_kernel(
    arrived, staged, remote_b, local_totals, dst_v, same, gather, place, mine,
    back, totals, sums, side_a, joined, frags, index, parts, turned, partial, *, per_frag,
):
    f32 = jnp.float32
    pairs = parts.shape[0]
    peers = pairs // SUB
    own = lax.shift_right_logical(iota(1), shift_of(GROUP)) == iota(0)

    def block(c, carry):
        first = c * peers
        lanes = pl.ds(pl.multiple_of(c * pairs, LANE), pairs)
        for u in range(peers):
            row = (first + u) * MSG + 3 * SUB
            index[u * SUB : (u + 1) * SUB, :] = arrived[pl.ds(row, SUB), :].astype(jnp.int32)

        def extras(u):
            row = arrived[pl.ds((first + u) * MSG + 4 * SUB, 1), :]
            frags[u * SUB : (u + 1) * SUB, :] = pick(row, iota(0) * GROUP + 13)
            return jnp.where(own, jnp.broadcast_to(row, (SUB, LANE)), 0.0)

        side_a[...] = turn(extras, gather[...], parts, 9)
        join_directions(side_a, remote_b.at[:, lanes], joined)
        turn_fields(
            lambda u, k: arrived[pl.ds((first + u) * MSG + SUB * k, SUB), :],
            lambda u, k: staged[
                pl.ds(pl.multiple_of((first + u) * TARGET, SUB) + SUB * k, SUB), :
            ],
            lambda u: index[u * SUB : (u + 1) * SUB, :],
            same[...],
            parts,
            turned,
        )
        for t in range(0, pairs, LANE):
            total = point_sums(turned, joined, partial, slice(t, t + LANE))
            at = pl.multiple_of(c * pairs, LANE) + t
            sums[:, pl.ds(at, LANE)] = total * side_a[12:13, t : t + LANE]
        rows = lax.dot_general(
            jnp.concatenate(halves_of(sums[:, lanes]), axis=0),
            place[...],
            (((0,), (0,)), ((), ())),
            preferred_element_type=f32,
        )
        slot = lax.shift_right_logical(iota(1), shift_of(GROUP)).astype(f32)[0:1, :]
        hit = frags[...] == jnp.broadcast_to(slot, (pairs, LANE))
        for half in range(2):
            part = jnp.where(hit, rows[:, half * LANE : (half + 1) * LANE], 0.0)
            high, low = halves_of(part)
            back[pl.ds(2 * first + half, peers, stride=2), :] = jnp.dot(
                mine[...], high, preferred_element_type=f32
            ) + jnp.dot(mine[...], low, preferred_element_type=f32)
        return carry

    lax.fori_loop(0, sums.shape[1] // pairs, block, 0)
    totals[...] = local_totals[...] + target_side(by_frag(sums, frag_of(dst_v[...], per_frag)))


def final_kernel(back, totals, gradient, hess, *, per_frag):
    devices = back.shape[0] // 2
    index = iota(0) * GROUP + lax.bitwise_and(iota(1), GROUP - 1)
    halves = []
    for half in range(2):
        tile = back[pl.ds(half, SUB, stride=2), :]
        for q in range(SUB, devices, SUB):
            tile = tile + back[pl.ds(2 * q + half, SUB, stride=2), :]
        halves.append(pick(jnp.sum(tile, axis=0, keepdims=True), index))
    total = jnp.where(iota(1) < GROUP, halves[0], halves[1]).T[0:18, :] + totals[...]
    gradient[...] = total[0:6, :] * (1.0 / LANE)
    for v in range(2):
        part = total[6 + 6 * v : 12 + 6 * v, :] * (1.0 / (LANE * per_frag))
        for j in range(6):
            hess[j, v : v + 1, :] = part[j : j + 1, :]


def call(kernel, outs, scratch, spaces, limit=VMEM_LIMIT, out_space="v", **more):
    kinds = {"v": pltpu.VMEM, "s": pltpu.SMEM, "h": pltpu.HBM}
    return pl.pallas_call(
        kernel,
        out_shape=outs,
        in_specs=[pl.BlockSpec(memory_space=kinds[s]) for s in spaces],
        out_specs=[pl.BlockSpec(memory_space=kinds[out_space])] * len(outs),
        scratch_shapes=scratch,
        compiler_params=pltpu.CompilerParams(vmem_limit_bytes=limit),
        **more,
    )


def in_hbm(values):
    return pltpu.with_memory_space_constraint(values, pltpu.HBM)


def exchange(rows, devices):
    sent = rows.reshape(devices, 1, -1)
    sent = lax.all_to_all(sent, AXES, split_axis=0, concat_axis=0, tiled=True)
    return sent.reshape(rows.shape)


def local(
    points, normals, poses, directions, local_pairs, local_maps,
    remote_src, remote_maps, remote_dst, counts,
):
    devices = lax.axis_size("tile") * lax.axis_size("band")
    blocks, _, count = points.shape
    frags = poses.shape[1]
    slots = remote_src.shape[1]
    pairs = local_pairs.shape[1]
    assert count == LANE and frags == SUB and slots == devices * SUB and devices % PEERS == 0
    per_frag = blocks // frags
    stride = blocks + SUB
    f32 = jnp.float32
    points = points.transpose(1, 0, 2)
    normals = normals.transpose(1, 0, 2)
    directions = directions.transpose(1, 0, 2)

    def array(*shape, dtype=f32):
        return jax.ShapeDtypeStruct(shape, dtype)

    def vmem(*shape, dtype=f32):
        return pltpu.VMEM(shape, dtype)

    i32, bf16 = jnp.int32, jnp.bfloat16
    part = PEERS * SUB
    (message,) = call(
        pack_kernel,
        [array(devices * MSG, LANE)],
        [
            vmem(3, blocks, LANE),
            pltpu.SMEM((6, frags), f32),
            vmem(6, 2, frags),
            pltpu.SMEM((1, slots), i32),
            vmem(1, slots, dtype=i32),
            vmem(slots, LANE, dtype=i32),
            vmem(1, devices, dtype=i32),
            vmem(3 * stride, LANE),
            vmem(2 * SUB, LANE),
            vmem(devices * MSG, LANE),
            pltpu.SemaphoreType.DMA((7,)),
            pltpu.SemaphoreType.DMA((devices // SUB,)),
        ],
        "hhhhhh",
        limit=PACK_LIMIT,
        out_space="h",
    )(*[in_hbm(x) for x in (points, poses, directions, remote_src, remote_maps[0], counts)])
    arrived = exchange(message, devices)
    staged, remote_b, totals, same, gather, place, mine = call(
        local_kernel,
        [
            array(devices * TARGET, LANE),
            array(2 * SUB, slots),
            array(18, frags),
            array(LANE, 2 * LANE, dtype=bf16),
            array(GROUP, 2 * LANE, dtype=bf16),
            array(2 * ROWS, 2 * LANE, dtype=bf16),
            array(PEERS, part, dtype=bf16),
        ],
        [
            vmem(6 * stride, LANE),
            vmem(2 * SUB, LANE),
            vmem(pairs // SUB * SOURCE, LANE),
            vmem(pairs // SUB * TARGET, LANE),
            vmem(ROWS, pairs),
            vmem(2 * SUB, pairs),
            vmem(2 * SUB, pairs),
            vmem(3 * SUB, pairs),
            vmem(pairs, 9 * 2 * LANE, dtype=bf16),
            vmem(9 * LANE, pairs),
            vmem(ROWS * SUB, LANE),
        ],
        "vvsvsvvsv",
        cost_estimate=pl.CostEstimate(
            flops=200 * pairs * LANE, bytes_accessed=4_000_000, transcendentals=0
        ),
    )(
        points, normals, poses, directions, local_pairs, local_pairs, local_maps,
        remote_dst, remote_dst,
    )
    back, totals = call(
        functools.partial(remote_kernel, per_frag=per_frag),
        [array(devices * 2, LANE), array(18, frags)],
        [
            vmem(ROWS, slots),
            vmem(2 * SUB, part),
            vmem(3 * SUB, part),
            vmem(part, LANE),
            vmem(part, LANE, dtype=i32),
            vmem(part, 10 * 2 * LANE, dtype=bf16),
            vmem(9 * LANE, part),
            vmem(ROWS * SUB, LANE),
        ],
        "vvvvvvvvv",
    )(arrived, staged, remote_b, totals, remote_dst, same, gather, place, mine)
    back = exchange(back, devices)
    gradient, hess = call(
        functools.partial(final_kernel, per_frag=per_frag),
        [array(6, frags), array(6, 2, frags)],
        [],
        "vv",
    )(back, totals)
    return (gradient, hess.transpose(1, 0, 2))


def solution(mesh):
    placed = (
        P(AXES, None, None),
        P(AXES, None, None),
        P(None, AXES),
        P(None, None, AXES),
        P(None, AXES),
        P(AXES, None),
        P(AXES, None),
        P(AXES, None, None),
        P(AXES, None),
        P(AXES, None),
    )
    return jax.shard_map(
        local,
        mesh=mesh,
        in_specs=placed,
        out_specs=(P(None, AXES), P(None, None, AXES)),
        check_vma=False,
    )
```

```python
import functools

import jax
import jax.numpy as jnp
from jax import lax
from jax.experimental import pallas as pl
from jax.experimental.pallas import tpu as pltpu
from jax.sharding import PartitionSpec as P

AXES = ("tile", "band")
SUB = 8
LANE = 128
MSG = 4 * SUB + 1
TARGET = 6 * SUB
SOURCE = 3 * SUB
ROWS = 32
GROUP = 16
VMEM_LIMIT = 16 * 1024 * 1024
PACK_LIMIT = 56 * 1024 * 1024
PEERS = 32


def iota(axis):
    return lax.broadcasted_iota(jnp.int32, (SUB, LANE), axis)


def pick(values, index):
    values = jnp.broadcast_to(values, (SUB, LANE))
    return jnp.take_along_axis(values, index, axis=1, mode="promise_in_bounds")


def shift_of(size):
    shift = size.bit_length() - 1
    assert 1 << shift == size
    return shift


def cross(left, right):
    return [
        left[1] * right[2] - left[2] * right[1],
        left[2] * right[0] - left[0] * right[2],
        left[0] * right[1] - left[1] * right[0],
    ]


def dot3(left, right):
    return left[0] * right[0] + left[1] * right[1] + left[2] * right[2]


def splat_rotation(poses, f):
    half = [jnp.full((SUB, LANE), poses[i, f] * 0.5, jnp.float32) for i in range(3)]
    w = 1.0 / jnp.sqrt(1.0 + half[0] * half[0] + half[1] * half[1] + half[2] * half[2])
    x, y, z = half[0] * w, half[1] * w, half[2] * w
    rotation = [
        [1.0 - 2.0 * (y * y + z * z), 2.0 * (x * y - w * z), 2.0 * (x * z + w * y)],
        [2.0 * (x * y + w * z), 1.0 - 2.0 * (x * x + z * z), 2.0 * (y * z - w * x)],
        [2.0 * (x * z - w * y), 2.0 * (y * z + w * x), 1.0 - 2.0 * (x * x + y * y)],
    ]
    return rotation, [jnp.full((SUB, LANE), poses[i, f], jnp.float32) for i in range(3, 6)]


def write_rotations(poses, turns):
    for f in range(poses.shape[1]):
        rotation, move = splat_rotation(poses, f)
        for i, tile in enumerate(rotation[0] + rotation[1] + rotation[2] + move):
            at = (12 * f + i) * SUB
            turns[at : at + SUB, :] = tile


def write_world(fields, turns, world, frags):
    blocks = fields[0].shape[1]
    total = turns.shape[0] // (12 * SUB)
    per_frag, stride = blocks // total, blocks + SUB
    for f in frags:
        tile = [turns[(12 * f + i) * SUB : (12 * f + i + 1) * SUB, :] for i in range(12)]
        for b in range(f * per_frag, (f + 1) * per_frag, SUB):
            for at, field in enumerate(fields):
                x = [field[j, b : b + SUB, :] for j in range(3)]
                for i in range(3):
                    row = dot3(tile[3 * i : 3 * i + 3], x)
                    if at == 0:
                        row = row + tile[9 + i]
                    world[pl.ds((3 * at + i) * stride + b, SUB), :] = row


def write_directions(directions, table):
    frags = directions.shape[2]
    for v in range(2):
        for j in range(6):
            table[6 * v + j : 6 * v + j + 1, 0:frags] = directions[j, v : v + 1, :]


def index_tile(row_ref, first, offset):
    tile = first // LANE * LANE
    return pick(row_ref[0:1, pl.ds(tile, LANE)], offset + first % LANE)


def pack_kernel(
    points_h, poses_h, directions_h, src_h, maps_h, counts_h, out_h,
    points, poses, directions, src_s, src_v, maps, used, world, turns, table, out, sems, out_sems,
):
    devices = counts_h.shape[1]
    per_frag = points.shape[1] // poses.shape[1]
    stride = points.shape[1] + SUB
    frags = poses.shape[1]
    half = points.shape[1] // 2
    pieces = [slice(i * half, (i + 1) * half) for i in range(2)]
    pairs = [(poses_h, poses), (directions_h, directions), (src_h, src_v), (counts_h, used)]
    pairs += [(points_h.at[j, rows], points.at[j, rows]) for rows in pieces for j in range(3)]
    rows = maps.shape[0] // 2
    pairs += [(src_h, src_s)]
    pairs += [(maps_h.at[pl.ds(i, rows)], maps.at[pl.ds(i, rows)]) for i in (0, rows)]
    copies = [pltpu.make_async_copy(a, b, sems.at[i]) for i, (a, b) in enumerate(pairs)]
    for i in (0, 4, 5, 6, 7, 8, 9, 10, 11, 12, 1, 2, 3):
        copies[i].start()
    copies[0].wait()
    write_rotations(poses, turns)
    for copy in copies[1:4]:
        copy.wait()
    write_directions(directions, table)
    limits = jnp.broadcast_to(used[0:1, :], (SUB, devices)).astype(jnp.float32)
    peers = lax.broadcasted_iota(jnp.int32, (SUB, devices), 1)
    row = lax.broadcasted_iota(jnp.int32, (SUB, devices), 0)
    slot = lax.shift_right_logical(iota(1), shift_of(GROUP))
    field = lax.bitwise_and(iota(1), GROUP - 1)
    for q in range(0, devices, SUB):
        block = index_tile(src_v, q * SUB, iota(0) * SUB + slot)
        frag = lax.shift_right_logical(block, shift_of(per_frag))
        limit = jnp.sum(jnp.where(peers == row + q, limits, 0.0), axis=1, keepdims=True)
        extras = jnp.where(slot.astype(jnp.float32) < limit, 1.0, 0.0)
        for j in range(12):
            extras = jnp.where(field == j, pick(table[j : j + 1, :], frag), extras)
        extras = jnp.where(field == 13, frag.astype(jnp.float32), extras)
        out[pl.ds(q * MSG + MSG - 1, SUB, stride=MSG), :] = extras
    for i in range(2):
        for copy in copies[4 + 3 * i : 7 + 3 * i]:
            copy.wait()
        write_world([points], turns, world, range(i * frags // 2, (i + 1) * frags // 2))
    for copy in copies[10:]:
        copy.wait()

    def peer(p):
        for s in range(SUB):
            block = src_s[0, p * SUB + s]
            out[pl.ds(p * MSG + s, 3, stride=SUB), :] = world[pl.ds(block, 3, stride=stride), :]
        rows = maps[pl.ds(pl.multiple_of(p * SUB, SUB), SUB), :]
        out[pl.ds(p * MSG + 3 * SUB, SUB), :] = rows.astype(jnp.float32)

    def piece(i):
        rows = pl.ds(pl.multiple_of(i * SUB * MSG, SUB), SUB * MSG)
        return pltpu.make_async_copy(out.at[rows], out_h.at[rows], out_sems.at[i])

    def pack(i, carry):
        for u in range(SUB):
            peer(i * SUB + u)
        piece(i).start()
        return carry

    lax.fori_loop(0, devices // SUB, pack, 0)
    for i in range(devices // SUB):
        piece(i).wait()


def halves_of(values):
    high = values.astype(jnp.bfloat16)
    return high, (values - high.astype(jnp.float32)).astype(jnp.bfloat16)


def turn(at, left, parts, i, t):
    columns = slice(i * 2 * LANE, i * 2 * LANE + LANE), slice(i * 2 * LANE + LANE, (i + 1) * 2 * LANE)
    for u in range(t // SUB, (t + LANE) // SUB, 2):
        high, low = halves_of(jnp.concatenate([at(u), at(u + 1)], axis=0))
        parts[u * SUB : (u + 2) * SUB, columns[0]] = high
        parts[u * SUB : (u + 2) * SUB, columns[1]] = low
    return lax.dot_general(
        left,
        parts[t : t + LANE, i * 2 * LANE : (i + 1) * 2 * LANE],
        (((1,), (1,)), ((), ())),
        preferred_element_type=jnp.float32,
    )


def turn_fields(source, target, index, same, parts, turned, t):
    lanes = slice(t, t + LANE)
    for k in range(6):

        def at(u, k=k):
            return pick(target(u, k), index(u))

        turned[k * LANE : (k + 1) * LANE, lanes] = turn(at, same, parts, k, t)
    for k in range(3):
        turned[(6 + k) * LANE : (7 + k) * LANE, lanes] = turn(
            lambda u, k=k: source(u, k), same, parts, 6 + k, t
        )


def join_directions(side_a, side_b, joined, lanes, lanes_b):
    joined[0:12, lanes] = side_a[0:12, lanes]
    for v in range(2):
        turn_rows, move_rows = slice(6 * v, 6 * v + 3), slice(6 * v + 3, 6 * v + 6)
        joined[move_rows, lanes] = side_a[move_rows, lanes] - side_b[move_rows, lanes_b]
        joined[12 + 3 * v : 15 + 3 * v, lanes] = side_b[turn_rows, lanes_b]


def point_sums(turned, joined, partial, t):
    lanes = slice(t, t + LANE)
    first = t // LANE * ROWS * SUB

    def add(i, totals):
        start = pl.multiple_of(i * SUB, SUB)
        field = [turned[pl.ds(start + k * LANE, SUB), lanes] for k in range(9)]
        way = [joined[j : j + 1, lanes] for j in range(18)]
        y, n, x = field[0:3], field[3:6], field[6:9]
        p, q = cross(x, n), cross(y, n)
        scalars = [dot3(n, [x[k] - y[k] for k in range(3)])]
        for v in range(2):
            a, b = way[6 * v : 6 * v + 6], way[12 + 3 * v : 15 + 3 * v]
            scalars.append(dot3(p, a[0:3]) + dot3(n, a[3:6]) - dot3(q, b))
        terms = []
        for s in scalars:
            terms += [s * value for value in p + n]
        for s in scalars:
            terms += [s * value for value in q]
        return tuple(total + term for total, term in zip(totals, terms))

    zero = jnp.zeros((SUB, LANE), jnp.float32)
    totals = lax.fori_loop(0, LANE // SUB, add, (zero,) * 27, unroll=LANE // SUB)
    for j in range(ROWS):
        partial[first + j * SUB : first + (j + 1) * SUB, :] = totals[j] if j < 27 else zero
    total = partial[pl.ds(first, ROWS, stride=SUB), :]
    for s in range(1, SUB):
        total = total + partial[pl.ds(first + s, ROWS, stride=SUB), :]
    return total


def frag_of(row, per_frag):
    return lax.shift_right_logical(row, shift_of(per_frag))


def look_up(table, frag, out):
    for at in range(0, frag.shape[1], LANE):
        index = jnp.broadcast_to(frag[:, at : at + LANE], (SUB, LANE))
        for j in range(0, 2 * SUB, SUB):
            out[j : j + SUB, at : at + LANE] = pick(table[j : j + SUB, :], index)


def by_frag(sums, frag):
    pairs = sums.shape[1]
    hot = jnp.broadcast_to(frag, (SUB, pairs)) == lax.broadcasted_iota(jnp.int32, (SUB, pairs), 0)
    return lax.dot_general(
        sums,
        hot.astype(jnp.float32),
        (((1,), (1,)), ((), ())),
        precision=lax.Precision.HIGHEST,
        preferred_element_type=jnp.float32,
    )


def target_side(total):
    rows = []
    for k in range(3):
        rows += [total[18 + 3 * k : 21 + 3 * k, :], total[6 * k + 3 : 6 * k + 6, :]]
    return -jnp.concatenate(rows, axis=0)


def constants(same, gather, place, mine):
    def wide(ref, axis):
        return lax.broadcasted_iota(jnp.int32, ref.shape, axis)

    def put(ref, hit):
        ref[...] = hit.astype(jnp.float32).astype(jnp.bfloat16)

    put(same, lax.bitwise_and(wide(same, 1), LANE - 1) == wide(same, 0))
    put(gather, lax.bitwise_and(wide(gather, 1), GROUP - 1) == wide(gather, 0))
    entry = lax.bitwise_and(wide(place, 1), GROUP - 1) + GROUP * lax.shift_right_logical(
        wide(place, 1), shift_of(LANE)
    )
    put(place, lax.bitwise_and(wide(place, 0), ROWS - 1) == entry)
    put(mine, lax.shift_right_logical(wide(mine, 1), shift_of(SUB)) == wide(mine, 0))


def local_kernel(
    points, normals, poses, directions, pairs_s, pairs_v, maps, dst_s, dst_v,
    staged, remote_b, totals, same, gather, place, mine,
    world, turns, table, sources, targets, side_a, side_b, joined, parts, turned, partial,
):
    per_frag = points.shape[1] // poses.shape[1]
    stride = points.shape[1] + SUB
    constants(same, gather, place, mine)
    table[...] = jnp.zeros_like(table)
    write_directions(directions, table)
    look_up(table, frag_of(dst_v[...], per_frag), remote_b)
    frag_a, frag_b = frag_of(pairs_v[0:1, :], per_frag), frag_of(pairs_v[1:2, :], per_frag)
    look_up(table, frag_a, side_a)
    look_up(table, frag_b, side_b)
    every = slice(0, pairs_s.shape[1])
    join_directions(side_a, side_b, joined, every, every)
    write_rotations(poses, turns)
    write_world([points, normals], turns, world, range(poses.shape[1]))

    def stage_remote(g, carry):
        for s in range(SUB):
            block = dst_s[0, g * SUB + s]
            staged[pl.ds(g * TARGET + s, 6, stride=SUB), :] = world[pl.ds(block, 6, stride=stride), :]
        return carry

    lax.fori_loop(0, dst_s.shape[1] // SUB, stage_remote, 0, unroll=4)

    def stage_local(g, carry):
        for s in range(SUB):
            a, b = pairs_s[0, g * SUB + s], pairs_s[1, g * SUB + s]
            targets[pl.ds(g * TARGET + s, 6, stride=SUB), :] = world[pl.ds(b, 6, stride=stride), :]
            sources[pl.ds(g * SOURCE + s, 3, stride=SUB), :] = world[pl.ds(a, 3, stride=stride), :]
        return carry

    lax.fori_loop(0, pairs_s.shape[1] // SUB, stage_local, 0, unroll=4)
    total = jnp.zeros(totals.shape, jnp.float32)
    for t in range(0, pairs_s.shape[1], LANE):
        turn_fields(
            lambda u, k: sources[u * SOURCE + k * SUB : u * SOURCE + (k + 1) * SUB, :],
            lambda u, k: targets[u * TARGET + k * SUB : u * TARGET + (k + 1) * SUB, :],
            lambda u: maps[u * SUB : (u + 1) * SUB, :],
            same[...],
            parts,
            turned,
            t,
        )
        sums = point_sums(turned, joined, partial, t)
        total = total + by_frag(sums, frag_a[:, t : t + LANE])[0:18, :]
        total = total + target_side(by_frag(sums, frag_b[:, t : t + LANE]))
    totals[...] = total


def remote_kernel(
    arrived, staged, remote_b, local_totals, dst_v, same, gather, place, mine,
    back, totals, side_a, joined, frags, index, parts, turned, partial, *, per_frag,
):
    f32 = jnp.float32
    pairs = parts.shape[0]
    peers = pairs // SUB
    own = lax.shift_right_logical(iota(1), shift_of(GROUP)) == iota(0)
    slot = lax.shift_right_logical(iota(1), shift_of(GROUP)).astype(f32)[0:1, :]

    def block(c, total):
        first = c * peers

        def extras(u):
            row = arrived[pl.ds((first + u) * MSG + 4 * SUB, 1), :]
            frags[u * SUB : (u + 1) * SUB, :] = pick(row, iota(0) * GROUP + 13)
            return jnp.where(own, jnp.broadcast_to(row, (SUB, LANE)), 0.0)

        rows = [jnp.zeros((peers, LANE), f32) for half in range(2)]
        for t in range(0, pairs, LANE):
            lanes = slice(t, t + LANE)
            lanes_b = pl.ds(pl.multiple_of(c * pairs, LANE) + t, LANE)
            for u in range(t // SUB, (t + LANE) // SUB):
                row = (first + u) * MSG + 3 * SUB
                index[u * SUB : (u + 1) * SUB, :] = arrived[pl.ds(row, SUB), :].astype(jnp.int32)
            side_a[:, lanes] = turn(extras, gather[...], parts, 9, t)
            join_directions(side_a, remote_b, joined, lanes, lanes_b)
            turn_fields(
                lambda u, k: arrived[pl.ds((first + u) * MSG + SUB * k, SUB), :],
                lambda u, k: staged[
                    pl.ds(pl.multiple_of((first + u) * TARGET, SUB) + SUB * k, SUB), :
                ],
                lambda u: index[u * SUB : (u + 1) * SUB, :],
                same[...],
                parts,
                turned,
                t,
            )
            sums = point_sums(turned, joined, partial, t) * side_a[12:13, lanes]
            placed = lax.dot_general(
                jnp.concatenate(halves_of(sums), axis=0),
                place[...],
                (((0,), (0,)), ((), ())),
                preferred_element_type=f32,
            )
            hit = frags[lanes, :] == jnp.broadcast_to(slot, (LANE, LANE))
            for half in range(2):
                part = jnp.where(hit, placed[:, half * LANE : (half + 1) * LANE], 0.0)
                for piece in halves_of(part):
                    rows[half] = rows[half] + jnp.dot(
                        mine[:, lanes], piece, preferred_element_type=f32
                    )
            total = total + target_side(by_frag(sums, frag_of(dst_v[0:1, lanes_b], per_frag)))
        for half in range(2):
            back[pl.ds(2 * first + half, peers, stride=2), :] = rows[half]
        return total

    totals[...] = lax.fori_loop(0, back.shape[0] // (2 * peers), block, local_totals[...])


def final_kernel(back, totals, gradient, hess, *, per_frag):
    devices = back.shape[0] // 2
    index = iota(0) * GROUP + lax.bitwise_and(iota(1), GROUP - 1)
    halves = []
    for half in range(2):
        tile = back[pl.ds(half, SUB, stride=2), :]
        for q in range(SUB, devices, SUB):
            tile = tile + back[pl.ds(2 * q + half, SUB, stride=2), :]
        halves.append(pick(jnp.sum(tile, axis=0, keepdims=True), index))
    total = jnp.where(iota(1) < GROUP, halves[0], halves[1]).T[0:18, :] + totals[...]
    gradient[...] = total[0:6, :] * (1.0 / LANE)
    for v in range(2):
        part = total[6 + 6 * v : 12 + 6 * v, :] * (1.0 / (LANE * per_frag))
        for j in range(6):
            hess[j, v : v + 1, :] = part[j : j + 1, :]


def call(kernel, outs, scratch, spaces, limit=VMEM_LIMIT, out_space="v", **more):
    kinds = {"v": pltpu.VMEM, "s": pltpu.SMEM, "h": pltpu.HBM}
    return pl.pallas_call(
        kernel,
        out_shape=outs,
        in_specs=[pl.BlockSpec(memory_space=kinds[s]) for s in spaces],
        out_specs=[pl.BlockSpec(memory_space=kinds[out_space])] * len(outs),
        scratch_shapes=scratch,
        compiler_params=pltpu.CompilerParams(vmem_limit_bytes=limit),
        **more,
    )


def in_hbm(values):
    return pltpu.with_memory_space_constraint(values, pltpu.HBM)


def exchange(rows, devices):
    sent = rows.reshape(devices, 1, -1)
    sent = lax.all_to_all(sent, AXES, split_axis=0, concat_axis=0, tiled=True)
    return sent.reshape(rows.shape)


def local(
    points, normals, poses, directions, local_pairs, local_maps,
    remote_src, remote_maps, remote_dst, counts,
):
    devices = lax.axis_size("tile") * lax.axis_size("band")
    blocks, _, count = points.shape
    frags = poses.shape[1]
    slots = remote_src.shape[1]
    pairs = local_pairs.shape[1]
    assert count == LANE and frags == SUB and slots == devices * SUB and devices % PEERS == 0
    per_frag = blocks // frags
    stride = blocks + SUB
    f32 = jnp.float32
    points = points.transpose(1, 0, 2)
    normals = normals.transpose(1, 0, 2)
    directions = directions.transpose(1, 0, 2)

    def array(*shape, dtype=f32):
        return jax.ShapeDtypeStruct(shape, dtype)

    def vmem(*shape, dtype=f32):
        return pltpu.VMEM(shape, dtype)

    i32, bf16 = jnp.int32, jnp.bfloat16
    part = PEERS * SUB
    (message,) = call(
        pack_kernel,
        [array(devices * MSG, LANE)],
        [
            vmem(3, blocks, LANE),
            pltpu.SMEM((6, frags), f32),
            vmem(6, 2, frags),
            pltpu.SMEM((1, slots), i32),
            vmem(1, slots, dtype=i32),
            vmem(slots, LANE, dtype=i32),
            vmem(1, devices, dtype=i32),
            vmem(3 * stride, LANE),
            vmem(12 * frags * SUB, LANE),
            vmem(2 * SUB, LANE),
            vmem(devices * MSG, LANE),
            pltpu.SemaphoreType.DMA((13,)),
            pltpu.SemaphoreType.DMA((devices // SUB,)),
        ],
        "hhhhhh",
        limit=PACK_LIMIT,
        out_space="h",
    )(*[in_hbm(x) for x in (points, poses, directions, remote_src, remote_maps[0], counts)])
    arrived = exchange(message, devices)
    staged, remote_b, totals, same, gather, place, mine = call(
        local_kernel,
        [
            array(devices * TARGET, LANE),
            array(2 * SUB, slots),
            array(18, frags),
            array(LANE, 2 * LANE, dtype=bf16),
            array(GROUP, 2 * LANE, dtype=bf16),
            array(2 * ROWS, 2 * LANE, dtype=bf16),
            array(PEERS, part, dtype=bf16),
        ],
        [
            vmem(6 * stride, LANE),
            vmem(12 * frags * SUB, LANE),
            vmem(2 * SUB, LANE),
            vmem(pairs // SUB * SOURCE, LANE),
            vmem(pairs // SUB * TARGET, LANE),
            vmem(2 * SUB, pairs),
            vmem(2 * SUB, pairs),
            vmem(3 * SUB, pairs),
            vmem(pairs, 9 * 2 * LANE, dtype=bf16),
            vmem(9 * LANE, pairs),
            vmem(pairs // LANE * ROWS * SUB, LANE),
        ],
        "vvsvsvvsv",
        cost_estimate=pl.CostEstimate(
            flops=200 * pairs * LANE, bytes_accessed=4_000_000, transcendentals=0
        ),
    )(
        points, normals, poses, directions, local_pairs, local_pairs, local_maps,
        remote_dst, remote_dst,
    )
    back, totals = call(
        functools.partial(remote_kernel, per_frag=per_frag),
        [array(devices * 2, LANE), array(18, frags)],
        [
            vmem(2 * SUB, part),
            vmem(3 * SUB, part),
            vmem(part, LANE),
            vmem(part, LANE, dtype=i32),
            vmem(part, 10 * 2 * LANE, dtype=bf16),
            vmem(9 * LANE, part),
            vmem(part // LANE * ROWS * SUB, LANE),
        ],
        "vvvvvvvvv",
    )(arrived, staged, remote_b, totals, remote_dst, same, gather, place, mine)
    back = exchange(back, devices)
    gradient, hess = call(
        functools.partial(final_kernel, per_frag=per_frag),
        [array(6, frags), array(6, 2, frags)],
        [],
        "vv",
    )(back, totals)
    return (gradient, hess.transpose(1, 0, 2))


def solution(mesh):
    placed = (
        P(AXES, None, None),
        P(AXES, None, None),
        P(None, AXES),
        P(None, None, AXES),
        P(None, AXES),
        P(AXES, None),
        P(AXES, None),
        P(AXES, None, None),
        P(AXES, None),
        P(AXES, None),
    )
    return jax.shard_map(
        local,
        mesh=mesh,
        in_specs=placed,
        out_specs=(P(None, AXES), P(None, None, AXES)),
        check_vma=False,
    )
```

```python
import functools

import jax
import jax.numpy as jnp
from jax import lax
from jax.experimental import pallas as pl
from jax.experimental.pallas import tpu as pltpu
from jax.sharding import PartitionSpec as P

AXES = ("tile", "band")
SUB = 8
LANE = 128
MSG = 4 * SUB + 1
TARGET = 6 * SUB
SOURCE = 3 * SUB
ROWS = 32
GROUP = 16
VMEM_LIMIT = 16 * 1024 * 1024
PACK_LIMIT = 56 * 1024 * 1024
PEERS = 32


def iota(axis):
    return lax.broadcasted_iota(jnp.int32, (SUB, LANE), axis)


def pick(values, index):
    values = jnp.broadcast_to(values, (SUB, LANE))
    return jnp.take_along_axis(values, index, axis=1, mode="promise_in_bounds")


def shift_of(size):
    shift = size.bit_length() - 1
    assert 1 << shift == size
    return shift


def cross(left, right):
    return [
        left[1] * right[2] - left[2] * right[1],
        left[2] * right[0] - left[0] * right[2],
        left[0] * right[1] - left[1] * right[0],
    ]


def dot3(left, right):
    return left[0] * right[0] + left[1] * right[1] + left[2] * right[2]


def splat_rotation(poses, f):
    half = [jnp.full((SUB, LANE), poses[i, f] * 0.5, jnp.float32) for i in range(3)]
    w = 1.0 / jnp.sqrt(1.0 + half[0] * half[0] + half[1] * half[1] + half[2] * half[2])
    x, y, z = half[0] * w, half[1] * w, half[2] * w
    rotation = [
        [1.0 - 2.0 * (y * y + z * z), 2.0 * (x * y - w * z), 2.0 * (x * z + w * y)],
        [2.0 * (x * y + w * z), 1.0 - 2.0 * (x * x + z * z), 2.0 * (y * z - w * x)],
        [2.0 * (x * z - w * y), 2.0 * (y * z + w * x), 1.0 - 2.0 * (x * x + y * y)],
    ]
    return rotation, [jnp.full((SUB, LANE), poses[i, f], jnp.float32) for i in range(3, 6)]


def write_rotations(poses, turns):
    for f in range(poses.shape[1]):
        rotation, move = splat_rotation(poses, f)
        for i, tile in enumerate(rotation[0] + rotation[1] + rotation[2] + move):
            at = (12 * f + i) * SUB
            turns[at : at + SUB, :] = tile


def write_world(fields, turns, world, frags):
    blocks = fields[0].shape[1]
    total = turns.shape[0] // (12 * SUB)
    per_frag, stride = blocks // total, blocks + SUB
    for f in frags:
        tile = [turns[(12 * f + i) * SUB : (12 * f + i + 1) * SUB, :] for i in range(12)]
        for b in range(f * per_frag, (f + 1) * per_frag, SUB):
            for at, field in enumerate(fields):
                x = [field[j, b : b + SUB, :] for j in range(3)]
                for i in range(3):
                    row = dot3(tile[3 * i : 3 * i + 3], x)
                    if at == 0:
                        row = row + tile[9 + i]
                    world[pl.ds((3 * at + i) * stride + b, SUB), :] = row


def write_directions(directions, table):
    frags = directions.shape[2]
    for v in range(2):
        for j in range(6):
            table[6 * v + j : 6 * v + j + 1, 0:frags] = directions[j, v : v + 1, :]


def index_tile(row_ref, first, offset):
    tile = first // LANE * LANE
    return pick(row_ref[0:1, pl.ds(tile, LANE)], offset + first % LANE)


def pack_kernel(
    points_h, poses_h, directions_h, src_h, maps_h, counts_h, out_h,
    points, poses, directions, src_s, src_v, maps, used, world, turns, table, out, sems, out_sems,
):
    devices = counts_h.shape[1]
    per_frag = points.shape[1] // poses.shape[1]
    stride = points.shape[1] + SUB
    frags = poses.shape[1]
    pairs = [(directions_h, directions), (src_h, src_v), (counts_h, used), (poses_h, poses)]
    pairs += [(points_h.at[j], points.at[j]) for j in range(3)]
    pairs += [(src_h, src_s), (maps_h, maps)]
    copies = [pltpu.make_async_copy(a, b, sems.at[i]) for i, (a, b) in enumerate(pairs)]
    for copy in copies:
        copy.start()
    for copy in copies[0:3]:
        copy.wait()
    write_directions(directions, table)
    limits = jnp.broadcast_to(used[0:1, :], (SUB, devices)).astype(jnp.float32)
    peers = lax.broadcasted_iota(jnp.int32, (SUB, devices), 1)
    row = lax.broadcasted_iota(jnp.int32, (SUB, devices), 0)
    slot = lax.shift_right_logical(iota(1), shift_of(GROUP))
    field = lax.bitwise_and(iota(1), GROUP - 1)
    for q in range(0, devices, SUB):
        block = index_tile(src_v, q * SUB, iota(0) * SUB + slot)
        frag = lax.shift_right_logical(block, shift_of(per_frag))
        limit = jnp.sum(jnp.where(peers == row + q, limits, 0.0), axis=1, keepdims=True)
        extras = jnp.where(slot.astype(jnp.float32) < limit, 1.0, 0.0)
        for j in range(12):
            extras = jnp.where(field == j, pick(table[j : j + 1, :], frag), extras)
        extras = jnp.where(field == 13, frag.astype(jnp.float32), extras)
        out[pl.ds(q * MSG + MSG - 1, SUB, stride=MSG), :] = extras
    copies[3].wait()
    write_rotations(poses, turns)
    for copy in copies[4:7]:
        copy.wait()
    write_world([points], turns, world, range(frags))
    for copy in copies[7:]:
        copy.wait()

    def peer(p):
        for s in range(SUB):
            block = src_s[0, p * SUB + s]
            out[pl.ds(p * MSG + s, 3, stride=SUB), :] = world[pl.ds(block, 3, stride=stride), :]
        rows = maps[pl.ds(pl.multiple_of(p * SUB, SUB), SUB), :]
        out[pl.ds(p * MSG + 3 * SUB, SUB), :] = rows.astype(jnp.float32)

    def piece(i):
        rows = pl.ds(pl.multiple_of(i * SUB * MSG, SUB), SUB * MSG)
        return pltpu.make_async_copy(out.at[rows], out_h.at[rows], out_sems.at[i])

    def pack(i, carry):
        for u in range(SUB):
            peer(i * SUB + u)
        piece(i).start()
        return carry

    lax.fori_loop(0, devices // SUB, pack, 0)
    for i in range(devices // SUB):
        piece(i).wait()


def halves_of(values):
    high = values.astype(jnp.bfloat16)
    return high, (values - high.astype(jnp.float32)).astype(jnp.bfloat16)


def turn(at, left, parts, i, t):
    columns = slice(i * 2 * LANE, i * 2 * LANE + LANE), slice(i * 2 * LANE + LANE, (i + 1) * 2 * LANE)
    for u in range(t // SUB, (t + LANE) // SUB, 2):
        high, low = halves_of(jnp.concatenate([at(u), at(u + 1)], axis=0))
        parts[u * SUB : (u + 2) * SUB, columns[0]] = high
        parts[u * SUB : (u + 2) * SUB, columns[1]] = low
    return lax.dot_general(
        left,
        parts[t : t + LANE, i * 2 * LANE : (i + 1) * 2 * LANE],
        (((1,), (1,)), ((), ())),
        preferred_element_type=jnp.float32,
    )


def turn_fields(source, target, index, same, parts, turned, t):
    lanes = slice(t, t + LANE)
    for k in range(6):

        def at(u, k=k):
            return pick(target(u, k), index(u))

        turned[k * LANE : (k + 1) * LANE, lanes] = turn(at, same, parts, k, t)
    for k in range(3):
        tiles = [source(u, k) for u in range(t // SUB, (t + LANE) // SUB)]
        turned[(6 + k) * LANE : (7 + k) * LANE, lanes] = jnp.concatenate(tiles, axis=0).T


def join_directions(side_a, side_b, joined, lanes, lanes_b):
    joined[0:12, lanes] = side_a[0:12, lanes]
    for v in range(2):
        turn_rows, move_rows = slice(6 * v, 6 * v + 3), slice(6 * v + 3, 6 * v + 6)
        joined[move_rows, lanes] = side_a[move_rows, lanes] - side_b[move_rows, lanes_b]
        joined[12 + 3 * v : 15 + 3 * v, lanes] = side_b[turn_rows, lanes_b]


def point_sums(turned, joined, partial, t):
    lanes = slice(t, t + LANE)
    first = t // LANE * ROWS * SUB

    def add(i, totals):
        start = pl.multiple_of(i * SUB, SUB)
        field = [turned[pl.ds(start + k * LANE, SUB), lanes] for k in range(9)]
        way = [joined[j : j + 1, lanes] for j in range(18)]
        y, n, x = field[0:3], field[3:6], field[6:9]
        p, q = cross(x, n), cross(y, n)
        scalars = [dot3(n, [x[k] - y[k] for k in range(3)])]
        for v in range(2):
            a, b = way[6 * v : 6 * v + 6], way[12 + 3 * v : 15 + 3 * v]
            scalars.append(dot3(p, a[0:3]) + dot3(n, a[3:6]) - dot3(q, b))
        terms = []
        for s in scalars:
            terms += [s * value for value in p + n]
        for s in scalars:
            terms += [s * value for value in q]
        return tuple(total + term for total, term in zip(totals, terms))

    zero = jnp.zeros((SUB, LANE), jnp.float32)
    totals = lax.fori_loop(0, LANE // SUB, add, (zero,) * 27, unroll=LANE // SUB)
    for j in range(ROWS):
        partial[first + j * SUB : first + (j + 1) * SUB, :] = totals[j] if j < 27 else zero
    total = partial[pl.ds(first, ROWS, stride=SUB), :]
    for s in range(1, SUB):
        total = total + partial[pl.ds(first + s, ROWS, stride=SUB), :]
    return total


def frag_of(row, per_frag):
    return lax.shift_right_logical(row, shift_of(per_frag))


def look_up(table, frag, out):
    for at in range(0, frag.shape[1], LANE):
        index = jnp.broadcast_to(frag[:, at : at + LANE], (SUB, LANE))
        for j in range(0, 2 * SUB, SUB):
            out[j : j + SUB, at : at + LANE] = pick(table[j : j + SUB, :], index)


def by_frag(sums, frag):
    pairs = sums.shape[1]
    hot = jnp.broadcast_to(frag, (SUB, pairs)) == lax.broadcasted_iota(jnp.int32, (SUB, pairs), 0)
    return lax.dot_general(
        sums,
        hot.astype(jnp.float32),
        (((1,), (1,)), ((), ())),
        precision=lax.Precision.HIGHEST,
        preferred_element_type=jnp.float32,
    )


def target_side(total):
    rows = []
    for k in range(3):
        rows += [total[18 + 3 * k : 21 + 3 * k, :], total[6 * k + 3 : 6 * k + 6, :]]
    return -jnp.concatenate(rows, axis=0)


def constants(same, gather, place, mine):
    def wide(ref, axis):
        return lax.broadcasted_iota(jnp.int32, ref.shape, axis)

    def put(ref, hit):
        ref[...] = hit.astype(jnp.float32).astype(jnp.bfloat16)

    put(same, lax.bitwise_and(wide(same, 1), LANE - 1) == wide(same, 0))
    put(gather, lax.bitwise_and(wide(gather, 1), GROUP - 1) == wide(gather, 0))
    entry = lax.bitwise_and(wide(place, 1), GROUP - 1) + GROUP * lax.shift_right_logical(
        wide(place, 1), shift_of(LANE)
    )
    put(place, lax.bitwise_and(wide(place, 0), ROWS - 1) == entry)
    put(mine, lax.shift_right_logical(wide(mine, 1), shift_of(SUB)) == wide(mine, 0))


def local_kernel(
    points, normals, poses, directions, pairs_s, pairs_v, maps, dst_s, dst_v,
    staged, remote_b, totals, same, gather, place, mine,
    world, turns, table, sources, targets, side_a, side_b, joined, parts, turned, partial,
):
    per_frag = points.shape[1] // poses.shape[1]
    stride = points.shape[1] + SUB
    constants(same, gather, place, mine)
    table[...] = jnp.zeros_like(table)
    write_directions(directions, table)
    look_up(table, frag_of(dst_v[...], per_frag), remote_b)
    frag_a, frag_b = frag_of(pairs_v[0:1, :], per_frag), frag_of(pairs_v[1:2, :], per_frag)
    look_up(table, frag_a, side_a)
    look_up(table, frag_b, side_b)
    every = slice(0, pairs_s.shape[1])
    join_directions(side_a, side_b, joined, every, every)
    write_rotations(poses, turns)
    write_world([points, normals], turns, world, range(poses.shape[1]))

    def stage_remote(g, carry):
        for s in range(SUB):
            block = dst_s[0, g * SUB + s]
            staged[pl.ds(g * TARGET + s, 6, stride=SUB), :] = world[pl.ds(block, 6, stride=stride), :]
        return carry

    lax.fori_loop(0, dst_s.shape[1] // SUB, stage_remote, 0, unroll=4)

    def stage_local(g, carry):
        for s in range(SUB):
            a, b = pairs_s[0, g * SUB + s], pairs_s[1, g * SUB + s]
            targets[pl.ds(g * TARGET + s, 6, stride=SUB), :] = world[pl.ds(b, 6, stride=stride), :]
            sources[pl.ds(g * SOURCE + s, 3, stride=SUB), :] = world[pl.ds(a, 3, stride=stride), :]
        return carry

    lax.fori_loop(0, pairs_s.shape[1] // SUB, stage_local, 0, unroll=4)
    total = jnp.zeros(totals.shape, jnp.float32)
    for t in range(0, pairs_s.shape[1], LANE):
        turn_fields(
            lambda u, k: sources[u * SOURCE + k * SUB : u * SOURCE + (k + 1) * SUB, :],
            lambda u, k: targets[u * TARGET + k * SUB : u * TARGET + (k + 1) * SUB, :],
            lambda u: maps[u * SUB : (u + 1) * SUB, :],
            same[...],
            parts,
            turned,
            t,
        )
        sums = point_sums(turned, joined, partial, t)
        total = total + by_frag(sums, frag_a[:, t : t + LANE])[0:18, :]
        total = total + target_side(by_frag(sums, frag_b[:, t : t + LANE]))
    totals[...] = total


def remote_kernel(
    arrived, staged, remote_b, local_totals, dst_v, same, gather, place, mine,
    back, totals, side_a, joined, frags, index, parts, turned, partial, *, per_frag,
):
    f32 = jnp.float32
    pairs = parts.shape[0]
    peers = pairs // SUB
    own = lax.shift_right_logical(iota(1), shift_of(GROUP)) == iota(0)
    slot = lax.shift_right_logical(iota(1), shift_of(GROUP)).astype(f32)[0:1, :]

    def block(c, total):
        first = c * peers

        def extras(u):
            row = arrived[pl.ds((first + u) * MSG + 4 * SUB, 1), :]
            frags[u * SUB : (u + 1) * SUB, :] = pick(row, iota(0) * GROUP + 13)
            return jnp.where(own, jnp.broadcast_to(row, (SUB, LANE)), 0.0)

        rows = [jnp.zeros((peers, LANE), f32) for half in range(2)]
        for t in range(0, pairs, LANE):
            lanes = slice(t, t + LANE)
            lanes_b = pl.ds(pl.multiple_of(c * pairs, LANE) + t, LANE)
            for u in range(t // SUB, (t + LANE) // SUB):
                row = (first + u) * MSG + 3 * SUB
                index[u * SUB : (u + 1) * SUB, :] = arrived[pl.ds(row, SUB), :].astype(jnp.int32)
            side_a[:, lanes] = turn(extras, gather[...], parts, 6, t)
            join_directions(side_a, remote_b, joined, lanes, lanes_b)
            turn_fields(
                lambda u, k: arrived[pl.ds((first + u) * MSG + SUB * k, SUB), :],
                lambda u, k: staged[
                    pl.ds(pl.multiple_of((first + u) * TARGET, SUB) + SUB * k, SUB), :
                ],
                lambda u: index[u * SUB : (u + 1) * SUB, :],
                same[...],
                parts,
                turned,
                t,
            )
            sums = point_sums(turned, joined, partial, t) * side_a[12:13, lanes]
            placed = lax.dot_general(
                jnp.concatenate(halves_of(sums), axis=0),
                place[...],
                (((0,), (0,)), ((), ())),
                preferred_element_type=f32,
            )
            hit = frags[lanes, :] == jnp.broadcast_to(slot, (LANE, LANE))
            for half in range(2):
                part = jnp.where(hit, placed[:, half * LANE : (half + 1) * LANE], 0.0)
                for piece in halves_of(part):
                    rows[half] = rows[half] + jnp.dot(
                        mine[:, lanes], piece, preferred_element_type=f32
                    )
            total = total + target_side(by_frag(sums, frag_of(dst_v[0:1, lanes_b], per_frag)))
        for half in range(2):
            back[pl.ds(2 * first + half, peers, stride=2), :] = rows[half]
        return total

    totals[...] = lax.fori_loop(0, back.shape[0] // (2 * peers), block, local_totals[...])


def final_kernel(back, totals, gradient, hess, *, per_frag):
    devices = back.shape[0] // 2
    index = iota(0) * GROUP + lax.bitwise_and(iota(1), GROUP - 1)
    halves = []
    for half in range(2):
        tile = back[pl.ds(half, SUB, stride=2), :]
        for q in range(SUB, devices, SUB):
            tile = tile + back[pl.ds(2 * q + half, SUB, stride=2), :]
        halves.append(pick(jnp.sum(tile, axis=0, keepdims=True), index))
    total = jnp.where(iota(1) < GROUP, halves[0], halves[1]).T[0:18, :] + totals[...]
    gradient[...] = total[0:6, :] * (1.0 / LANE)
    for v in range(2):
        part = total[6 + 6 * v : 12 + 6 * v, :] * (1.0 / (LANE * per_frag))
        for j in range(6):
            hess[j, v : v + 1, :] = part[j : j + 1, :]


def call(kernel, outs, scratch, spaces, limit=VMEM_LIMIT, out_space="v", **more):
    kinds = {"v": pltpu.VMEM, "s": pltpu.SMEM, "h": pltpu.HBM}
    return pl.pallas_call(
        kernel,
        out_shape=outs,
        in_specs=[pl.BlockSpec(memory_space=kinds[s]) for s in spaces],
        out_specs=[pl.BlockSpec(memory_space=kinds[out_space])] * len(outs),
        scratch_shapes=scratch,
        compiler_params=pltpu.CompilerParams(vmem_limit_bytes=limit),
        **more,
    )


def in_hbm(values):
    return pltpu.with_memory_space_constraint(values, pltpu.HBM)


def exchange(rows, devices):
    sent = rows.reshape(devices, 1, -1)
    sent = lax.all_to_all(sent, AXES, split_axis=0, concat_axis=0, tiled=True)
    return sent.reshape(rows.shape)


def local(
    points, normals, poses, directions, local_pairs, local_maps,
    remote_src, remote_maps, remote_dst, counts,
):
    devices = lax.axis_size("tile") * lax.axis_size("band")
    blocks, _, count = points.shape
    frags = poses.shape[1]
    slots = remote_src.shape[1]
    pairs = local_pairs.shape[1]
    assert count == LANE and frags == SUB and slots == devices * SUB and devices % PEERS == 0
    per_frag = blocks // frags
    stride = blocks + SUB
    f32 = jnp.float32
    points = points.transpose(1, 0, 2)
    normals = normals.transpose(1, 0, 2)
    directions = directions.transpose(1, 0, 2)

    def array(*shape, dtype=f32):
        return jax.ShapeDtypeStruct(shape, dtype)

    def vmem(*shape, dtype=f32):
        return pltpu.VMEM(shape, dtype)

    i32, bf16 = jnp.int32, jnp.bfloat16
    part = PEERS * SUB
    (message,) = call(
        pack_kernel,
        [array(devices * MSG, LANE)],
        [
            vmem(3, blocks, LANE),
            pltpu.SMEM((6, frags), f32),
            vmem(6, 2, frags),
            pltpu.SMEM((1, slots), i32),
            vmem(1, slots, dtype=i32),
            vmem(slots, LANE, dtype=i32),
            vmem(1, devices, dtype=i32),
            vmem(3 * stride, LANE),
            vmem(12 * frags * SUB, LANE),
            vmem(2 * SUB, LANE),
            vmem(devices * MSG, LANE),
            pltpu.SemaphoreType.DMA((9,)),
            pltpu.SemaphoreType.DMA((devices // SUB,)),
        ],
        "hhhhhh",
        limit=PACK_LIMIT,
        out_space="h",
    )(*[in_hbm(x) for x in (points, poses, directions, remote_src, remote_maps[0], counts)])
    arrived = exchange(message, devices)
    staged, remote_b, totals, same, gather, place, mine = call(
        local_kernel,
        [
            array(devices * TARGET, LANE),
            array(2 * SUB, slots),
            array(18, frags),
            array(LANE, 2 * LANE, dtype=bf16),
            array(GROUP, 2 * LANE, dtype=bf16),
            array(2 * ROWS, 2 * LANE, dtype=bf16),
            array(PEERS, part, dtype=bf16),
        ],
        [
            vmem(6 * stride, LANE),
            vmem(12 * frags * SUB, LANE),
            vmem(2 * SUB, LANE),
            vmem(pairs // SUB * SOURCE, LANE),
            vmem(pairs // SUB * TARGET, LANE),
            vmem(2 * SUB, pairs),
            vmem(2 * SUB, pairs),
            vmem(3 * SUB, pairs),
            vmem(pairs, 6 * 2 * LANE, dtype=bf16),
            vmem(9 * LANE, pairs),
            vmem(pairs // LANE * ROWS * SUB, LANE),
        ],
        "vvsvsvvsv",
        cost_estimate=pl.CostEstimate(
            flops=200 * pairs * LANE, bytes_accessed=4_000_000, transcendentals=0
        ),
    )(
        points, normals, poses, directions, local_pairs, local_pairs, local_maps,
        remote_dst, remote_dst,
    )
    back, totals = call(
        functools.partial(remote_kernel, per_frag=per_frag),
        [array(devices * 2, LANE), array(18, frags)],
        [
            vmem(2 * SUB, part),
            vmem(3 * SUB, part),
            vmem(part, LANE),
            vmem(part, LANE, dtype=i32),
            vmem(part, 7 * 2 * LANE, dtype=bf16),
            vmem(9 * LANE, part),
            vmem(part // LANE * ROWS * SUB, LANE),
        ],
        "vvvvvvvvv",
    )(arrived, staged, remote_b, totals, remote_dst, same, gather, place, mine)
    back = exchange(back, devices)
    gradient, hess = call(
        functools.partial(final_kernel, per_frag=per_frag),
        [array(6, frags), array(6, 2, frags)],
        [],
        "vv",
    )(back, totals)
    return (gradient, hess.transpose(1, 0, 2))


def solution(mesh):
    placed = (
        P(AXES, None, None),
        P(AXES, None, None),
        P(None, AXES),
        P(None, None, AXES),
        P(None, AXES),
        P(AXES, None),
        P(AXES, None),
        P(AXES, None, None),
        P(AXES, None),
        P(AXES, None),
    )
    return jax.shard_map(
        local,
        mesh=mesh,
        in_specs=placed,
        out_specs=(P(None, AXES), P(None, None, AXES)),
        check_vma=False,
    )
```

```python
import functools

import jax
import jax.numpy as jnp
from jax import lax
from jax.experimental import pallas as pl
from jax.experimental.pallas import tpu as pltpu
from jax.sharding import PartitionSpec as P

AXES = ("tile", "band")
ORDER = ("band", "tile")
SUB = 8
LANE = 128
MSG = 4 * SUB + 1
TARGET = 6 * SUB
SOURCE = 3 * SUB
ROWS = 32
GROUP = 16
VMEM_LIMIT = 16 * 1024 * 1024
PACK_LIMIT = 56 * 1024 * 1024
PEERS = 32


def iota(axis):
    return lax.broadcasted_iota(jnp.int32, (SUB, LANE), axis)


def pick(values, index):
    values = jnp.broadcast_to(values, (SUB, LANE))
    return jnp.take_along_axis(values, index, axis=1, mode="promise_in_bounds")


def shift_of(size):
    shift = size.bit_length() - 1
    assert 1 << shift == size
    return shift


def cross(left, right):
    return [
        left[1] * right[2] - left[2] * right[1],
        left[2] * right[0] - left[0] * right[2],
        left[0] * right[1] - left[1] * right[0],
    ]


def dot3(left, right):
    return left[0] * right[0] + left[1] * right[1] + left[2] * right[2]


def splat_rotation(poses, f):
    half = [jnp.full((SUB, LANE), poses[i, f] * 0.5, jnp.float32) for i in range(3)]
    w = 1.0 / jnp.sqrt(1.0 + half[0] * half[0] + half[1] * half[1] + half[2] * half[2])
    x, y, z = half[0] * w, half[1] * w, half[2] * w
    rotation = [
        [1.0 - 2.0 * (y * y + z * z), 2.0 * (x * y - w * z), 2.0 * (x * z + w * y)],
        [2.0 * (x * y + w * z), 1.0 - 2.0 * (x * x + z * z), 2.0 * (y * z - w * x)],
        [2.0 * (x * z - w * y), 2.0 * (y * z + w * x), 1.0 - 2.0 * (x * x + y * y)],
    ]
    return rotation, [jnp.full((SUB, LANE), poses[i, f], jnp.float32) for i in range(3, 6)]


def write_rotations(poses, turns):
    for f in range(poses.shape[1]):
        rotation, move = splat_rotation(poses, f)
        for i, tile in enumerate(rotation[0] + rotation[1] + rotation[2] + move):
            at = (12 * f + i) * SUB
            turns[at : at + SUB, :] = tile


def write_world(fields, turns, world, frags):
    blocks = fields[0].shape[1]
    total = turns.shape[0] // (12 * SUB)
    per_frag, stride = blocks // total, blocks + SUB
    for f in frags:
        tile = [turns[(12 * f + i) * SUB : (12 * f + i + 1) * SUB, :] for i in range(12)]
        for b in range(f * per_frag, (f + 1) * per_frag, SUB):
            for at, field in enumerate(fields):
                x = [field[j, b : b + SUB, :] for j in range(3)]
                for i in range(3):
                    row = dot3(tile[3 * i : 3 * i + 3], x)
                    if at == 0:
                        row = row + tile[9 + i]
                    world[pl.ds((3 * at + i) * stride + b, SUB), :] = row


def write_directions(directions, table):
    frags = directions.shape[2]
    for v in range(2):
        for j in range(6):
            table[6 * v + j : 6 * v + j + 1, 0:frags] = directions[j, v : v + 1, :]


def peer_at(place, sizes):
    n_tile, n_band = sizes
    tile = lax.bitwise_and(place, n_tile - 1)
    return tile * n_band + lax.shift_right_logical(place, shift_of(n_tile))


def entries(row_ref, index):
    out = jnp.zeros((SUB, LANE), row_ref.dtype)
    tile = lax.shift_right_logical(index, shift_of(LANE))
    for t in range(row_ref.shape[1] // LANE):
        hit = pick(row_ref[0:1, t * LANE : (t + 1) * LANE], lax.bitwise_and(index, LANE - 1))
        out = jnp.where(tile == t, hit, out)
    return out


def pack_kernel(
    points_h, poses_h, directions_h, src_h, maps_h, counts_h, out_h,
    points, poses, directions, src_s, src_v, maps, used, world, turns, table, out, sems, out_sems, *, sizes,
):
    devices = counts_h.shape[1]
    per_frag = points.shape[1] // poses.shape[1]
    stride = points.shape[1] + SUB
    frags = poses.shape[1]
    pairs = [(directions_h, directions), (src_h, src_v), (counts_h, used), (poses_h, poses)]
    pairs += [(points_h.at[j], points.at[j]) for j in range(3)]
    pairs += [(src_h, src_s), (maps_h, maps)]
    copies = [pltpu.make_async_copy(a, b, sems.at[i]) for i, (a, b) in enumerate(pairs)]
    for copy in copies:
        copy.start()
    for copy in copies[0:3]:
        copy.wait()
    write_directions(directions, table)
    limits = jnp.broadcast_to(used[0:1, :], (SUB, devices)).astype(jnp.float32)
    peers = lax.broadcasted_iota(jnp.int32, (SUB, devices), 1)
    row = lax.broadcasted_iota(jnp.int32, (SUB, devices), 0)
    slot = lax.shift_right_logical(iota(1), shift_of(GROUP))
    field = lax.bitwise_and(iota(1), GROUP - 1)
    for q in range(0, devices, SUB):
        block = entries(src_v, peer_at(iota(0) + q, sizes) * SUB + slot)
        frag = lax.shift_right_logical(block, shift_of(per_frag))
        hit = peers == peer_at(row + q, sizes)
        limit = jnp.sum(jnp.where(hit, limits, 0.0), axis=1, keepdims=True)
        extras = jnp.where(slot.astype(jnp.float32) < limit, 1.0, 0.0)
        for j in range(12):
            extras = jnp.where(field == j, pick(table[j : j + 1, :], frag), extras)
        extras = jnp.where(field == 13, frag.astype(jnp.float32), extras)
        out[pl.ds(q * MSG + MSG - 1, SUB, stride=MSG), :] = extras
    copies[3].wait()
    write_rotations(poses, turns)
    for copy in copies[4:7]:
        copy.wait()
    write_world([points], turns, world, range(frags))
    for copy in copies[7:]:
        copy.wait()

    def peer(q):
        p = peer_at(q, sizes)
        for s in range(SUB):
            block = src_s[0, p * SUB + s]
            out[pl.ds(q * MSG + s, 3, stride=SUB), :] = world[pl.ds(block, 3, stride=stride), :]
        rows = maps[pl.ds(pl.multiple_of(p * SUB, SUB), SUB), :]
        out[pl.ds(q * MSG + 3 * SUB, SUB), :] = rows.astype(jnp.float32)

    def piece(i):
        rows = pl.ds(pl.multiple_of(i * SUB * MSG, SUB), SUB * MSG)
        return pltpu.make_async_copy(out.at[rows], out_h.at[rows], out_sems.at[i])

    def pack(i, carry):
        for u in range(SUB):
            peer(i * SUB + u)
        piece(i).start()
        return carry

    lax.fori_loop(0, devices // SUB, pack, 0)
    for i in range(devices // SUB):
        piece(i).wait()


def halves_of(values):
    high = values.astype(jnp.bfloat16)
    return high, (values - high.astype(jnp.float32)).astype(jnp.bfloat16)


def turn(at, left, parts, i, t):
    columns = slice(i * 2 * LANE, i * 2 * LANE + LANE), slice(i * 2 * LANE + LANE, (i + 1) * 2 * LANE)
    for u in range(t // SUB, (t + LANE) // SUB, 2):
        high, low = halves_of(jnp.concatenate([at(u), at(u + 1)], axis=0))
        parts[u * SUB : (u + 2) * SUB, columns[0]] = high
        parts[u * SUB : (u + 2) * SUB, columns[1]] = low
    return lax.dot_general(
        left,
        parts[t : t + LANE, i * 2 * LANE : (i + 1) * 2 * LANE],
        (((1,), (1,)), ((), ())),
        preferred_element_type=jnp.float32,
    )


def turn_fields(source, target, index, same, parts, turned, t):
    lanes = slice(t, t + LANE)
    for k in range(6):

        def at(u, k=k):
            return pick(target(u, k), index(u))

        turned[k * LANE : (k + 1) * LANE, lanes] = turn(at, same, parts, k, t)
    for k in range(3):
        tiles = [source(u, k) for u in range(t // SUB, (t + LANE) // SUB)]
        turned[(6 + k) * LANE : (7 + k) * LANE, lanes] = jnp.concatenate(tiles, axis=0).T


def join_directions(side_a, side_b, joined, lanes, lanes_b):
    joined[0:12, lanes] = side_a[0:12, lanes]
    for v in range(2):
        turn_rows, move_rows = slice(6 * v, 6 * v + 3), slice(6 * v + 3, 6 * v + 6)
        joined[move_rows, lanes] = side_a[move_rows, lanes] - side_b[move_rows, lanes_b]
        joined[12 + 3 * v : 15 + 3 * v, lanes] = side_b[turn_rows, lanes_b]


def point_sums(turned, joined, partial, t):
    lanes = slice(t, t + LANE)
    first = t // LANE * ROWS * SUB

    def add(i, totals):
        start = pl.multiple_of(i * SUB, SUB)
        field = [turned[pl.ds(start + k * LANE, SUB), lanes] for k in range(9)]
        way = [joined[j : j + 1, lanes] for j in range(18)]
        y, n, x = field[0:3], field[3:6], field[6:9]
        p, q = cross(x, n), cross(y, n)
        scalars = [dot3(n, [x[k] - y[k] for k in range(3)])]
        for v in range(2):
            a, b = way[6 * v : 6 * v + 6], way[12 + 3 * v : 15 + 3 * v]
            scalars.append(dot3(p, a[0:3]) + dot3(n, a[3:6]) - dot3(q, b))
        terms = []
        for s in scalars:
            terms += [s * value for value in p + n]
        for s in scalars:
            terms += [s * value for value in q]
        return tuple(total + term for total, term in zip(totals, terms))

    zero = jnp.zeros((SUB, LANE), jnp.float32)
    totals = lax.fori_loop(0, LANE // SUB, add, (zero,) * 27, unroll=LANE // SUB)
    for j in range(ROWS):
        partial[first + j * SUB : first + (j + 1) * SUB, :] = totals[j] if j < 27 else zero
    total = partial[pl.ds(first, ROWS, stride=SUB), :]
    for s in range(1, SUB):
        total = total + partial[pl.ds(first + s, ROWS, stride=SUB), :]
    return total


def frag_of(row, per_frag):
    return lax.shift_right_logical(row, shift_of(per_frag))


def look_up(table, frag, out):
    for at in range(0, frag.shape[1], LANE):
        index = jnp.broadcast_to(frag[:, at : at + LANE], (SUB, LANE))
        for j in range(0, 2 * SUB, SUB):
            out[j : j + SUB, at : at + LANE] = pick(table[j : j + SUB, :], index)


def by_frag(sums, frag):
    pairs = sums.shape[1]
    hot = jnp.broadcast_to(frag, (SUB, pairs)) == lax.broadcasted_iota(jnp.int32, (SUB, pairs), 0)
    return lax.dot_general(
        sums,
        hot.astype(jnp.float32),
        (((1,), (1,)), ((), ())),
        precision=lax.Precision.HIGHEST,
        preferred_element_type=jnp.float32,
    )


def target_side(total):
    rows = []
    for k in range(3):
        rows += [total[18 + 3 * k : 21 + 3 * k, :], total[6 * k + 3 : 6 * k + 6, :]]
    return -jnp.concatenate(rows, axis=0)


def constants(same, gather, place, mine):
    def wide(ref, axis):
        return lax.broadcasted_iota(jnp.int32, ref.shape, axis)

    def put(ref, hit):
        ref[...] = hit.astype(jnp.float32).astype(jnp.bfloat16)

    put(same, lax.bitwise_and(wide(same, 1), LANE - 1) == wide(same, 0))
    put(gather, lax.bitwise_and(wide(gather, 1), GROUP - 1) == wide(gather, 0))
    entry = lax.bitwise_and(wide(place, 1), GROUP - 1) + GROUP * lax.shift_right_logical(
        wide(place, 1), shift_of(LANE)
    )
    put(place, lax.bitwise_and(wide(place, 0), ROWS - 1) == entry)
    put(mine, lax.shift_right_logical(wide(mine, 1), shift_of(SUB)) == wide(mine, 0))


def local_kernel(
    points, normals, poses, directions, pairs_s, pairs_v, maps, dst_s, dst_v,
    staged, remote_b, remote_frag, totals, same, gather, place, mine,
    world, turns, table, sources, targets, side_a, side_b, joined, parts, turned, partial, *, sizes,
):
    per_frag = points.shape[1] // poses.shape[1]
    stride = points.shape[1] + SUB
    constants(same, gather, place, mine)
    table[...] = jnp.zeros_like(table)
    write_directions(directions, table)
    for at in range(0, dst_v.shape[1], LANE):
        flat = iota(1) + at
        peer = peer_at(lax.shift_right_logical(flat, shift_of(SUB)), sizes)
        block = entries(dst_v, peer * SUB + lax.bitwise_and(flat, SUB - 1))
        remote_frag[0:1, at : at + LANE] = frag_of(block, per_frag)[0:1, :]
    look_up(table, remote_frag[...], remote_b)
    frag_a, frag_b = frag_of(pairs_v[0:1, :], per_frag), frag_of(pairs_v[1:2, :], per_frag)
    look_up(table, frag_a, side_a)
    look_up(table, frag_b, side_b)
    every = slice(0, pairs_s.shape[1])
    join_directions(side_a, side_b, joined, every, every)
    write_rotations(poses, turns)
    write_world([points, normals], turns, world, range(poses.shape[1]))

    def stage_remote(g, carry):
        for s in range(SUB):
            block = dst_s[0, peer_at(g, sizes) * SUB + s]
            staged[pl.ds(g * TARGET + s, 6, stride=SUB), :] = world[pl.ds(block, 6, stride=stride), :]
        return carry

    lax.fori_loop(0, dst_s.shape[1] // SUB, stage_remote, 0, unroll=4)

    def stage_local(g, carry):
        for s in range(SUB):
            a, b = pairs_s[0, g * SUB + s], pairs_s[1, g * SUB + s]
            targets[pl.ds(g * TARGET + s, 6, stride=SUB), :] = world[pl.ds(b, 6, stride=stride), :]
            sources[pl.ds(g * SOURCE + s, 3, stride=SUB), :] = world[pl.ds(a, 3, stride=stride), :]
        return carry

    lax.fori_loop(0, pairs_s.shape[1] // SUB, stage_local, 0, unroll=4)
    total = jnp.zeros(totals.shape, jnp.float32)
    for t in range(0, pairs_s.shape[1], LANE):
        turn_fields(
            lambda u, k: sources[u * SOURCE + k * SUB : u * SOURCE + (k + 1) * SUB, :],
            lambda u, k: targets[u * TARGET + k * SUB : u * TARGET + (k + 1) * SUB, :],
            lambda u: maps[u * SUB : (u + 1) * SUB, :],
            same[...],
            parts,
            turned,
            t,
        )
        sums = point_sums(turned, joined, partial, t)
        total = total + by_frag(sums, frag_a[:, t : t + LANE])[0:18, :]
        total = total + target_side(by_frag(sums, frag_b[:, t : t + LANE]))
    totals[...] = total


def remote_kernel(
    arrived, staged, remote_b, remote_frag, local_totals, same, gather, place, mine,
    back, totals, side_a, joined, frags, index, parts, turned, partial,
):
    f32 = jnp.float32
    pairs = parts.shape[0]
    peers = pairs // SUB
    own = lax.shift_right_logical(iota(1), shift_of(GROUP)) == iota(0)
    slot = lax.shift_right_logical(iota(1), shift_of(GROUP)).astype(f32)[0:1, :]

    def block(c, total):
        first = c * peers

        def extras(u):
            row = arrived[pl.ds((first + u) * MSG + 4 * SUB, 1), :]
            frags[u * SUB : (u + 1) * SUB, :] = pick(row, iota(0) * GROUP + 13)
            return jnp.where(own, jnp.broadcast_to(row, (SUB, LANE)), 0.0)

        rows = [jnp.zeros((peers, LANE), f32) for half in range(2)]
        for t in range(0, pairs, LANE):
            lanes = slice(t, t + LANE)
            lanes_b = pl.ds(pl.multiple_of(c * pairs, LANE) + t, LANE)
            for u in range(t // SUB, (t + LANE) // SUB):
                row = (first + u) * MSG + 3 * SUB
                index[u * SUB : (u + 1) * SUB, :] = arrived[pl.ds(row, SUB), :].astype(jnp.int32)
            side_a[:, lanes] = turn(extras, gather[...], parts, 6, t)
            join_directions(side_a, remote_b, joined, lanes, lanes_b)
            turn_fields(
                lambda u, k: arrived[pl.ds((first + u) * MSG + SUB * k, SUB), :],
                lambda u, k: staged[
                    pl.ds(pl.multiple_of((first + u) * TARGET, SUB) + SUB * k, SUB), :
                ],
                lambda u: index[u * SUB : (u + 1) * SUB, :],
                same[...],
                parts,
                turned,
                t,
            )
            sums = point_sums(turned, joined, partial, t) * side_a[12:13, lanes]
            placed = lax.dot_general(
                jnp.concatenate(halves_of(sums), axis=0),
                place[...],
                (((0,), (0,)), ((), ())),
                preferred_element_type=f32,
            )
            hit = frags[lanes, :] == jnp.broadcast_to(slot, (LANE, LANE))
            for half in range(2):
                part = jnp.where(hit, placed[:, half * LANE : (half + 1) * LANE], 0.0)
                for piece in halves_of(part):
                    rows[half] = rows[half] + jnp.dot(
                        mine[:, lanes], piece, preferred_element_type=f32
                    )
            total = total + target_side(by_frag(sums, remote_frag[0:1, lanes_b]))
        for half in range(2):
            back[pl.ds(2 * first + half, peers, stride=2), :] = rows[half]
        return total

    totals[...] = lax.fori_loop(0, back.shape[0] // (2 * peers), block, local_totals[...])


def final_kernel(back, totals, gradient, hess, *, per_frag):
    devices = back.shape[0] // 2
    index = iota(0) * GROUP + lax.bitwise_and(iota(1), GROUP - 1)
    halves = []
    for half in range(2):
        tile = back[pl.ds(half, SUB, stride=2), :]
        for q in range(SUB, devices, SUB):
            tile = tile + back[pl.ds(2 * q + half, SUB, stride=2), :]
        halves.append(pick(jnp.sum(tile, axis=0, keepdims=True), index))
    total = jnp.where(iota(1) < GROUP, halves[0], halves[1]).T[0:18, :] + totals[...]
    gradient[...] = total[0:6, :] * (1.0 / LANE)
    for v in range(2):
        part = total[6 + 6 * v : 12 + 6 * v, :] * (1.0 / (LANE * per_frag))
        for j in range(6):
            hess[j, v : v + 1, :] = part[j : j + 1, :]


def call(kernel, outs, scratch, spaces, limit=VMEM_LIMIT, out_space="v", **more):
    kinds = {"v": pltpu.VMEM, "s": pltpu.SMEM, "h": pltpu.HBM}
    return pl.pallas_call(
        kernel,
        out_shape=outs,
        in_specs=[pl.BlockSpec(memory_space=kinds[s]) for s in spaces],
        out_specs=[pl.BlockSpec(memory_space=kinds[out_space])] * len(outs),
        scratch_shapes=scratch,
        compiler_params=pltpu.CompilerParams(vmem_limit_bytes=limit),
        **more,
    )


def in_hbm(values):
    return pltpu.with_memory_space_constraint(values, pltpu.HBM)


def exchange(rows, devices):
    sent = rows.reshape(devices, 1, -1)
    sent = lax.all_to_all(sent, ORDER, split_axis=0, concat_axis=0, tiled=True)
    return sent.reshape(rows.shape)


def local(
    points, normals, poses, directions, local_pairs, local_maps,
    remote_src, remote_maps, remote_dst, counts,
):
    sizes = lax.axis_size("tile"), lax.axis_size("band")
    devices = sizes[0] * sizes[1]
    blocks, _, count = points.shape
    frags = poses.shape[1]
    slots = remote_src.shape[1]
    pairs = local_pairs.shape[1]
    assert count == LANE and frags == SUB and slots == devices * SUB and devices % PEERS == 0
    per_frag = blocks // frags
    stride = blocks + SUB
    f32 = jnp.float32
    points = points.transpose(1, 0, 2)
    normals = normals.transpose(1, 0, 2)
    directions = directions.transpose(1, 0, 2)

    def array(*shape, dtype=f32):
        return jax.ShapeDtypeStruct(shape, dtype)

    def vmem(*shape, dtype=f32):
        return pltpu.VMEM(shape, dtype)

    i32, bf16 = jnp.int32, jnp.bfloat16
    part = PEERS * SUB
    (message,) = call(
        functools.partial(pack_kernel, sizes=sizes),
        [array(devices * MSG, LANE)],
        [
            vmem(3, blocks, LANE),
            pltpu.SMEM((6, frags), f32),
            vmem(6, 2, frags),
            pltpu.SMEM((1, slots), i32),
            vmem(1, slots, dtype=i32),
            vmem(slots, LANE, dtype=i32),
            vmem(1, devices, dtype=i32),
            vmem(3 * stride, LANE),
            vmem(12 * frags * SUB, LANE),
            vmem(2 * SUB, LANE),
            vmem(devices * MSG, LANE),
            pltpu.SemaphoreType.DMA((9,)),
            pltpu.SemaphoreType.DMA((devices // SUB,)),
        ],
        "hhhhhh",
        limit=PACK_LIMIT,
        out_space="h",
    )(*[in_hbm(x) for x in (points, poses, directions, remote_src, remote_maps[0], counts)])
    arrived = exchange(message, devices)
    staged, remote_b, remote_frag, totals, same, gather, place, mine = call(
        functools.partial(local_kernel, sizes=sizes),
        [
            array(devices * TARGET, LANE),
            array(2 * SUB, slots),
            array(1, slots, dtype=i32),
            array(18, frags),
            array(LANE, 2 * LANE, dtype=bf16),
            array(GROUP, 2 * LANE, dtype=bf16),
            array(2 * ROWS, 2 * LANE, dtype=bf16),
            array(PEERS, part, dtype=bf16),
        ],
        [
            vmem(6 * stride, LANE),
            vmem(12 * frags * SUB, LANE),
            vmem(2 * SUB, LANE),
            vmem(pairs // SUB * SOURCE, LANE),
            vmem(pairs // SUB * TARGET, LANE),
            vmem(2 * SUB, pairs),
            vmem(2 * SUB, pairs),
            vmem(3 * SUB, pairs),
            vmem(pairs, 6 * 2 * LANE, dtype=bf16),
            vmem(9 * LANE, pairs),
            vmem(pairs // LANE * ROWS * SUB, LANE),
        ],
        "vvsvsvvsv",
        cost_estimate=pl.CostEstimate(
            flops=200 * pairs * LANE, bytes_accessed=4_000_000, transcendentals=0
        ),
    )(
        points, normals, poses, directions, local_pairs, local_pairs, local_maps,
        remote_dst, remote_dst,
    )
    back, totals = call(
        remote_kernel,
        [array(devices * 2, LANE), array(18, frags)],
        [
            vmem(2 * SUB, part),
            vmem(3 * SUB, part),
            vmem(part, LANE),
            vmem(part, LANE, dtype=i32),
            vmem(part, 7 * 2 * LANE, dtype=bf16),
            vmem(9 * LANE, part),
            vmem(part // LANE * ROWS * SUB, LANE),
        ],
        "vvvvvvvvv",
    )(arrived, staged, remote_b, remote_frag, totals, same, gather, place, mine)
    back = exchange(back, devices)
    gradient, hess = call(
        functools.partial(final_kernel, per_frag=per_frag),
        [array(6, frags), array(6, 2, frags)],
        [],
        "vv",
    )(back, totals)
    return (gradient, hess.transpose(1, 0, 2))


def solution(mesh):
    placed = (
        P(AXES, None, None),
        P(AXES, None, None),
        P(None, AXES),
        P(None, None, AXES),
        P(None, AXES),
        P(AXES, None),
        P(AXES, None),
        P(AXES, None, None),
        P(AXES, None),
        P(AXES, None),
    )
    return jax.shard_map(
        local,
        mesh=mesh,
        in_specs=placed,
        out_specs=(P(None, AXES), P(None, None, AXES)),
        check_vma=False,
    )
```

```python
import functools

import jax
import jax.numpy as jnp
from jax import lax
from jax.experimental import pallas as pl
from jax.experimental.pallas import tpu as pltpu
from jax.sharding import PartitionSpec as P

AXES = ("tile", "band")
ORDER = ("band", "tile")
SUB = 8
LANE = 128
MSG = 4 * SUB + 1
TARGET = 6 * SUB
SOURCE = 3 * SUB
ROWS = 32
GROUP = 16
VMEM_LIMIT = 16 * 1024 * 1024
PACK_LIMIT = 56 * 1024 * 1024
PEERS = 32


def iota(axis):
    return lax.broadcasted_iota(jnp.int32, (SUB, LANE), axis)


def pick(values, index):
    values = jnp.broadcast_to(values, (SUB, LANE))
    return jnp.take_along_axis(values, index, axis=1, mode="promise_in_bounds")


def shift_of(size):
    shift = size.bit_length() - 1
    assert 1 << shift == size
    return shift


def cross(left, right):
    return [
        left[1] * right[2] - left[2] * right[1],
        left[2] * right[0] - left[0] * right[2],
        left[0] * right[1] - left[1] * right[0],
    ]


def dot3(left, right):
    return left[0] * right[0] + left[1] * right[1] + left[2] * right[2]


def splat_rotation(poses, f):
    half = [jnp.full((SUB, LANE), poses[i, f] * 0.5, jnp.float32) for i in range(3)]
    w = 1.0 / jnp.sqrt(1.0 + half[0] * half[0] + half[1] * half[1] + half[2] * half[2])
    x, y, z = half[0] * w, half[1] * w, half[2] * w
    rotation = [
        [1.0 - 2.0 * (y * y + z * z), 2.0 * (x * y - w * z), 2.0 * (x * z + w * y)],
        [2.0 * (x * y + w * z), 1.0 - 2.0 * (x * x + z * z), 2.0 * (y * z - w * x)],
        [2.0 * (x * z - w * y), 2.0 * (y * z + w * x), 1.0 - 2.0 * (x * x + y * y)],
    ]
    return rotation, [jnp.full((SUB, LANE), poses[i, f], jnp.float32) for i in range(3, 6)]


def write_rotations(poses, turns):
    for f in range(poses.shape[1]):
        rotation, move = splat_rotation(poses, f)
        for i, tile in enumerate(rotation[0] + rotation[1] + rotation[2] + move):
            at = (12 * f + i) * SUB
            turns[at : at + SUB, :] = tile


def write_world(fields, turns, world, frags):
    blocks = fields[0].shape[1]
    total = turns.shape[0] // (12 * SUB)
    per_frag, stride = blocks // total, blocks + SUB
    for f in frags:
        tile = [turns[(12 * f + i) * SUB : (12 * f + i + 1) * SUB, :] for i in range(12)]
        for b in range(f * per_frag, (f + 1) * per_frag, SUB):
            for at, field in enumerate(fields):
                x = [field[j, b : b + SUB, :] for j in range(3)]
                for i in range(3):
                    row = dot3(tile[3 * i : 3 * i + 3], x)
                    if at == 0:
                        row = row + tile[9 + i]
                    world[pl.ds((3 * at + i) * stride + b, SUB), :] = row


def write_directions(directions, table):
    frags = directions.shape[2]
    for v in range(2):
        for j in range(6):
            table[6 * v + j : 6 * v + j + 1, 0:frags] = directions[j, v : v + 1, :]


def peer_at(place, sizes):
    n_tile, n_band = sizes
    tile = lax.bitwise_and(place, n_tile - 1)
    return tile * n_band + lax.shift_right_logical(place, shift_of(n_tile))


def entries(row_ref, index):
    out = jnp.zeros((SUB, LANE), row_ref.dtype)
    tile = lax.shift_right_logical(index, shift_of(LANE))
    for t in range(row_ref.shape[1] // LANE):
        hit = pick(row_ref[0:1, t * LANE : (t + 1) * LANE], lax.bitwise_and(index, LANE - 1))
        out = jnp.where(tile == t, hit, out)
    return out


def pack_kernel(
    points_h, poses_h, directions_h, src_h, maps_h, counts_h, out_h,
    points, poses, directions, src_s, src_v, maps, used, world, turns, table, out, sems, out_sems, *, sizes,
):
    devices = counts_h.shape[1]
    per_frag = points.shape[1] // poses.shape[1]
    stride = points.shape[1] + SUB
    frags = poses.shape[1]
    pairs = [(directions_h, directions), (src_h, src_v), (counts_h, used), (poses_h, poses)]
    pairs += [(points_h.at[j], points.at[j]) for j in range(3)]
    pairs += [(src_h, src_s), (maps_h, maps)]
    copies = [pltpu.make_async_copy(a, b, sems.at[i]) for i, (a, b) in enumerate(pairs)]
    for copy in copies:
        copy.start()
    for copy in copies[0:3]:
        copy.wait()
    write_directions(directions, table)
    limits = jnp.broadcast_to(used[0:1, :], (SUB, devices)).astype(jnp.float32)
    peers = lax.broadcasted_iota(jnp.int32, (SUB, devices), 1)
    row = lax.broadcasted_iota(jnp.int32, (SUB, devices), 0)
    slot = lax.shift_right_logical(iota(1), shift_of(GROUP))
    field = lax.bitwise_and(iota(1), GROUP - 1)
    for q in range(0, devices, SUB):
        block = entries(src_v, peer_at(iota(0) + q, sizes) * SUB + slot)
        frag = lax.shift_right_logical(block, shift_of(per_frag))
        hit = peers == peer_at(row + q, sizes)
        limit = jnp.sum(jnp.where(hit, limits, 0.0), axis=1, keepdims=True)
        extras = jnp.where(slot.astype(jnp.float32) < limit, 1.0, 0.0)
        for j in range(12):
            extras = jnp.where(field == j, pick(table[j : j + 1, :], frag), extras)
        extras = jnp.where(field == 13, frag.astype(jnp.float32), extras)
        out[pl.ds(q * MSG + MSG - 1, SUB, stride=MSG), :] = extras
    copies[3].wait()
    write_rotations(poses, turns)
    for copy in copies[4:7]:
        copy.wait()
    write_world([points], turns, world, range(frags))
    for copy in copies[7:]:
        copy.wait()

    def peer(q):
        p = peer_at(q, sizes)
        for s in range(SUB):
            block = src_s[0, p * SUB + s]
            out[pl.ds(q * MSG + s, 3, stride=SUB), :] = world[pl.ds(block, 3, stride=stride), :]
        rows = maps[pl.ds(pl.multiple_of(p * SUB, SUB), SUB), :]
        out[pl.ds(q * MSG + 3 * SUB, SUB), :] = rows.astype(jnp.float32)

    def piece(i):
        rows = pl.ds(pl.multiple_of(i * SUB * MSG, SUB), SUB * MSG)
        return pltpu.make_async_copy(out.at[rows], out_h.at[rows], out_sems.at[i])

    def pack(i, carry):
        for u in range(SUB):
            peer(i * SUB + u)
        piece(i).start()
        return carry

    lax.fori_loop(0, devices // SUB, pack, 0)
    for i in range(devices // SUB):
        piece(i).wait()


def halves_of(values):
    high = values.astype(jnp.bfloat16)
    return high, (values - high.astype(jnp.float32)).astype(jnp.bfloat16)


def turn_steps(at, left, parts, i, t, put):
    first, second = i * 2 * LANE, i * 2 * LANE + LANE

    def split(u):
        high, low = halves_of(jnp.concatenate([at(u), at(u + 1)], axis=0))
        parts[u * SUB : (u + 2) * SUB, first : first + LANE] = high
        parts[u * SUB : (u + 2) * SUB, second : second + LANE] = low

    def multiply():
        put(
            lax.dot_general(
                left,
                parts[t : t + LANE, first : second + LANE],
                (((1,), (1,)), ((), ())),
                preferred_element_type=jnp.float32,
            )
        )

    tiles = range(t // SUB, (t + LANE) // SUB, 2)
    return [functools.partial(split, u) for u in tiles] + [multiply]


def field_steps(source, target, index, same, parts, turned, t):
    def put(k, value):
        turned[k * LANE : (k + 1) * LANE, t : t + LANE] = value

    def turn_source(k):
        tiles = [source(u, k) for u in range(t // SUB, (t + LANE) // SUB)]
        put(6 + k, jnp.concatenate(tiles, axis=0).T)

    steps = []
    for k in range(6):

        def at(u, k=k):
            return pick(target(u, k), index(u))

        steps += turn_steps(at, same, parts, k, t, functools.partial(put, k))
    return steps + [functools.partial(turn_source, k) for k in range(3)]


def run(steps):
    for step in steps:
        step()


def join_directions(side_a, side_b, joined, lanes, lanes_b):
    joined[0:12, lanes] = side_a[0:12, lanes]
    for v in range(2):
        turn_rows, move_rows = slice(6 * v, 6 * v + 3), slice(6 * v + 3, 6 * v + 6)
        joined[move_rows, lanes] = side_a[move_rows, lanes] - side_b[move_rows, lanes_b]
        joined[12 + 3 * v : 15 + 3 * v, lanes] = side_b[turn_rows, lanes_b]


def point_sums(turned, joined, partial, t, between=()):
    lanes = slice(t, t + LANE)
    first = t // LANE * ROWS * SUB
    zero = jnp.zeros((SUB, LANE), jnp.float32)
    totals = [zero] * 27
    rounds = LANE // SUB
    for i in range(rounds):
        field = [turned[i * SUB + k * LANE : (i + 1) * SUB + k * LANE, lanes] for k in range(9)]
        way = [joined[j : j + 1, lanes] for j in range(18)]
        y, n, x = field[0:3], field[3:6], field[6:9]
        p, q = cross(x, n), cross(y, n)
        scalars = [dot3(n, [x[k] - y[k] for k in range(3)])]
        for v in range(2):
            a, b = way[6 * v : 6 * v + 6], way[12 + 3 * v : 15 + 3 * v]
            scalars.append(dot3(p, a[0:3]) + dot3(n, a[3:6]) - dot3(q, b))
        terms = []
        for s in scalars:
            terms += [s * value for value in p + n]
        for s in scalars:
            terms += [s * value for value in q]
        totals = [total + term for total, term in zip(totals, terms)]
        run(between[i * len(between) // rounds : (i + 1) * len(between) // rounds])
    for j in range(ROWS):
        partial[first + j * SUB : first + (j + 1) * SUB, :] = totals[j] if j < 27 else zero
    total = partial[pl.ds(first, ROWS, stride=SUB), :]
    for s in range(1, SUB):
        total = total + partial[pl.ds(first + s, ROWS, stride=SUB), :]
    return total


def frag_of(row, per_frag):
    return lax.shift_right_logical(row, shift_of(per_frag))


def look_up(table, frag, out):
    for at in range(0, frag.shape[1], LANE):
        index = jnp.broadcast_to(frag[:, at : at + LANE], (SUB, LANE))
        for j in range(0, 2 * SUB, SUB):
            out[j : j + SUB, at : at + LANE] = pick(table[j : j + SUB, :], index)


def by_frag(sums, frag):
    pairs = sums.shape[1]
    hot = jnp.broadcast_to(frag, (SUB, pairs)) == lax.broadcasted_iota(jnp.int32, (SUB, pairs), 0)
    return lax.dot_general(
        sums,
        hot.astype(jnp.float32),
        (((1,), (1,)), ((), ())),
        precision=lax.Precision.HIGHEST,
        preferred_element_type=jnp.float32,
    )


def target_side(total):
    rows = []
    for k in range(3):
        rows += [total[18 + 3 * k : 21 + 3 * k, :], total[6 * k + 3 : 6 * k + 6, :]]
    return -jnp.concatenate(rows, axis=0)


def constants(same, gather, place, mine):
    def wide(ref, axis):
        return lax.broadcasted_iota(jnp.int32, ref.shape, axis)

    def put(ref, hit):
        ref[...] = hit.astype(jnp.float32).astype(jnp.bfloat16)

    put(same, lax.bitwise_and(wide(same, 1), LANE - 1) == wide(same, 0))
    put(gather, lax.bitwise_and(wide(gather, 1), GROUP - 1) == wide(gather, 0))
    entry = lax.bitwise_and(wide(place, 1), GROUP - 1) + GROUP * lax.shift_right_logical(
        wide(place, 1), shift_of(LANE)
    )
    put(place, lax.bitwise_and(wide(place, 0), ROWS - 1) == entry)
    put(mine, lax.shift_right_logical(wide(mine, 1), shift_of(SUB)) == wide(mine, 0))


def local_kernel(
    points, normals, poses, directions, pairs_s, pairs_v, maps, dst_s, dst_v,
    staged, remote_b, remote_frag, totals, same, gather, place, mine,
    world, turns, table, sources, targets, side_a, side_b, joined, parts, turned, partial, *, sizes,
):
    per_frag = points.shape[1] // poses.shape[1]
    stride = points.shape[1] + SUB
    constants(same, gather, place, mine)
    table[...] = jnp.zeros_like(table)
    write_directions(directions, table)
    for at in range(0, dst_v.shape[1], LANE):
        flat = iota(1) + at
        peer = peer_at(lax.shift_right_logical(flat, shift_of(SUB)), sizes)
        block = entries(dst_v, peer * SUB + lax.bitwise_and(flat, SUB - 1))
        remote_frag[0:1, at : at + LANE] = frag_of(block, per_frag)[0:1, :]
    look_up(table, remote_frag[...], remote_b)
    frag_a, frag_b = frag_of(pairs_v[0:1, :], per_frag), frag_of(pairs_v[1:2, :], per_frag)
    look_up(table, frag_a, side_a)
    look_up(table, frag_b, side_b)
    every = slice(0, pairs_s.shape[1])
    join_directions(side_a, side_b, joined, every, every)
    write_rotations(poses, turns)
    write_world([points, normals], turns, world, range(poses.shape[1]))

    def stage_remote(g, carry):
        for s in range(SUB):
            block = dst_s[0, peer_at(g, sizes) * SUB + s]
            staged[pl.ds(g * TARGET + s, 6, stride=SUB), :] = world[pl.ds(block, 6, stride=stride), :]
        return carry

    lax.fori_loop(0, dst_s.shape[1] // SUB, stage_remote, 0, unroll=4)

    def stage_local(g, carry):
        for s in range(SUB):
            a, b = pairs_s[0, g * SUB + s], pairs_s[1, g * SUB + s]
            targets[pl.ds(g * TARGET + s, 6, stride=SUB), :] = world[pl.ds(b, 6, stride=stride), :]
            sources[pl.ds(g * SOURCE + s, 3, stride=SUB), :] = world[pl.ds(a, 3, stride=stride), :]
        return carry

    lax.fori_loop(0, pairs_s.shape[1] // SUB, stage_local, 0, unroll=4)
    total = jnp.zeros(totals.shape, jnp.float32)
    tiles = range(0, pairs_s.shape[1], LANE)
    steps = [
        field_steps(
            lambda u, k: sources[u * SOURCE + k * SUB : u * SOURCE + (k + 1) * SUB, :],
            lambda u, k: targets[u * TARGET + k * SUB : u * TARGET + (k + 1) * SUB, :],
            lambda u: maps[u * SUB : (u + 1) * SUB, :],
            same[...],
            parts,
            turned,
            t,
        )
        for t in tiles
    ]
    run(steps[0])
    for i, t in enumerate(tiles):
        between = steps[i + 1] if i + 1 < len(steps) else ()
        sums = point_sums(turned, joined, partial, t, between)
        total = total + by_frag(sums, frag_a[:, t : t + LANE])[0:18, :]
        total = total + target_side(by_frag(sums, frag_b[:, t : t + LANE]))
    totals[...] = total


def remote_kernel(
    arrived, staged, remote_b, remote_frag, local_totals, same, gather, place, mine,
    back, totals, side_a, joined, frags, index, parts, turned, partial,
):
    f32 = jnp.float32
    pairs = parts.shape[0]
    peers = pairs // SUB
    own = lax.shift_right_logical(iota(1), shift_of(GROUP)) == iota(0)
    slot = lax.shift_right_logical(iota(1), shift_of(GROUP)).astype(f32)[0:1, :]

    def block(c, total):
        first = c * peers
        start = c * pairs if isinstance(c, int) else pl.multiple_of(c * pairs, LANE)

        def row_at(u, size, row):
            at = (first + u) * size + row
            return at if isinstance(c, int) or size == MSG else pl.multiple_of(at, SUB)

        def extras(u):
            row = arrived[pl.ds(row_at(u, MSG, 4 * SUB), 1), :]
            frags[u * SUB : (u + 1) * SUB, :] = pick(row, iota(0) * GROUP + 13)
            return jnp.where(own, jnp.broadcast_to(row, (SUB, LANE)), 0.0)

        def front(t):
            lanes = slice(t, t + LANE)

            def indices():
                for u in range(t // SUB, (t + LANE) // SUB):
                    rows = arrived[pl.ds(row_at(u, MSG, 3 * SUB), SUB), :]
                    index[u * SUB : (u + 1) * SUB, :] = rows.astype(jnp.int32)

            def put(value):
                side_a[:, lanes] = value
                join_directions(side_a, remote_b, joined, lanes, pl.ds(start + t, LANE))

            return (
                [indices]
                + turn_steps(extras, gather[...], parts, 6, t, put)
                + field_steps(
                    lambda u, k: arrived[pl.ds(row_at(u, MSG, SUB * k), SUB), :],
                    lambda u, k: staged[pl.ds(row_at(u, TARGET, SUB * k), SUB), :],
                    lambda u: index[u * SUB : (u + 1) * SUB, :],
                    same[...],
                    parts,
                    turned,
                    t,
                )
            )

        rows = [jnp.zeros((peers, LANE), f32) for half in range(2)]

        def back_steps(sums, t):
            lanes = slice(t, t + LANE)
            held = {}

            def scatter():
                held["placed"] = lax.dot_general(
                    jnp.concatenate(halves_of(sums), axis=0),
                    place[...],
                    (((0,), (0,)), ((), ())),
                    preferred_element_type=f32,
                )

            def add(half):
                hit = frags[lanes, :] == jnp.broadcast_to(slot, (LANE, LANE))
                part = jnp.where(hit, held["placed"][:, half * LANE : (half + 1) * LANE], 0.0)
                for piece in halves_of(part):
                    rows[half] = rows[half] + jnp.dot(
                        mine[:, lanes], piece, preferred_element_type=f32
                    )

            def own_side():
                frag = remote_frag[0:1, pl.ds(start + t, LANE)]
                held["total"] = target_side(by_frag(sums, frag))

            return [scatter, functools.partial(add, 0), functools.partial(add, 1), own_side], held

        tiles = range(0, pairs, LANE)
        steps = front(tiles[0])
        run(steps)
        behind, held = [], []
        for t in tiles:
            between = behind + (front(t + LANE) if t + LANE < pairs else [])
            sums = point_sums(turned, joined, partial, t, between)
            sums = sums * side_a[12:13, t : t + LANE]
            behind, kept = back_steps(sums, t)
            held.append(kept)
        run(behind)
        for kept in held:
            total = total + kept["total"]
        for half in range(2):
            back[pl.ds(2 * first + half, peers, stride=2), :] = rows[half]
        return total

    blocks = back.shape[0] // (2 * peers)
    total = local_totals[...]
    totals[...] = block(0, total) if blocks == 1 else lax.fori_loop(0, blocks, block, total)


def final_kernel(back, totals, gradient, hess, *, per_frag):
    devices = back.shape[0] // 2
    index = iota(0) * GROUP + lax.bitwise_and(iota(1), GROUP - 1)
    halves = []
    for half in range(2):
        tile = back[pl.ds(half, SUB, stride=2), :]
        for q in range(SUB, devices, SUB):
            tile = tile + back[pl.ds(2 * q + half, SUB, stride=2), :]
        halves.append(pick(jnp.sum(tile, axis=0, keepdims=True), index))
    total = jnp.where(iota(1) < GROUP, halves[0], halves[1]).T[0:18, :] + totals[...]
    gradient[...] = total[0:6, :] * (1.0 / LANE)
    for v in range(2):
        part = total[6 + 6 * v : 12 + 6 * v, :] * (1.0 / (LANE * per_frag))
        for j in range(6):
            hess[j, v : v + 1, :] = part[j : j + 1, :]


def call(kernel, outs, scratch, spaces, limit=VMEM_LIMIT, out_space="v", **more):
    kinds = {"v": pltpu.VMEM, "s": pltpu.SMEM, "h": pltpu.HBM}
    return pl.pallas_call(
        kernel,
        out_shape=outs,
        in_specs=[pl.BlockSpec(memory_space=kinds[s]) for s in spaces],
        out_specs=[pl.BlockSpec(memory_space=kinds[out_space])] * len(outs),
        scratch_shapes=scratch,
        compiler_params=pltpu.CompilerParams(vmem_limit_bytes=limit),
        **more,
    )


def in_hbm(values):
    return pltpu.with_memory_space_constraint(values, pltpu.HBM)


def exchange(rows, devices):
    sent = rows.reshape(devices, 1, -1)
    sent = lax.all_to_all(sent, ORDER, split_axis=0, concat_axis=0, tiled=True)
    return sent.reshape(rows.shape)


def local(
    points, normals, poses, directions, local_pairs, local_maps,
    remote_src, remote_maps, remote_dst, counts,
):
    sizes = lax.axis_size("tile"), lax.axis_size("band")
    devices = sizes[0] * sizes[1]
    blocks, _, count = points.shape
    frags = poses.shape[1]
    slots = remote_src.shape[1]
    pairs = local_pairs.shape[1]
    assert count == LANE and frags == SUB and slots == devices * SUB and devices % PEERS == 0
    per_frag = blocks // frags
    stride = blocks + SUB
    f32 = jnp.float32
    points = points.transpose(1, 0, 2)
    normals = normals.transpose(1, 0, 2)
    directions = directions.transpose(1, 0, 2)

    def array(*shape, dtype=f32):
        return jax.ShapeDtypeStruct(shape, dtype)

    def vmem(*shape, dtype=f32):
        return pltpu.VMEM(shape, dtype)

    i32, bf16 = jnp.int32, jnp.bfloat16
    part = PEERS * SUB
    (message,) = call(
        functools.partial(pack_kernel, sizes=sizes),
        [array(devices * MSG, LANE)],
        [
            vmem(3, blocks, LANE),
            pltpu.SMEM((6, frags), f32),
            vmem(6, 2, frags),
            pltpu.SMEM((1, slots), i32),
            vmem(1, slots, dtype=i32),
            vmem(slots, LANE, dtype=i32),
            vmem(1, devices, dtype=i32),
            vmem(3 * stride, LANE),
            vmem(12 * frags * SUB, LANE),
            vmem(2 * SUB, LANE),
            vmem(devices * MSG, LANE),
            pltpu.SemaphoreType.DMA((9,)),
            pltpu.SemaphoreType.DMA((devices // SUB,)),
        ],
        "hhhhhh",
        limit=PACK_LIMIT,
        out_space="h",
    )(*[in_hbm(x) for x in (points, poses, directions, remote_src, remote_maps[0], counts)])
    arrived = exchange(message, devices)
    staged, remote_b, remote_frag, totals, same, gather, place, mine = call(
        functools.partial(local_kernel, sizes=sizes),
        [
            array(devices * TARGET, LANE),
            array(2 * SUB, slots),
            array(1, slots, dtype=i32),
            array(18, frags),
            array(LANE, 2 * LANE, dtype=bf16),
            array(GROUP, 2 * LANE, dtype=bf16),
            array(2 * ROWS, 2 * LANE, dtype=bf16),
            array(PEERS, part, dtype=bf16),
        ],
        [
            vmem(6 * stride, LANE),
            vmem(12 * frags * SUB, LANE),
            vmem(2 * SUB, LANE),
            vmem(pairs // SUB * SOURCE, LANE),
            vmem(pairs // SUB * TARGET, LANE),
            vmem(2 * SUB, pairs),
            vmem(2 * SUB, pairs),
            vmem(3 * SUB, pairs),
            vmem(pairs, 6 * 2 * LANE, dtype=bf16),
            vmem(9 * LANE, pairs),
            vmem(pairs // LANE * ROWS * SUB, LANE),
        ],
        "vvsvsvvsv",
        cost_estimate=pl.CostEstimate(
            flops=200 * pairs * LANE, bytes_accessed=4_000_000, transcendentals=0
        ),
    )(
        points, normals, poses, directions, local_pairs, local_pairs, local_maps,
        remote_dst, remote_dst,
    )
    back, totals = call(
        remote_kernel,
        [array(devices * 2, LANE), array(18, frags)],
        [
            vmem(2 * SUB, part),
            vmem(3 * SUB, part),
            vmem(part, LANE),
            vmem(part, LANE, dtype=i32),
            vmem(part, 7 * 2 * LANE, dtype=bf16),
            vmem(9 * LANE, part),
            vmem(part // LANE * ROWS * SUB, LANE),
        ],
        "vvvvvvvvv",
    )(arrived, staged, remote_b, remote_frag, totals, same, gather, place, mine)
    back = exchange(back, devices)
    gradient, hess = call(
        functools.partial(final_kernel, per_frag=per_frag),
        [array(6, frags), array(6, 2, frags)],
        [],
        "vv",
    )(back, totals)
    return (gradient, hess.transpose(1, 0, 2))


def solution(mesh):
    placed = (
        P(AXES, None, None),
        P(AXES, None, None),
        P(None, AXES),
        P(None, None, AXES),
        P(None, AXES),
        P(AXES, None),
        P(AXES, None),
        P(AXES, None, None),
        P(AXES, None),
        P(AXES, None),
    )
    return jax.shard_map(
        local,
        mesh=mesh,
        in_specs=placed,
        out_specs=(P(None, AXES), P(None, None, AXES)),
        check_vma=False,
    )
```

```python
import functools

import jax
import jax.numpy as jnp
from jax import lax
from jax.experimental import pallas as pl
from jax.experimental.pallas import tpu as pltpu
from jax.sharding import PartitionSpec as P

AXES = ("tile", "band")
ORDER = ("band", "tile")
SUB = 8
LANE = 128
MSG = 4 * SUB + 1
TARGET = 6 * SUB
SOURCE = 3 * SUB
ROWS = 32
GROUP = 16
VMEM_LIMIT = 16 * 1024 * 1024
PACK_LIMIT = 56 * 1024 * 1024
PEERS = 32


def iota(axis):
    return lax.broadcasted_iota(jnp.int32, (SUB, LANE), axis)


def pick(values, index):
    values = jnp.broadcast_to(values, (SUB, LANE))
    return jnp.take_along_axis(values, index, axis=1, mode="promise_in_bounds")


def shift_of(size):
    shift = size.bit_length() - 1
    assert 1 << shift == size
    return shift


def cross(left, right):
    return [
        left[1] * right[2] - left[2] * right[1],
        left[2] * right[0] - left[0] * right[2],
        left[0] * right[1] - left[1] * right[0],
    ]


def dot3(left, right):
    return left[0] * right[0] + left[1] * right[1] + left[2] * right[2]


def splat_rotation(poses, f):
    half = [jnp.full((SUB, LANE), poses[i, f] * 0.5, jnp.float32) for i in range(3)]
    w = 1.0 / jnp.sqrt(1.0 + half[0] * half[0] + half[1] * half[1] + half[2] * half[2])
    x, y, z = half[0] * w, half[1] * w, half[2] * w
    rotation = [
        [1.0 - 2.0 * (y * y + z * z), 2.0 * (x * y - w * z), 2.0 * (x * z + w * y)],
        [2.0 * (x * y + w * z), 1.0 - 2.0 * (x * x + z * z), 2.0 * (y * z - w * x)],
        [2.0 * (x * z - w * y), 2.0 * (y * z + w * x), 1.0 - 2.0 * (x * x + y * y)],
    ]
    return rotation, [jnp.full((SUB, LANE), poses[i, f], jnp.float32) for i in range(3, 6)]


def write_rotations(poses, turns):
    for f in range(poses.shape[1]):
        rotation, move = splat_rotation(poses, f)
        for i, tile in enumerate(rotation[0] + rotation[1] + rotation[2] + move):
            at = (12 * f + i) * SUB
            turns[at : at + SUB, :] = tile


def write_world(fields, turns, world, frags):
    blocks = fields[0].shape[1]
    total = turns.shape[0] // (12 * SUB)
    per_frag, stride = blocks // total, blocks + SUB
    for f in frags:
        tile = [turns[(12 * f + i) * SUB : (12 * f + i + 1) * SUB, :] for i in range(12)]
        for b in range(f * per_frag, (f + 1) * per_frag, SUB):
            for at, field in enumerate(fields):
                x = [field[j, b : b + SUB, :] for j in range(3)]
                for i in range(3):
                    row = dot3(tile[3 * i : 3 * i + 3], x)
                    if at == 0:
                        row = row + tile[9 + i]
                    world[pl.ds((3 * at + i) * stride + b, SUB), :] = row


def write_directions(directions, table):
    frags = directions.shape[2]
    for v in range(2):
        for j in range(6):
            table[6 * v + j : 6 * v + j + 1, 0:frags] = directions[j, v : v + 1, :]


def peer_at(place, sizes):
    n_tile, n_band = sizes
    if isinstance(place, int):
        return place % n_tile * n_band + place // n_tile
    tile = lax.bitwise_and(place, n_tile - 1)
    return tile * n_band + lax.shift_right_logical(place, shift_of(n_tile))


def entries(row_ref, index):
    out = jnp.zeros((SUB, LANE), row_ref.dtype)
    tile = lax.shift_right_logical(index, shift_of(LANE))
    for t in range(row_ref.shape[1] // LANE):
        hit = pick(row_ref[0:1, t * LANE : (t + 1) * LANE], lax.bitwise_and(index, LANE - 1))
        out = jnp.where(tile == t, hit, out)
    return out


def pack_kernel(
    points_h, poses_h, directions_h, src_h, maps_h, counts_h, out_h,
    points, poses, directions, src_s, src_v, maps, used, world, turns, table, out, sems, out_sems, *, sizes,
):
    devices = counts_h.shape[1]
    per_frag = points.shape[1] // poses.shape[1]
    stride = points.shape[1] + SUB
    frags = poses.shape[1]
    pairs = [(directions_h, directions), (src_h, src_v), (counts_h, used), (poses_h, poses)]
    pairs += [(points_h.at[j], points.at[j]) for j in range(3)]
    pairs += [(src_h, src_s), (maps_h, maps)]
    copies = [pltpu.make_async_copy(a, b, sems.at[i]) for i, (a, b) in enumerate(pairs)]
    for copy in copies:
        copy.start()
    for copy in copies[0:3]:
        copy.wait()
    write_directions(directions, table)
    limits = jnp.broadcast_to(used[0:1, :], (SUB, devices)).astype(jnp.float32)
    peers = lax.broadcasted_iota(jnp.int32, (SUB, devices), 1)
    row = lax.broadcasted_iota(jnp.int32, (SUB, devices), 0)
    slot = lax.shift_right_logical(iota(1), shift_of(GROUP))
    field = lax.bitwise_and(iota(1), GROUP - 1)
    for q in range(0, devices, SUB):
        block = entries(src_v, peer_at(iota(0) + q, sizes) * SUB + slot)
        frag = lax.shift_right_logical(block, shift_of(per_frag))
        hit = peers == peer_at(row + q, sizes)
        limit = jnp.sum(jnp.where(hit, limits, 0.0), axis=1, keepdims=True)
        extras = jnp.where(slot.astype(jnp.float32) < limit, 1.0, 0.0)
        for j in range(12):
            extras = jnp.where(field == j, pick(table[j : j + 1, :], frag), extras)
        extras = jnp.where(field == 13, frag.astype(jnp.float32), extras)
        out[pl.ds(q * MSG + MSG - 1, SUB, stride=MSG), :] = extras
    copies[3].wait()
    write_rotations(poses, turns)
    for copy in copies[4:7]:
        copy.wait()
    write_world([points], turns, world, range(frags))
    for copy in copies[7:]:
        copy.wait()

    def peer(q):
        p = peer_at(q, sizes)
        for s in range(SUB):
            block = src_s[0, p * SUB + s]
            out[pl.ds(q * MSG + s, 3, stride=SUB), :] = world[pl.ds(block, 3, stride=stride), :]
        rows = maps[p * SUB : (p + 1) * SUB, :]
        out[pl.ds(q * MSG + 3 * SUB, SUB), :] = rows.astype(jnp.float32)

    def piece(i):
        rows = pl.ds(i * SUB * MSG, SUB * MSG)
        return pltpu.make_async_copy(out.at[rows], out_h.at[rows], out_sems.at[i])

    for i in range(devices // SUB):
        for u in range(SUB):
            peer(i * SUB + u)
        piece(i).start()
    for i in range(devices // SUB):
        piece(i).wait()


def halves_of(values):
    high = values.astype(jnp.bfloat16)
    return high, (values - high.astype(jnp.float32)).astype(jnp.bfloat16)


def turn_steps(at, left, parts, i, t, put):
    first, second = i * 2 * LANE, i * 2 * LANE + LANE

    def split(u):
        high, low = halves_of(jnp.concatenate([at(u), at(u + 1)], axis=0))
        parts[u * SUB : (u + 2) * SUB, first : first + LANE] = high
        parts[u * SUB : (u + 2) * SUB, second : second + LANE] = low

    def multiply():
        put(
            lax.dot_general(
                left,
                parts[t : t + LANE, first : second + LANE],
                (((1,), (1,)), ((), ())),
                preferred_element_type=jnp.float32,
            )
        )

    tiles = range(t // SUB, (t + LANE) // SUB, 2)
    return [functools.partial(split, u) for u in tiles], multiply


def field_steps(source, target, index, same, parts, turned, t):
    def put(k, value):
        turned[k * LANE : (k + 1) * LANE, t : t + LANE] = value

    def turn_source(k):
        tiles = [source(u, k) for u in range(t // SUB, (t + LANE) // SUB)]
        put(6 + k, jnp.concatenate(tiles, axis=0).T)

    splits, products = [], []
    for k in range(6):

        def at(u, k=k):
            return pick(target(u, k), index(u))

        split, product = turn_steps(at, same, parts, k, t, functools.partial(put, k))
        splits.append(split)
        products.append(product)
    steps = [split[u] for u in range(len(splits[0])) for split in splits]
    return steps + products + [functools.partial(turn_source, k) for k in range(3)]


def run(steps):
    for step in steps:
        step()


def join_directions(side_a, side_b, joined, lanes, lanes_b):
    joined[0:12, lanes] = side_a[0:12, lanes]
    for v in range(2):
        turn_rows, move_rows = slice(6 * v, 6 * v + 3), slice(6 * v + 3, 6 * v + 6)
        joined[move_rows, lanes] = side_a[move_rows, lanes] - side_b[move_rows, lanes_b]
        joined[12 + 3 * v : 15 + 3 * v, lanes] = side_b[turn_rows, lanes_b]


def point_sums(turned, joined, partial, t, between=()):
    lanes = slice(t, t + LANE)
    first = t // LANE * ROWS * SUB
    zero = jnp.zeros((SUB, LANE), jnp.float32)
    totals = [zero] * 27
    rounds = LANE // SUB
    for i in range(rounds):
        field = [turned[i * SUB + k * LANE : (i + 1) * SUB + k * LANE, lanes] for k in range(9)]
        way = [joined[j : j + 1, lanes] for j in range(18)]
        y, n, x = field[0:3], field[3:6], field[6:9]
        p, q = cross(x, n), cross(y, n)
        scalars = [dot3(n, [x[k] - y[k] for k in range(3)])]
        for v in range(2):
            a, b = way[6 * v : 6 * v + 6], way[12 + 3 * v : 15 + 3 * v]
            scalars.append(dot3(p, a[0:3]) + dot3(n, a[3:6]) - dot3(q, b))
        terms = []
        for s in scalars:
            terms += [s * value for value in p + n]
        for s in scalars:
            terms += [s * value for value in q]
        totals = [total + term for total, term in zip(totals, terms)]
        run(between[i * len(between) // rounds : (i + 1) * len(between) // rounds])
    for j in range(ROWS):
        partial[first + j * SUB : first + (j + 1) * SUB, :] = totals[j] if j < 27 else zero
    total = partial[pl.ds(first, ROWS, stride=SUB), :]
    for s in range(1, SUB):
        total = total + partial[pl.ds(first + s, ROWS, stride=SUB), :]
    return total


def frag_of(row, per_frag):
    return lax.shift_right_logical(row, shift_of(per_frag))


def look_up(table, frag, out):
    for at in range(0, frag.shape[1], LANE):
        index = jnp.broadcast_to(frag[:, at : at + LANE], (SUB, LANE))
        for j in range(0, 2 * SUB, SUB):
            out[j : j + SUB, at : at + LANE] = pick(table[j : j + SUB, :], index)


def by_frag(sums, frag):
    pairs = sums.shape[1]
    hot = jnp.broadcast_to(frag, (SUB, pairs)) == lax.broadcasted_iota(jnp.int32, (SUB, pairs), 0)
    return lax.dot_general(
        sums,
        hot.astype(jnp.float32),
        (((1,), (1,)), ((), ())),
        precision=lax.Precision.HIGHEST,
        preferred_element_type=jnp.float32,
    )


def target_side(total):
    rows = []
    for k in range(3):
        rows += [total[18 + 3 * k : 21 + 3 * k, :], total[6 * k + 3 : 6 * k + 6, :]]
    return -jnp.concatenate(rows, axis=0)


def constants(same, gather, place, mine):
    def wide(ref, axis):
        return lax.broadcasted_iota(jnp.int32, ref.shape, axis)

    def put(ref, hit):
        ref[...] = hit.astype(jnp.float32).astype(jnp.bfloat16)

    put(same, lax.bitwise_and(wide(same, 1), LANE - 1) == wide(same, 0))
    put(gather, lax.bitwise_and(wide(gather, 1), GROUP - 1) == wide(gather, 0))
    entry = lax.bitwise_and(wide(place, 1), GROUP - 1) + GROUP * lax.shift_right_logical(
        wide(place, 1), shift_of(LANE)
    )
    put(place, lax.bitwise_and(wide(place, 0), ROWS - 1) == entry)
    put(mine, lax.shift_right_logical(wide(mine, 1), shift_of(SUB)) == wide(mine, 0))


def local_kernel(
    points, normals, poses, directions, pairs_s, pairs_v, maps, dst_s, dst_v,
    staged, remote_b, remote_frag, totals, same, gather, place, mine,
    world, turns, table, sources, targets, side_a, side_b, joined, parts, turned, partial, *, sizes,
):
    per_frag = points.shape[1] // poses.shape[1]
    stride = points.shape[1] + SUB
    constants(same, gather, place, mine)
    table[...] = jnp.zeros_like(table)
    write_directions(directions, table)
    for at in range(0, dst_v.shape[1], LANE):
        flat = iota(1) + at
        peer = peer_at(lax.shift_right_logical(flat, shift_of(SUB)), sizes)
        block = entries(dst_v, peer * SUB + lax.bitwise_and(flat, SUB - 1))
        remote_frag[0:1, at : at + LANE] = frag_of(block, per_frag)[0:1, :]
    look_up(table, remote_frag[...], remote_b)
    frag_a, frag_b = frag_of(pairs_v[0:1, :], per_frag), frag_of(pairs_v[1:2, :], per_frag)
    look_up(table, frag_a, side_a)
    look_up(table, frag_b, side_b)
    every = slice(0, pairs_s.shape[1])
    join_directions(side_a, side_b, joined, every, every)
    write_rotations(poses, turns)
    write_world([points, normals], turns, world, range(poses.shape[1]))

    def stage_remote(g, carry):
        for s in range(SUB):
            block = dst_s[0, peer_at(g, sizes) * SUB + s]
            staged[pl.ds(g * TARGET + s, 6, stride=SUB), :] = world[pl.ds(block, 6, stride=stride), :]
        return carry

    lax.fori_loop(0, dst_s.shape[1] // SUB, stage_remote, 0, unroll=4)

    def stage_local(g, carry):
        for s in range(SUB):
            a, b = pairs_s[0, g * SUB + s], pairs_s[1, g * SUB + s]
            targets[pl.ds(g * TARGET + s, 6, stride=SUB), :] = world[pl.ds(b, 6, stride=stride), :]
            sources[pl.ds(g * SOURCE + s, 3, stride=SUB), :] = world[pl.ds(a, 3, stride=stride), :]
        return carry

    lax.fori_loop(0, pairs_s.shape[1] // SUB, stage_local, 0, unroll=4)
    total = jnp.zeros(totals.shape, jnp.float32)
    tiles = range(0, pairs_s.shape[1], LANE)
    steps = [
        field_steps(
            lambda u, k: sources[u * SOURCE + k * SUB : u * SOURCE + (k + 1) * SUB, :],
            lambda u, k: targets[u * TARGET + k * SUB : u * TARGET + (k + 1) * SUB, :],
            lambda u: maps[u * SUB : (u + 1) * SUB, :],
            same[...],
            parts,
            turned,
            t,
        )
        for t in tiles
    ]
    run(steps[0])
    for i, t in enumerate(tiles):
        between = steps[i + 1] if i + 1 < len(steps) else ()
        sums = point_sums(turned, joined, partial, t, between)
        total = total + by_frag(sums, frag_a[:, t : t + LANE])[0:18, :]
        total = total + target_side(by_frag(sums, frag_b[:, t : t + LANE]))
    totals[...] = total


def remote_kernel(
    arrived, staged, remote_b, remote_frag, local_totals, same, gather, place, mine,
    back, totals, side_a, joined, frags, index, parts, turned, partial,
):
    f32 = jnp.float32
    pairs = parts.shape[0]
    peers = pairs // SUB
    own = lax.shift_right_logical(iota(1), shift_of(GROUP)) == iota(0)
    slot = lax.shift_right_logical(iota(1), shift_of(GROUP)).astype(f32)[0:1, :]

    def block(c, total):
        first = c * peers
        start = c * pairs if isinstance(c, int) else pl.multiple_of(c * pairs, LANE)

        def row_at(u, size, row):
            at = (first + u) * size + row
            return at if isinstance(c, int) or size == MSG else pl.multiple_of(at, SUB)

        def extras(u):
            row = arrived[pl.ds(row_at(u, MSG, 4 * SUB), 1), :]
            frags[u * SUB : (u + 1) * SUB, :] = pick(row, iota(0) * GROUP + 13)
            return jnp.where(own, jnp.broadcast_to(row, (SUB, LANE)), 0.0)

        def front(t):
            lanes = slice(t, t + LANE)

            def indices():
                for u in range(t // SUB, (t + LANE) // SUB):
                    rows = arrived[pl.ds(row_at(u, MSG, 3 * SUB), SUB), :]
                    index[u * SUB : (u + 1) * SUB, :] = rows.astype(jnp.int32)

            def put(value):
                side_a[:, lanes] = value
                join_directions(side_a, remote_b, joined, lanes, pl.ds(start + t, LANE))

            split, product = turn_steps(extras, gather[...], parts, 6, t, put)
            return (
                [indices]
                + split
                + [product]
                + field_steps(
                    lambda u, k: arrived[pl.ds(row_at(u, MSG, SUB * k), SUB), :],
                    lambda u, k: staged[pl.ds(row_at(u, TARGET, SUB * k), SUB), :],
                    lambda u: index[u * SUB : (u + 1) * SUB, :],
                    same[...],
                    parts,
                    turned,
                    t,
                )
            )

        rows = [jnp.zeros((peers, LANE), f32) for half in range(2)]

        def back_steps(sums, t):
            lanes = slice(t, t + LANE)
            held = {}

            def scatter():
                held["placed"] = lax.dot_general(
                    jnp.concatenate(halves_of(sums), axis=0),
                    place[...],
                    (((0,), (0,)), ((), ())),
                    preferred_element_type=f32,
                )

            def add(half):
                hit = frags[lanes, :] == jnp.broadcast_to(slot, (LANE, LANE))
                part = jnp.where(hit, held["placed"][:, half * LANE : (half + 1) * LANE], 0.0)
                for piece in halves_of(part):
                    rows[half] = rows[half] + jnp.dot(
                        mine[:, lanes], piece, preferred_element_type=f32
                    )

            def own_side():
                frag = remote_frag[0:1, pl.ds(start + t, LANE)]
                held["total"] = target_side(by_frag(sums, frag))

            return [scatter, functools.partial(add, 0), functools.partial(add, 1), own_side], held

        tiles = range(0, pairs, LANE)
        steps = front(tiles[0])
        run(steps)
        behind, held = [], []
        for t in tiles:
            between = behind + (front(t + LANE) if t + LANE < pairs else [])
            sums = point_sums(turned, joined, partial, t, between)
            sums = sums * side_a[12:13, t : t + LANE]
            behind, kept = back_steps(sums, t)
            held.append(kept)
        run(behind)
        for kept in held:
            total = total + kept["total"]
        for half in range(2):
            back[pl.ds(2 * first + half, peers, stride=2), :] = rows[half]
        return total

    blocks = back.shape[0] // (2 * peers)
    total = local_totals[...]
    totals[...] = block(0, total) if blocks == 1 else lax.fori_loop(0, blocks, block, total)


def final_kernel(back, totals, gradient, hess, *, per_frag):
    devices = back.shape[0] // 2
    index = iota(0) * GROUP + lax.bitwise_and(iota(1), GROUP - 1)
    halves = []
    for half in range(2):
        tile = back[pl.ds(half, SUB, stride=2), :]
        for q in range(SUB, devices, SUB):
            tile = tile + back[pl.ds(2 * q + half, SUB, stride=2), :]
        halves.append(pick(jnp.sum(tile, axis=0, keepdims=True), index))
    total = jnp.where(iota(1) < GROUP, halves[0], halves[1]).T[0:18, :] + totals[...]
    gradient[...] = total[0:6, :] * (1.0 / LANE)
    for v in range(2):
        part = total[6 + 6 * v : 12 + 6 * v, :] * (1.0 / (LANE * per_frag))
        for j in range(6):
            hess[j, v : v + 1, :] = part[j : j + 1, :]


def call(kernel, outs, scratch, spaces, limit=VMEM_LIMIT, out_space="v", **more):
    kinds = {"v": pltpu.VMEM, "s": pltpu.SMEM, "h": pltpu.HBM}
    return pl.pallas_call(
        kernel,
        out_shape=outs,
        in_specs=[pl.BlockSpec(memory_space=kinds[s]) for s in spaces],
        out_specs=[pl.BlockSpec(memory_space=kinds[out_space])] * len(outs),
        scratch_shapes=scratch,
        compiler_params=pltpu.CompilerParams(vmem_limit_bytes=limit),
        **more,
    )


def in_hbm(values):
    return pltpu.with_memory_space_constraint(values, pltpu.HBM)


def exchange(rows, devices):
    sent = rows.reshape(devices, 1, -1)
    sent = lax.all_to_all(sent, ORDER, split_axis=0, concat_axis=0, tiled=True)
    return sent.reshape(rows.shape)


def local(
    points, normals, poses, directions, local_pairs, local_maps,
    remote_src, remote_maps, remote_dst, counts,
):
    sizes = lax.axis_size("tile"), lax.axis_size("band")
    devices = sizes[0] * sizes[1]
    blocks, _, count = points.shape
    frags = poses.shape[1]
    slots = remote_src.shape[1]
    pairs = local_pairs.shape[1]
    assert count == LANE and frags == SUB and slots == devices * SUB and devices % PEERS == 0
    per_frag = blocks // frags
    stride = blocks + SUB
    f32 = jnp.float32
    points = points.transpose(1, 0, 2)
    normals = normals.transpose(1, 0, 2)
    directions = directions.transpose(1, 0, 2)

    def array(*shape, dtype=f32):
        return jax.ShapeDtypeStruct(shape, dtype)

    def vmem(*shape, dtype=f32):
        return pltpu.VMEM(shape, dtype)

    i32, bf16 = jnp.int32, jnp.bfloat16
    part = PEERS * SUB
    (message,) = call(
        functools.partial(pack_kernel, sizes=sizes),
        [array(devices * MSG, LANE)],
        [
            vmem(3, blocks, LANE),
            pltpu.SMEM((6, frags), f32),
            vmem(6, 2, frags),
            pltpu.SMEM((1, slots), i32),
            vmem(1, slots, dtype=i32),
            vmem(slots, LANE, dtype=i32),
            vmem(1, devices, dtype=i32),
            vmem(3 * stride, LANE),
            vmem(12 * frags * SUB, LANE),
            vmem(2 * SUB, LANE),
            vmem(devices * MSG, LANE),
            pltpu.SemaphoreType.DMA((9,)),
            pltpu.SemaphoreType.DMA((devices // SUB,)),
        ],
        "hhhhhh",
        limit=PACK_LIMIT,
        out_space="h",
    )(*[in_hbm(x) for x in (points, poses, directions, remote_src, remote_maps[0], counts)])
    arrived = exchange(message, devices)
    staged, remote_b, remote_frag, totals, same, gather, place, mine = call(
        functools.partial(local_kernel, sizes=sizes),
        [
            array(devices * TARGET, LANE),
            array(2 * SUB, slots),
            array(1, slots, dtype=i32),
            array(18, frags),
            array(LANE, 2 * LANE, dtype=bf16),
            array(GROUP, 2 * LANE, dtype=bf16),
            array(2 * ROWS, 2 * LANE, dtype=bf16),
            array(PEERS, part, dtype=bf16),
        ],
        [
            vmem(6 * stride, LANE),
            vmem(12 * frags * SUB, LANE),
            vmem(2 * SUB, LANE),
            vmem(pairs // SUB * SOURCE, LANE),
            vmem(pairs // SUB * TARGET, LANE),
            vmem(2 * SUB, pairs),
            vmem(2 * SUB, pairs),
            vmem(3 * SUB, pairs),
            vmem(pairs, 6 * 2 * LANE, dtype=bf16),
            vmem(9 * LANE, pairs),
            vmem(pairs // LANE * ROWS * SUB, LANE),
        ],
        "vvsvsvvsv",
        cost_estimate=pl.CostEstimate(
            flops=200 * pairs * LANE, bytes_accessed=4_000_000, transcendentals=0
        ),
    )(
        points, normals, poses, directions, local_pairs, local_pairs, local_maps,
        remote_dst, remote_dst,
    )
    back, totals = call(
        remote_kernel,
        [array(devices * 2, LANE), array(18, frags)],
        [
            vmem(2 * SUB, part),
            vmem(3 * SUB, part),
            vmem(part, LANE),
            vmem(part, LANE, dtype=i32),
            vmem(part, 7 * 2 * LANE, dtype=bf16),
            vmem(9 * LANE, part),
            vmem(part // LANE * ROWS * SUB, LANE),
        ],
        "vvvvvvvvv",
    )(arrived, staged, remote_b, remote_frag, totals, same, gather, place, mine)
    back = exchange(back, devices)
    gradient, hess = call(
        functools.partial(final_kernel, per_frag=per_frag),
        [array(6, frags), array(6, 2, frags)],
        [],
        "vv",
    )(back, totals)
    return (gradient, hess.transpose(1, 0, 2))


def solution(mesh):
    placed = (
        P(AXES, None, None),
        P(AXES, None, None),
        P(None, AXES),
        P(None, None, AXES),
        P(None, AXES),
        P(AXES, None),
        P(AXES, None),
        P(AXES, None, None),
        P(AXES, None),
        P(AXES, None),
    )
    return jax.shard_map(
        local,
        mesh=mesh,
        in_specs=placed,
        out_specs=(P(None, AXES), P(None, None, AXES)),
        check_vma=False,
    )
```

```python
import functools

import jax
import jax.numpy as jnp
from jax import lax
from jax.experimental import pallas as pl
from jax.experimental.pallas import tpu as pltpu
from jax.sharding import PartitionSpec as P

AXES = ("tile", "band")
ORDER = ("band", "tile")
SUB = 8
LANE = 128
MSG = 4 * SUB + 1
TARGET = 6 * SUB
SOURCE = 3 * SUB
ROWS = 32
GROUP = 16
VMEM_LIMIT = 16 * 1024 * 1024
PACK_LIMIT = 56 * 1024 * 1024
PEERS = 32


def iota(axis):
    return lax.broadcasted_iota(jnp.int32, (SUB, LANE), axis)


def pick(values, index):
    values = jnp.broadcast_to(values, (SUB, LANE))
    return jnp.take_along_axis(values, index, axis=1, mode="promise_in_bounds")


def shift_of(size):
    shift = size.bit_length() - 1
    assert 1 << shift == size
    return shift


def cross(left, right):
    return [
        left[1] * right[2] - left[2] * right[1],
        left[2] * right[0] - left[0] * right[2],
        left[0] * right[1] - left[1] * right[0],
    ]


def dot3(left, right):
    return left[0] * right[0] + left[1] * right[1] + left[2] * right[2]


def splat_rotation(poses, f):
    half = [jnp.full((SUB, LANE), poses[i, f] * 0.5, jnp.float32) for i in range(3)]
    w = 1.0 / jnp.sqrt(1.0 + half[0] * half[0] + half[1] * half[1] + half[2] * half[2])
    x, y, z = half[0] * w, half[1] * w, half[2] * w
    rotation = [
        [1.0 - 2.0 * (y * y + z * z), 2.0 * (x * y - w * z), 2.0 * (x * z + w * y)],
        [2.0 * (x * y + w * z), 1.0 - 2.0 * (x * x + z * z), 2.0 * (y * z - w * x)],
        [2.0 * (x * z - w * y), 2.0 * (y * z + w * x), 1.0 - 2.0 * (x * x + y * y)],
    ]
    return rotation, [jnp.full((SUB, LANE), poses[i, f], jnp.float32) for i in range(3, 6)]


def write_rotations(poses, turns):
    for f in range(poses.shape[1]):
        rotation, move = splat_rotation(poses, f)
        for i, tile in enumerate(rotation[0] + rotation[1] + rotation[2] + move):
            at = (12 * f + i) * SUB
            turns[at : at + SUB, :] = tile


def write_world(fields, turns, world, frags):
    blocks = fields[0].shape[1]
    total = turns.shape[0] // (12 * SUB)
    per_frag, stride = blocks // total, blocks + SUB
    for f in frags:
        tile = [turns[(12 * f + i) * SUB : (12 * f + i + 1) * SUB, :] for i in range(12)]
        for b in range(f * per_frag, (f + 1) * per_frag, SUB):
            for at, field in enumerate(fields):
                x = [field[j, b : b + SUB, :] for j in range(3)]
                for i in range(3):
                    row = dot3(tile[3 * i : 3 * i + 3], x)
                    if at == 0:
                        row = row + tile[9 + i]
                    world[pl.ds((3 * at + i) * stride + b, SUB), :] = row


def write_directions(directions, table):
    frags = directions.shape[2]
    for v in range(2):
        for j in range(6):
            table[6 * v + j : 6 * v + j + 1, 0:frags] = directions[j, v : v + 1, :]


def peer_at(place, sizes):
    n_tile, n_band = sizes
    if isinstance(place, int):
        return place % n_tile * n_band + place // n_tile
    tile = lax.bitwise_and(place, n_tile - 1)
    return tile * n_band + lax.shift_right_logical(place, shift_of(n_tile))


def entries(row_ref, index):
    out = jnp.zeros((SUB, LANE), row_ref.dtype)
    tile = lax.shift_right_logical(index, shift_of(LANE))
    for t in range(row_ref.shape[1] // LANE):
        hit = pick(row_ref[0:1, t * LANE : (t + 1) * LANE], lax.bitwise_and(index, LANE - 1))
        out = jnp.where(tile == t, hit, out)
    return out


def pack_kernel(
    points_h, poses_h, directions_h, src_h, maps_h, counts_h, out_h,
    points, poses, directions, src_s, src_v, maps, used, world, turns, table, out, sems, out_sems, *, sizes,
):
    devices = counts_h.shape[1]
    per_frag = points.shape[1] // poses.shape[1]
    stride = points.shape[1] + SUB
    frags = poses.shape[1]
    pairs = [(directions_h, directions), (src_h, src_v), (counts_h, used), (poses_h, poses)]
    pairs += [(src_h, src_s), (maps_h, maps)]
    pairs += [(points_h.at[j], points.at[j]) for j in range(3)]
    copies = [pltpu.make_async_copy(a, b, sems.at[i]) for i, (a, b) in enumerate(pairs)]
    for copy in copies:
        copy.start()
    for copy in copies[0:3]:
        copy.wait()
    write_directions(directions, table)
    limits = jnp.broadcast_to(used[0:1, :], (SUB, devices)).astype(jnp.float32)
    peers = lax.broadcasted_iota(jnp.int32, (SUB, devices), 1)
    row = lax.broadcasted_iota(jnp.int32, (SUB, devices), 0)
    slot = lax.shift_right_logical(iota(1), shift_of(GROUP))
    field = lax.bitwise_and(iota(1), GROUP - 1)
    for q in range(0, devices, SUB):
        block = entries(src_v, peer_at(iota(0) + q, sizes) * SUB + slot)
        frag = lax.shift_right_logical(block, shift_of(per_frag))
        hit = peers == peer_at(row + q, sizes)
        limit = jnp.sum(jnp.where(hit, limits, 0.0), axis=1, keepdims=True)
        extras = jnp.where(slot.astype(jnp.float32) < limit, 1.0, 0.0)
        for j in range(12):
            extras = jnp.where(field == j, pick(table[j : j + 1, :], frag), extras)
        extras = jnp.where(field == 13, frag.astype(jnp.float32), extras)
        out[pl.ds(q * MSG + MSG - 1, SUB, stride=MSG), :] = extras
    copies[3].wait()
    write_rotations(poses, turns)
    copies[5].wait()
    for q in range(devices):
        p = peer_at(q, sizes)
        rows = maps[p * SUB : (p + 1) * SUB, :]
        out[pl.ds(q * MSG + 3 * SUB, SUB), :] = rows.astype(jnp.float32)
    for copy in copies[6:]:
        copy.wait()
    write_world([points], turns, world, range(frags))
    copies[4].wait()

    def peer(q):
        p = peer_at(q, sizes)
        for s in range(SUB):
            block = src_s[0, p * SUB + s]
            out[pl.ds(q * MSG + s, 3, stride=SUB), :] = world[pl.ds(block, 3, stride=stride), :]

    def piece(i):
        rows = pl.ds(i * SUB * MSG, SUB * MSG)
        return pltpu.make_async_copy(out.at[rows], out_h.at[rows], out_sems.at[i])

    for i in range(devices // SUB):
        for u in range(SUB):
            peer(i * SUB + u)
        piece(i).start()
    for i in range(devices // SUB):
        piece(i).wait()


def halves_of(values):
    high = values.astype(jnp.bfloat16)
    return high, (values - high.astype(jnp.float32)).astype(jnp.bfloat16)


def turn_steps(at, left, parts, i, t, put):
    first, second = i * 2 * LANE, i * 2 * LANE + LANE

    def split(u):
        high, low = halves_of(jnp.concatenate([at(u), at(u + 1)], axis=0))
        parts[u * SUB : (u + 2) * SUB, first : first + LANE] = high
        parts[u * SUB : (u + 2) * SUB, second : second + LANE] = low

    def multiply():
        put(
            lax.dot_general(
                left,
                parts[t : t + LANE, first : second + LANE],
                (((1,), (1,)), ((), ())),
                preferred_element_type=jnp.float32,
            )
        )

    tiles = range(t // SUB, (t + LANE) // SUB, 2)
    return [functools.partial(split, u) for u in tiles], multiply


def field_steps(source, target, index, same, parts, turned, t):
    def put(k, value):
        turned[k * LANE : (k + 1) * LANE, t : t + LANE] = value

    def turn_source(k):
        tiles = [source(u, k) for u in range(t // SUB, (t + LANE) // SUB)]
        put(6 + k, jnp.concatenate(tiles, axis=0).T)

    splits, products = [], []
    for k in range(6):

        def at(u, k=k):
            return pick(target(u, k), index(u))

        split, product = turn_steps(at, same, parts, k, t, functools.partial(put, k))
        splits.append(split)
        products.append(product)
    steps = [split[u] for u in range(len(splits[0])) for split in splits]
    return steps + products + [functools.partial(turn_source, k) for k in range(3)]


def run(steps):
    for step in steps:
        step()


def join_directions(side_a, side_b, joined, lanes, lanes_b):
    joined[0:12, lanes] = side_a[0:12, lanes]
    for v in range(2):
        turn_rows, move_rows = slice(6 * v, 6 * v + 3), slice(6 * v + 3, 6 * v + 6)
        joined[move_rows, lanes] = side_a[move_rows, lanes] - side_b[move_rows, lanes_b]
        joined[12 + 3 * v : 15 + 3 * v, lanes] = side_b[turn_rows, lanes_b]


def point_sums(turned, joined, partial, t, between=()):
    lanes = slice(t, t + LANE)
    first = t // LANE * ROWS * SUB
    zero = jnp.zeros((SUB, LANE), jnp.float32)
    totals = [zero] * 27
    rounds = LANE // SUB
    for i in range(rounds):
        field = [turned[i * SUB + k * LANE : (i + 1) * SUB + k * LANE, lanes] for k in range(9)]
        way = [joined[j : j + 1, lanes] for j in range(18)]
        y, n, x = field[0:3], field[3:6], field[6:9]
        p, q = cross(x, n), cross(y, n)
        scalars = [dot3(n, [x[k] - y[k] for k in range(3)])]
        for v in range(2):
            a, b = way[6 * v : 6 * v + 6], way[12 + 3 * v : 15 + 3 * v]
            scalars.append(dot3(p, a[0:3]) + dot3(n, a[3:6]) - dot3(q, b))
        terms = []
        for s in scalars:
            terms += [s * value for value in p + n]
        for s in scalars:
            terms += [s * value for value in q]
        totals = [total + term for total, term in zip(totals, terms)]
        run(between[i * len(between) // rounds : (i + 1) * len(between) // rounds])
    for j in range(ROWS):
        partial[first + j * SUB : first + (j + 1) * SUB, :] = totals[j] if j < 27 else zero
    total = partial[pl.ds(first, ROWS, stride=SUB), :]
    for s in range(1, SUB):
        total = total + partial[pl.ds(first + s, ROWS, stride=SUB), :]
    return total


def frag_of(row, per_frag):
    return lax.shift_right_logical(row, shift_of(per_frag))


def look_up(table, frag, out):
    for at in range(0, frag.shape[1], LANE):
        index = jnp.broadcast_to(frag[:, at : at + LANE], (SUB, LANE))
        for j in range(0, 2 * SUB, SUB):
            out[j : j + SUB, at : at + LANE] = pick(table[j : j + SUB, :], index)


def by_frag(sums, frag):
    pairs = sums.shape[1]
    hot = jnp.broadcast_to(frag, (SUB, pairs)) == lax.broadcasted_iota(jnp.int32, (SUB, pairs), 0)
    return lax.dot_general(
        sums,
        hot.astype(jnp.float32),
        (((1,), (1,)), ((), ())),
        precision=lax.Precision.HIGHEST,
        preferred_element_type=jnp.float32,
    )


def target_side(total):
    rows = []
    for k in range(3):
        rows += [total[18 + 3 * k : 21 + 3 * k, :], total[6 * k + 3 : 6 * k + 6, :]]
    return -jnp.concatenate(rows, axis=0)


def constants(same, gather, place, mine):
    def wide(ref, axis):
        return lax.broadcasted_iota(jnp.int32, ref.shape, axis)

    def put(ref, hit):
        ref[...] = hit.astype(jnp.float32).astype(jnp.bfloat16)

    put(same, lax.bitwise_and(wide(same, 1), LANE - 1) == wide(same, 0))
    put(gather, lax.bitwise_and(wide(gather, 1), GROUP - 1) == wide(gather, 0))
    entry = lax.bitwise_and(wide(place, 1), GROUP - 1) + GROUP * lax.shift_right_logical(
        wide(place, 1), shift_of(LANE)
    )
    put(place, lax.bitwise_and(wide(place, 0), ROWS - 1) == entry)
    put(mine, lax.shift_right_logical(wide(mine, 1), shift_of(SUB)) == wide(mine, 0))


def local_kernel(
    points, normals, poses, directions, pairs_s, pairs_v, maps, dst_s, dst_v,
    staged, remote_b, remote_frag, totals, same, gather, place, mine,
    world, turns, table, sources, targets, side_a, side_b, joined, parts, turned, partial, *, sizes,
):
    per_frag = points.shape[1] // poses.shape[1]
    stride = points.shape[1] + SUB
    constants(same, gather, place, mine)
    table[...] = jnp.zeros_like(table)
    write_directions(directions, table)
    for at in range(0, dst_v.shape[1], LANE):
        flat = iota(1) + at
        peer = peer_at(lax.shift_right_logical(flat, shift_of(SUB)), sizes)
        block = entries(dst_v, peer * SUB + lax.bitwise_and(flat, SUB - 1))
        remote_frag[0:1, at : at + LANE] = frag_of(block, per_frag)[0:1, :]
    look_up(table, remote_frag[...], remote_b)
    frag_a, frag_b = frag_of(pairs_v[0:1, :], per_frag), frag_of(pairs_v[1:2, :], per_frag)
    look_up(table, frag_a, side_a)
    look_up(table, frag_b, side_b)
    every = slice(0, pairs_s.shape[1])
    join_directions(side_a, side_b, joined, every, every)
    write_rotations(poses, turns)
    write_world([points, normals], turns, world, range(poses.shape[1]))

    def stage_remote(g, carry):
        for s in range(SUB):
            block = dst_s[0, peer_at(g, sizes) * SUB + s]
            staged[pl.ds(g * TARGET + s, 6, stride=SUB), :] = world[pl.ds(block, 6, stride=stride), :]
        return carry

    lax.fori_loop(0, dst_s.shape[1] // SUB, stage_remote, 0, unroll=4)

    def stage_local(g, carry):
        for s in range(SUB):
            a, b = pairs_s[0, g * SUB + s], pairs_s[1, g * SUB + s]
            targets[pl.ds(g * TARGET + s, 6, stride=SUB), :] = world[pl.ds(b, 6, stride=stride), :]
            sources[pl.ds(g * SOURCE + s, 3, stride=SUB), :] = world[pl.ds(a, 3, stride=stride), :]
        return carry

    lax.fori_loop(0, pairs_s.shape[1] // SUB, stage_local, 0, unroll=4)
    total = jnp.zeros(totals.shape, jnp.float32)
    tiles = range(0, pairs_s.shape[1], LANE)
    steps = [
        field_steps(
            lambda u, k: sources[u * SOURCE + k * SUB : u * SOURCE + (k + 1) * SUB, :],
            lambda u, k: targets[u * TARGET + k * SUB : u * TARGET + (k + 1) * SUB, :],
            lambda u: maps[u * SUB : (u + 1) * SUB, :],
            same[...],
            parts,
            turned,
            t,
        )
        for t in tiles
    ]
    run(steps[0])
    for i, t in enumerate(tiles):
        between = steps[i + 1] if i + 1 < len(steps) else ()
        sums = point_sums(turned, joined, partial, t, between)
        total = total + by_frag(sums, frag_a[:, t : t + LANE])[0:18, :]
        total = total + target_side(by_frag(sums, frag_b[:, t : t + LANE]))
    totals[...] = total


def remote_kernel(
    arrived, staged, remote_b, remote_frag, local_totals, same, gather, place, mine,
    back, totals, side_a, joined, frags, index, parts, turned, partial,
):
    f32 = jnp.float32
    pairs = parts.shape[0]
    peers = pairs // SUB
    own = lax.shift_right_logical(iota(1), shift_of(GROUP)) == iota(0)
    slot = lax.shift_right_logical(iota(1), shift_of(GROUP)).astype(f32)[0:1, :]

    def block(c, total):
        first = c * peers
        start = c * pairs if isinstance(c, int) else pl.multiple_of(c * pairs, LANE)

        def row_at(u, size, row):
            at = (first + u) * size + row
            return at if isinstance(c, int) or size == MSG else pl.multiple_of(at, SUB)

        def extras(u):
            row = arrived[pl.ds(row_at(u, MSG, 4 * SUB), 1), :]
            frags[u * SUB : (u + 1) * SUB, :] = pick(row, iota(0) * GROUP + 13)
            return jnp.where(own, jnp.broadcast_to(row, (SUB, LANE)), 0.0)

        def front(t):
            lanes = slice(t, t + LANE)

            def indices():
                for u in range(t // SUB, (t + LANE) // SUB):
                    rows = arrived[pl.ds(row_at(u, MSG, 3 * SUB), SUB), :]
                    index[u * SUB : (u + 1) * SUB, :] = rows.astype(jnp.int32)

            def put(value):
                side_a[:, lanes] = value
                join_directions(side_a, remote_b, joined, lanes, pl.ds(start + t, LANE))

            split, product = turn_steps(extras, gather[...], parts, 6, t, put)
            return (
                [indices]
                + split
                + [product]
                + field_steps(
                    lambda u, k: arrived[pl.ds(row_at(u, MSG, SUB * k), SUB), :],
                    lambda u, k: staged[pl.ds(row_at(u, TARGET, SUB * k), SUB), :],
                    lambda u: index[u * SUB : (u + 1) * SUB, :],
                    same[...],
                    parts,
                    turned,
                    t,
                )
            )

        rows = [jnp.zeros((peers, LANE), f32) for half in range(2)]

        def back_steps(sums, t):
            lanes = slice(t, t + LANE)
            held = {}

            def scatter():
                held["placed"] = lax.dot_general(
                    jnp.concatenate(halves_of(sums), axis=0),
                    place[...],
                    (((0,), (0,)), ((), ())),
                    preferred_element_type=f32,
                )

            def add(half):
                hit = frags[lanes, :] == jnp.broadcast_to(slot, (LANE, LANE))
                part = jnp.where(hit, held["placed"][:, half * LANE : (half + 1) * LANE], 0.0)
                for piece in halves_of(part):
                    rows[half] = rows[half] + jnp.dot(
                        mine[:, lanes], piece, preferred_element_type=f32
                    )

            def own_side():
                frag = remote_frag[0:1, pl.ds(start + t, LANE)]
                held["total"] = target_side(by_frag(sums, frag))

            return [scatter, functools.partial(add, 0), functools.partial(add, 1), own_side], held

        tiles = range(0, pairs, LANE)
        steps = front(tiles[0])
        run(steps)
        behind, held = [], []
        for t in tiles:
            between = behind + (front(t + LANE) if t + LANE < pairs else [])
            sums = point_sums(turned, joined, partial, t, between)
            sums = sums * side_a[12:13, t : t + LANE]
            behind, kept = back_steps(sums, t)
            held.append(kept)
        run(behind)
        for kept in held:
            total = total + kept["total"]
        for half in range(2):
            back[pl.ds(2 * first + half, peers, stride=2), :] = rows[half]
        return total

    blocks = back.shape[0] // (2 * peers)
    total = local_totals[...]
    totals[...] = block(0, total) if blocks == 1 else lax.fori_loop(0, blocks, block, total)


def final_kernel(back, totals, gradient, hess, *, per_frag):
    devices = back.shape[0] // 2
    frags = gradient.shape[1]
    index = lax.bitwise_and(iota(1), frags - 1) * GROUP + iota(0)
    halves = []
    for half in range(2):
        tile = back[pl.ds(half, SUB, stride=2), :]
        for q in range(SUB, devices, SUB):
            tile = tile + back[pl.ds(2 * q + half, SUB, stride=2), :]
        halves.append(jnp.sum(tile, axis=0, keepdims=True))
    parts = [pick(halves[0], index), pick(halves[0], index + SUB), pick(halves[1], index)]
    total = jnp.concatenate(parts, axis=0)[0:18, 0:frags] + totals[...]
    gradient[...] = total[0:6, :] * (1.0 / LANE)
    for v in range(2):
        part = total[6 + 6 * v : 12 + 6 * v, :] * (1.0 / (LANE * per_frag))
        for j in range(6):
            hess[j, v : v + 1, :] = part[j : j + 1, :]


def call(kernel, outs, scratch, spaces, limit=VMEM_LIMIT, out_space="v", **more):
    kinds = {"v": pltpu.VMEM, "s": pltpu.SMEM, "h": pltpu.HBM}
    return pl.pallas_call(
        kernel,
        out_shape=outs,
        in_specs=[pl.BlockSpec(memory_space=kinds[s]) for s in spaces],
        out_specs=[pl.BlockSpec(memory_space=kinds[out_space])] * len(outs),
        scratch_shapes=scratch,
        compiler_params=pltpu.CompilerParams(vmem_limit_bytes=limit),
        **more,
    )


def in_hbm(values):
    return pltpu.with_memory_space_constraint(values, pltpu.HBM)


def exchange(rows, devices):
    sent = rows.reshape(devices, 1, -1)
    sent = lax.all_to_all(sent, ORDER, split_axis=0, concat_axis=0, tiled=True)
    return sent.reshape(rows.shape)


def local(
    points, normals, poses, directions, local_pairs, local_maps,
    remote_src, remote_maps, remote_dst, counts,
):
    sizes = lax.axis_size("tile"), lax.axis_size("band")
    devices = sizes[0] * sizes[1]
    blocks, _, count = points.shape
    frags = poses.shape[1]
    slots = remote_src.shape[1]
    pairs = local_pairs.shape[1]
    assert count == LANE and frags == SUB and slots == devices * SUB and devices % PEERS == 0
    per_frag = blocks // frags
    stride = blocks + SUB
    f32 = jnp.float32
    points = points.transpose(1, 0, 2)
    normals = normals.transpose(1, 0, 2)
    directions = directions.transpose(1, 0, 2)

    def array(*shape, dtype=f32):
        return jax.ShapeDtypeStruct(shape, dtype)

    def vmem(*shape, dtype=f32):
        return pltpu.VMEM(shape, dtype)

    i32, bf16 = jnp.int32, jnp.bfloat16
    part = PEERS * SUB
    (message,) = call(
        functools.partial(pack_kernel, sizes=sizes),
        [array(devices * MSG, LANE)],
        [
            vmem(3, blocks, LANE),
            pltpu.SMEM((6, frags), f32),
            vmem(6, 2, frags),
            pltpu.SMEM((1, slots), i32),
            vmem(1, slots, dtype=i32),
            vmem(slots, LANE, dtype=i32),
            vmem(1, devices, dtype=i32),
            vmem(3 * stride, LANE),
            vmem(12 * frags * SUB, LANE),
            vmem(2 * SUB, LANE),
            vmem(devices * MSG, LANE),
            pltpu.SemaphoreType.DMA((9,)),
            pltpu.SemaphoreType.DMA((devices // SUB,)),
        ],
        "hhhhhh",
        limit=PACK_LIMIT,
        out_space="h",
    )(*[in_hbm(x) for x in (points, poses, directions, remote_src, remote_maps[0], counts)])
    arrived = exchange(message, devices)
    staged, remote_b, remote_frag, totals, same, gather, place, mine = call(
        functools.partial(local_kernel, sizes=sizes),
        [
            array(devices * TARGET, LANE),
            array(2 * SUB, slots),
            array(1, slots, dtype=i32),
            array(18, frags),
            array(LANE, 2 * LANE, dtype=bf16),
            array(GROUP, 2 * LANE, dtype=bf16),
            array(2 * ROWS, 2 * LANE, dtype=bf16),
            array(PEERS, part, dtype=bf16),
        ],
        [
            vmem(6 * stride, LANE),
            vmem(12 * frags * SUB, LANE),
            vmem(2 * SUB, LANE),
            vmem(pairs // SUB * SOURCE, LANE),
            vmem(pairs // SUB * TARGET, LANE),
            vmem(2 * SUB, pairs),
            vmem(2 * SUB, pairs),
            vmem(3 * SUB, pairs),
            vmem(pairs, 6 * 2 * LANE, dtype=bf16),
            vmem(9 * LANE, pairs),
            vmem(pairs // LANE * ROWS * SUB, LANE),
        ],
        "vvsvsvvsv",
        cost_estimate=pl.CostEstimate(
            flops=200 * pairs * LANE, bytes_accessed=4_000_000, transcendentals=0
        ),
    )(
        points, normals, poses, directions, local_pairs, local_pairs, local_maps,
        remote_dst, remote_dst,
    )
    back, totals = call(
        remote_kernel,
        [array(devices * 2, LANE), array(18, frags)],
        [
            vmem(2 * SUB, part),
            vmem(3 * SUB, part),
            vmem(part, LANE),
            vmem(part, LANE, dtype=i32),
            vmem(part, 7 * 2 * LANE, dtype=bf16),
            vmem(9 * LANE, part),
            vmem(part // LANE * ROWS * SUB, LANE),
        ],
        "vvvvvvvvv",
    )(arrived, staged, remote_b, remote_frag, totals, same, gather, place, mine)
    back = exchange(back, devices)
    gradient, hess = call(
        functools.partial(final_kernel, per_frag=per_frag),
        [array(6, frags), array(6, 2, frags)],
        [],
        "vv",
    )(back, totals)
    return (gradient, hess.transpose(1, 0, 2))


def solution(mesh):
    placed = (
        P(AXES, None, None),
        P(AXES, None, None),
        P(None, AXES),
        P(None, None, AXES),
        P(None, AXES),
        P(AXES, None),
        P(AXES, None),
        P(AXES, None, None),
        P(AXES, None),
        P(AXES, None),
    )
    return jax.shard_map(
        local,
        mesh=mesh,
        in_specs=placed,
        out_specs=(P(None, AXES), P(None, None, AXES)),
        check_vma=False,
    )
```

```python
import functools

import jax
import jax.numpy as jnp
from jax import lax
from jax.experimental import pallas as pl
from jax.experimental.pallas import tpu as pltpu
from jax.sharding import PartitionSpec as P

AXES = ("tile", "band")
ORDER = ("band", "tile")
SUB = 8
LANE = 128
MSG = 4 * SUB + 1
TARGET = 6 * SUB
SOURCE = 3 * SUB
ROWS = 32
GROUP = 16
VMEM_LIMIT = 16 * 1024 * 1024
PACK_LIMIT = 56 * 1024 * 1024
PEERS = 32


def iota(axis):
    return lax.broadcasted_iota(jnp.int32, (SUB, LANE), axis)


def pick(values, index):
    values = jnp.broadcast_to(values, (SUB, LANE))
    return jnp.take_along_axis(values, index, axis=1, mode="promise_in_bounds")


def shift_of(size):
    shift = size.bit_length() - 1
    assert 1 << shift == size
    return shift


def cross(left, right):
    return [
        left[1] * right[2] - left[2] * right[1],
        left[2] * right[0] - left[0] * right[2],
        left[0] * right[1] - left[1] * right[0],
    ]


def dot3(left, right):
    return left[0] * right[0] + left[1] * right[1] + left[2] * right[2]


def splat_rotation(poses, f):
    half = [jnp.full((SUB, LANE), poses[i, f] * 0.5, jnp.float32) for i in range(3)]
    w = 1.0 / jnp.sqrt(1.0 + half[0] * half[0] + half[1] * half[1] + half[2] * half[2])
    x, y, z = half[0] * w, half[1] * w, half[2] * w
    rotation = [
        [1.0 - 2.0 * (y * y + z * z), 2.0 * (x * y - w * z), 2.0 * (x * z + w * y)],
        [2.0 * (x * y + w * z), 1.0 - 2.0 * (x * x + z * z), 2.0 * (y * z - w * x)],
        [2.0 * (x * z - w * y), 2.0 * (y * z + w * x), 1.0 - 2.0 * (x * x + y * y)],
    ]
    return rotation, [jnp.full((SUB, LANE), poses[i, f], jnp.float32) for i in range(3, 6)]


def write_rotations(poses, turns):
    for f in range(poses.shape[1]):
        rotation, move = splat_rotation(poses, f)
        for i, tile in enumerate(rotation[0] + rotation[1] + rotation[2] + move):
            at = (12 * f + i) * SUB
            turns[at : at + SUB, :] = tile


def write_world(fields, turns, world, frags):
    blocks = fields[0].shape[1]
    total = turns.shape[0] // (12 * SUB)
    per_frag, stride = blocks // total, blocks + SUB
    for f in frags:
        tile = [turns[(12 * f + i) * SUB : (12 * f + i + 1) * SUB, :] for i in range(12)]
        for b in range(f * per_frag, (f + 1) * per_frag, SUB):
            for at, field in enumerate(fields):
                x = [field[j, b : b + SUB, :] for j in range(3)]
                for i in range(3):
                    row = dot3(tile[3 * i : 3 * i + 3], x)
                    if at == 0:
                        row = row + tile[9 + i]
                    world[pl.ds((3 * at + i) * stride + b, SUB), :] = row


def write_directions(directions, table):
    frags = directions.shape[2]
    for v in range(2):
        for j in range(6):
            table[6 * v + j : 6 * v + j + 1, 0:frags] = directions[j, v : v + 1, :]


def peer_at(place, sizes):
    n_tile, n_band = sizes
    if isinstance(place, int):
        return place % n_tile * n_band + place // n_tile
    tile = lax.bitwise_and(place, n_tile - 1)
    return tile * n_band + lax.shift_right_logical(place, shift_of(n_tile))


def entries(row_ref, index):
    out = jnp.zeros((SUB, LANE), row_ref.dtype)
    tile = lax.shift_right_logical(index, shift_of(LANE))
    for t in range(row_ref.shape[1] // LANE):
        hit = pick(row_ref[0:1, t * LANE : (t + 1) * LANE], lax.bitwise_and(index, LANE - 1))
        out = jnp.where(tile == t, hit, out)
    return out


def pack_kernel(
    points_h, poses_h, directions_h, src_h, maps_h, counts_h, out_h,
    points, poses, directions, src_s, src_v, maps, used, world, turns, table, out, sems, out_sems, *, sizes,
):
    devices = counts_h.shape[1]
    per_frag = points.shape[1] // poses.shape[1]
    stride = points.shape[1] + SUB
    frags = poses.shape[1]
    pairs = [(directions_h, directions), (src_h, src_v), (counts_h, used), (poses_h, poses)]
    pairs += [(points_h.at[j], points.at[j]) for j in range(3)]
    pairs += [(src_h, src_s), (maps_h, maps)]
    copies = [pltpu.make_async_copy(a, b, sems.at[i]) for i, (a, b) in enumerate(pairs)]
    for copy in copies:
        copy.start()
    for copy in copies[0:3]:
        copy.wait()
    write_directions(directions, table)
    limits = jnp.broadcast_to(used[0:1, :], (SUB, devices)).astype(jnp.float32)
    peers = lax.broadcasted_iota(jnp.int32, (SUB, devices), 1)
    row = lax.broadcasted_iota(jnp.int32, (SUB, devices), 0)
    slot = lax.shift_right_logical(iota(1), shift_of(GROUP))
    field = lax.bitwise_and(iota(1), GROUP - 1)
    for q in range(0, devices, SUB):
        block = entries(src_v, peer_at(iota(0) + q, sizes) * SUB + slot)
        frag = lax.shift_right_logical(block, shift_of(per_frag))
        hit = peers == peer_at(row + q, sizes)
        limit = jnp.sum(jnp.where(hit, limits, 0.0), axis=1, keepdims=True)
        extras = jnp.where(slot.astype(jnp.float32) < limit, 1.0, 0.0)
        for j in range(12):
            extras = jnp.where(field == j, pick(table[j : j + 1, :], frag), extras)
        extras = jnp.where(field == 13, frag.astype(jnp.float32), extras)
        out[pl.ds(q * MSG + MSG - 1, SUB, stride=MSG), :] = extras
    copies[3].wait()
    write_rotations(poses, turns)
    for copy in copies[4:7]:
        copy.wait()
    write_world([points], turns, world, range(frags))
    for copy in copies[7:]:
        copy.wait()

    def peer(q):
        p = peer_at(q, sizes)
        for s in range(SUB):
            block = src_s[0, p * SUB + s]
            out[pl.ds(q * MSG + s, 3, stride=SUB), :] = world[pl.ds(block, 3, stride=stride), :]
        rows = maps[p * SUB : (p + 1) * SUB, :]
        out[pl.ds(q * MSG + 3 * SUB, SUB), :] = rows.astype(jnp.float32)

    def piece(i):
        rows = pl.ds(i * SUB * MSG, SUB * MSG)
        return pltpu.make_async_copy(out.at[rows], out_h.at[rows], out_sems.at[i])

    for i in range(devices // SUB):
        for u in range(SUB):
            peer(i * SUB + u)
        piece(i).start()
    for i in range(devices // SUB):
        piece(i).wait()


def halves_of(values):
    high = values.astype(jnp.bfloat16)
    return high, (values - high.astype(jnp.float32)).astype(jnp.bfloat16)


def turn_steps(at, left, parts, i, t, put):
    first, second = i * 2 * LANE, i * 2 * LANE + LANE

    def split(u):
        high, low = halves_of(jnp.concatenate([at(u), at(u + 1)], axis=0))
        parts[u * SUB : (u + 2) * SUB, first : first + LANE] = high
        parts[u * SUB : (u + 2) * SUB, second : second + LANE] = low

    def multiply():
        put(
            lax.dot_general(
                left,
                parts[t : t + LANE, first : second + LANE],
                (((1,), (1,)), ((), ())),
                preferred_element_type=jnp.float32,
            )
        )

    tiles = range(t // SUB, (t + LANE) // SUB, 2)
    return [functools.partial(split, u) for u in tiles], multiply


def field_steps(source, target, index, same, parts, turned, t):
    def put(k, value):
        turned[k * LANE : (k + 1) * LANE, t : t + LANE] = value

    def turn_source(k):
        tiles = [source(u, k) for u in range(t // SUB, (t + LANE) // SUB)]
        put(6 + k, jnp.concatenate(tiles, axis=0).T)

    splits, products = [], []
    for k in range(6):

        def at(u, k=k):
            return pick(target(u, k), index(u))

        split, product = turn_steps(at, same, parts, k, t, functools.partial(put, k))
        splits.append(split)
        products.append(product)
    steps = [split[u] for u in range(len(splits[0])) for split in splits]
    return steps + products + [functools.partial(turn_source, k) for k in range(3)]


def run(steps):
    for step in steps:
        step()


def join_directions(side_a, side_b, joined, lanes, lanes_b):
    joined[0:12, lanes] = side_a[0:12, lanes]
    for v in range(2):
        turn_rows, move_rows = slice(6 * v, 6 * v + 3), slice(6 * v + 3, 6 * v + 6)
        joined[move_rows, lanes] = side_a[move_rows, lanes] - side_b[move_rows, lanes_b]
        joined[12 + 3 * v : 15 + 3 * v, lanes] = side_b[turn_rows, lanes_b]


def point_sums(turned, joined, partial, t, between=()):
    lanes = slice(t, t + LANE)
    first = t // LANE * ROWS * SUB
    zero = jnp.zeros((SUB, LANE), jnp.float32)
    totals = [zero] * 27
    rounds = LANE // SUB
    for i in range(rounds):
        field = [turned[i * SUB + k * LANE : (i + 1) * SUB + k * LANE, lanes] for k in range(9)]
        way = [joined[j : j + 1, lanes] for j in range(18)]
        y, n, x = field[0:3], field[3:6], field[6:9]
        p, q = cross(x, n), cross(y, n)
        scalars = [dot3(n, [x[k] - y[k] for k in range(3)])]
        for v in range(2):
            a, b = way[6 * v : 6 * v + 6], way[12 + 3 * v : 15 + 3 * v]
            scalars.append(dot3(p, a[0:3]) + dot3(n, a[3:6]) - dot3(q, b))
        terms = []
        for s in scalars:
            terms += [s * value for value in p + n]
        for s in scalars:
            terms += [s * value for value in q]
        totals = [total + term for total, term in zip(totals, terms)]
        run(between[i * len(between) // rounds : (i + 1) * len(between) // rounds])
    for j in range(ROWS):
        partial[first + j * SUB : first + (j + 1) * SUB, :] = totals[j] if j < 27 else zero
    total = partial[pl.ds(first, ROWS, stride=SUB), :]
    for s in range(1, SUB):
        total = total + partial[pl.ds(first + s, ROWS, stride=SUB), :]
    return total


def frag_of(row, per_frag):
    return lax.shift_right_logical(row, shift_of(per_frag))


def look_up(table, frag, out):
    for at in range(0, frag.shape[1], LANE):
        index = jnp.broadcast_to(frag[:, at : at + LANE], (SUB, LANE))
        for j in range(0, 2 * SUB, SUB):
            out[j : j + SUB, at : at + LANE] = pick(table[j : j + SUB, :], index)


def by_frag(sums, frag):
    pairs = sums.shape[1]
    hot = jnp.broadcast_to(frag, (SUB, pairs)) == lax.broadcasted_iota(jnp.int32, (SUB, pairs), 0)
    return lax.dot_general(
        sums,
        hot.astype(jnp.float32),
        (((1,), (1,)), ((), ())),
        precision=lax.Precision.HIGHEST,
        preferred_element_type=jnp.float32,
    )


def target_side(total):
    rows = []
    for k in range(3):
        rows += [total[18 + 3 * k : 21 + 3 * k, :], total[6 * k + 3 : 6 * k + 6, :]]
    return -jnp.concatenate(rows, axis=0)


def constants(same, gather, place, mine):
    def wide(ref, axis):
        return lax.broadcasted_iota(jnp.int32, ref.shape, axis)

    def put(ref, hit):
        ref[...] = hit.astype(jnp.float32).astype(jnp.bfloat16)

    put(same, lax.bitwise_and(wide(same, 1), LANE - 1) == wide(same, 0))
    put(gather, lax.bitwise_and(wide(gather, 1), GROUP - 1) == wide(gather, 0))
    entry = lax.bitwise_and(wide(place, 1), GROUP - 1) + GROUP * lax.shift_right_logical(
        wide(place, 1), shift_of(LANE)
    )
    put(place, lax.bitwise_and(wide(place, 0), ROWS - 1) == entry)
    put(mine, lax.shift_right_logical(wide(mine, 1), shift_of(SUB)) == wide(mine, 0))


def local_kernel(
    points, normals, poses, directions, pairs_s, pairs_v, maps, dst_s, dst_v,
    staged, remote_b, remote_frag, totals, same, gather, place, mine,
    world, turns, table, sources, targets, side_a, side_b, joined, parts, turned, partial, *, sizes,
):
    per_frag = points.shape[1] // poses.shape[1]
    stride = points.shape[1] + SUB
    constants(same, gather, place, mine)
    table[...] = jnp.zeros_like(table)
    write_directions(directions, table)
    for at in range(0, dst_v.shape[1], LANE):
        flat = iota(1) + at
        peer = peer_at(lax.shift_right_logical(flat, shift_of(SUB)), sizes)
        block = entries(dst_v, peer * SUB + lax.bitwise_and(flat, SUB - 1))
        remote_frag[0:1, at : at + LANE] = frag_of(block, per_frag)[0:1, :]
    look_up(table, remote_frag[...], remote_b)
    frag_a, frag_b = frag_of(pairs_v[0:1, :], per_frag), frag_of(pairs_v[1:2, :], per_frag)
    look_up(table, frag_a, side_a)
    look_up(table, frag_b, side_b)
    every = slice(0, pairs_s.shape[1])
    join_directions(side_a, side_b, joined, every, every)
    write_rotations(poses, turns)
    write_world([points, normals], turns, world, range(poses.shape[1]))

    def stage_remote(g, carry):
        for s in range(SUB):
            block = dst_s[0, peer_at(g, sizes) * SUB + s]
            staged[pl.ds(g * TARGET + s, 6, stride=SUB), :] = world[pl.ds(block, 6, stride=stride), :]
        return carry

    lax.fori_loop(0, dst_s.shape[1] // SUB, stage_remote, 0, unroll=4)

    def stage_local(g, carry):
        for s in range(SUB):
            a, b = pairs_s[0, g * SUB + s], pairs_s[1, g * SUB + s]
            targets[pl.ds(g * TARGET + s, 6, stride=SUB), :] = world[pl.ds(b, 6, stride=stride), :]
            sources[pl.ds(g * SOURCE + s, 3, stride=SUB), :] = world[pl.ds(a, 3, stride=stride), :]
        return carry

    lax.fori_loop(0, pairs_s.shape[1] // SUB, stage_local, 0, unroll=4)
    total = jnp.zeros(totals.shape, jnp.float32)
    tiles = range(0, pairs_s.shape[1], LANE)
    steps = [
        field_steps(
            lambda u, k: sources[u * SOURCE + k * SUB : u * SOURCE + (k + 1) * SUB, :],
            lambda u, k: targets[u * TARGET + k * SUB : u * TARGET + (k + 1) * SUB, :],
            lambda u: maps[u * SUB : (u + 1) * SUB, :],
            same[...],
            parts,
            turned,
            t,
        )
        for t in tiles
    ]
    run(steps[0])
    for i, t in enumerate(tiles):
        between = steps[i + 1] if i + 1 < len(steps) else ()
        sums = point_sums(turned, joined, partial, t, between)
        total = total + by_frag(sums, frag_a[:, t : t + LANE])[0:18, :]
        total = total + target_side(by_frag(sums, frag_b[:, t : t + LANE]))
    totals[...] = total


def remote_kernel(
    arrived, staged, remote_b, remote_frag, local_totals, same, gather, place, mine,
    back, totals, side_a, joined, frags, index, parts, turned, partial,
):
    f32 = jnp.float32
    pairs = parts.shape[0]
    peers = pairs // SUB
    own = lax.shift_right_logical(iota(1), shift_of(GROUP)) == iota(0)
    slot = lax.shift_right_logical(iota(1), shift_of(GROUP)).astype(f32)[0:1, :]

    def block(c, total):
        first = c * peers
        start = c * pairs if isinstance(c, int) else pl.multiple_of(c * pairs, LANE)

        def row_at(u, size, row):
            at = (first + u) * size + row
            return at if isinstance(c, int) or size == MSG else pl.multiple_of(at, SUB)

        def extras(u):
            row = arrived[pl.ds(row_at(u, MSG, 4 * SUB), 1), :]
            frags[u * SUB : (u + 1) * SUB, :] = pick(row, iota(0) * GROUP + 13)
            return jnp.where(own, jnp.broadcast_to(row, (SUB, LANE)), 0.0)

        def front(t):
            lanes = slice(t, t + LANE)

            def indices():
                for u in range(t // SUB, (t + LANE) // SUB):
                    rows = arrived[pl.ds(row_at(u, MSG, 3 * SUB), SUB), :]
                    index[u * SUB : (u + 1) * SUB, :] = rows.astype(jnp.int32)

            def put(value):
                side_a[:, lanes] = value
                join_directions(side_a, remote_b, joined, lanes, pl.ds(start + t, LANE))

            split, product = turn_steps(extras, gather[...], parts, 6, t, put)
            return (
                [indices]
                + split
                + [product]
                + field_steps(
                    lambda u, k: arrived[pl.ds(row_at(u, MSG, SUB * k), SUB), :],
                    lambda u, k: staged[pl.ds(row_at(u, TARGET, SUB * k), SUB), :],
                    lambda u: index[u * SUB : (u + 1) * SUB, :],
                    same[...],
                    parts,
                    turned,
                    t,
                )
            )

        rows = [jnp.zeros((peers, LANE), f32) for half in range(2)]

        def back_steps(sums, t):
            lanes = slice(t, t + LANE)
            held = {}
            both = jnp.concatenate(halves_of(sums), axis=0)

            def scatter():
                held["placed"] = lax.dot_general(
                    both,
                    place[...],
                    (((0,), (0,)), ((), ())),
                    preferred_element_type=f32,
                )

            def add(half):
                hit = frags[lanes, :] == jnp.broadcast_to(slot, (LANE, LANE))
                part = jnp.where(hit, held["placed"][:, half * LANE : (half + 1) * LANE], 0.0)
                for piece in halves_of(part):
                    rows[half] = rows[half] + jnp.dot(
                        mine[:, lanes], piece, preferred_element_type=f32
                    )

            def own_side():
                frag = remote_frag[0:1, pl.ds(start + t, LANE)]
                hot = jnp.broadcast_to(frag, (SUB, LANE)) == iota(0)
                added = lax.dot_general(
                    both,
                    hot.astype(f32).astype(jnp.bfloat16),
                    (((1,), (1,)), ((), ())),
                    preferred_element_type=f32,
                )
                held["total"] = target_side(added[0:ROWS, :] + added[ROWS:, :])

            return [scatter, functools.partial(add, 0), functools.partial(add, 1), own_side], held

        tiles = range(0, pairs, LANE)
        steps = front(tiles[0])
        run(steps)
        behind, held = [], []
        for t in tiles:
            between = behind + (front(t + LANE) if t + LANE < pairs else [])
            sums = point_sums(turned, joined, partial, t, between)
            sums = sums * side_a[12:13, t : t + LANE]
            behind, kept = back_steps(sums, t)
            held.append(kept)
        run(behind)
        for kept in held:
            total = total + kept["total"]
        for half in range(2):
            back[pl.ds(2 * first + half, peers, stride=2), :] = rows[half]
        return total

    blocks = back.shape[0] // (2 * peers)
    total = local_totals[...]
    totals[...] = block(0, total) if blocks == 1 else lax.fori_loop(0, blocks, block, total)


def final_kernel(back, totals, gradient, hess, *, per_frag):
    devices = back.shape[0] // 2
    frags = gradient.shape[1]
    index = lax.bitwise_and(iota(1), frags - 1) * GROUP + iota(0)
    halves = []
    for half in range(2):
        tile = back[pl.ds(half, SUB, stride=2), :]
        for q in range(SUB, devices, SUB):
            tile = tile + back[pl.ds(2 * q + half, SUB, stride=2), :]
        halves.append(jnp.sum(tile, axis=0, keepdims=True))
    parts = [pick(halves[0], index), pick(halves[0], index + SUB), pick(halves[1], index)]
    total = jnp.concatenate(parts, axis=0)[0:18, 0:frags] + totals[...]
    gradient[...] = total[0:6, :] * (1.0 / LANE)
    for v in range(2):
        part = total[6 + 6 * v : 12 + 6 * v, :] * (1.0 / (LANE * per_frag))
        for j in range(6):
            hess[j, v : v + 1, :] = part[j : j + 1, :]


def call(kernel, outs, scratch, spaces, limit=VMEM_LIMIT, out_space="v", **more):
    kinds = {"v": pltpu.VMEM, "s": pltpu.SMEM, "h": pltpu.HBM}
    return pl.pallas_call(
        kernel,
        out_shape=outs,
        in_specs=[pl.BlockSpec(memory_space=kinds[s]) for s in spaces],
        out_specs=[pl.BlockSpec(memory_space=kinds[out_space])] * len(outs),
        scratch_shapes=scratch,
        compiler_params=pltpu.CompilerParams(vmem_limit_bytes=limit),
        **more,
    )


def in_hbm(values):
    return pltpu.with_memory_space_constraint(values, pltpu.HBM)


def exchange(rows, devices):
    sent = rows.reshape(devices, 1, -1)
    sent = lax.all_to_all(sent, ORDER, split_axis=0, concat_axis=0, tiled=True)
    return sent.reshape(rows.shape)


def local(
    points, normals, poses, directions, local_pairs, local_maps,
    remote_src, remote_maps, remote_dst, counts,
):
    sizes = lax.axis_size("tile"), lax.axis_size("band")
    devices = sizes[0] * sizes[1]
    blocks, _, count = points.shape
    frags = poses.shape[1]
    slots = remote_src.shape[1]
    pairs = local_pairs.shape[1]
    assert count == LANE and frags == SUB and slots == devices * SUB and devices % PEERS == 0
    per_frag = blocks // frags
    stride = blocks + SUB
    f32 = jnp.float32
    points = points.transpose(1, 0, 2)
    normals = normals.transpose(1, 0, 2)
    directions = directions.transpose(1, 0, 2)

    def array(*shape, dtype=f32):
        return jax.ShapeDtypeStruct(shape, dtype)

    def vmem(*shape, dtype=f32):
        return pltpu.VMEM(shape, dtype)

    i32, bf16 = jnp.int32, jnp.bfloat16
    part = PEERS * SUB
    (message,) = call(
        functools.partial(pack_kernel, sizes=sizes),
        [array(devices * MSG, LANE)],
        [
            vmem(3, blocks, LANE),
            pltpu.SMEM((6, frags), f32),
            vmem(6, 2, frags),
            pltpu.SMEM((1, slots), i32),
            vmem(1, slots, dtype=i32),
            vmem(slots, LANE, dtype=i32),
            vmem(1, devices, dtype=i32),
            vmem(3 * stride, LANE),
            vmem(12 * frags * SUB, LANE),
            vmem(2 * SUB, LANE),
            vmem(devices * MSG, LANE),
            pltpu.SemaphoreType.DMA((9,)),
            pltpu.SemaphoreType.DMA((devices // SUB,)),
        ],
        "hhhhhh",
        limit=PACK_LIMIT,
        out_space="h",
    )(*[in_hbm(x) for x in (points, poses, directions, remote_src, remote_maps[0], counts)])
    arrived = exchange(message, devices)
    staged, remote_b, remote_frag, totals, same, gather, place, mine = call(
        functools.partial(local_kernel, sizes=sizes),
        [
            array(devices * TARGET, LANE),
            array(2 * SUB, slots),
            array(1, slots, dtype=i32),
            array(18, frags),
            array(LANE, 2 * LANE, dtype=bf16),
            array(GROUP, 2 * LANE, dtype=bf16),
            array(2 * ROWS, 2 * LANE, dtype=bf16),
            array(PEERS, part, dtype=bf16),
        ],
        [
            vmem(6 * stride, LANE),
            vmem(12 * frags * SUB, LANE),
            vmem(2 * SUB, LANE),
            vmem(pairs // SUB * SOURCE, LANE),
            vmem(pairs // SUB * TARGET, LANE),
            vmem(2 * SUB, pairs),
            vmem(2 * SUB, pairs),
            vmem(3 * SUB, pairs),
            vmem(pairs, 6 * 2 * LANE, dtype=bf16),
            vmem(9 * LANE, pairs),
            vmem(pairs // LANE * ROWS * SUB, LANE),
        ],
        "vvsvsvvsv",
        cost_estimate=pl.CostEstimate(
            flops=200 * pairs * LANE, bytes_accessed=4_000_000, transcendentals=0
        ),
    )(
        points, normals, poses, directions, local_pairs, local_pairs, local_maps,
        remote_dst, remote_dst,
    )
    back, totals = call(
        remote_kernel,
        [array(devices * 2, LANE), array(18, frags)],
        [
            vmem(2 * SUB, part),
            vmem(3 * SUB, part),
            vmem(part, LANE),
            vmem(part, LANE, dtype=i32),
            vmem(part, 7 * 2 * LANE, dtype=bf16),
            vmem(9 * LANE, part),
            vmem(part // LANE * ROWS * SUB, LANE),
        ],
        "vvvvvvvvv",
    )(arrived, staged, remote_b, remote_frag, totals, same, gather, place, mine)
    back = exchange(back, devices)
    gradient, hess = call(
        functools.partial(final_kernel, per_frag=per_frag),
        [array(6, frags), array(6, 2, frags)],
        [],
        "vv",
    )(back, totals)
    return (gradient, hess.transpose(1, 0, 2))


def solution(mesh):
    placed = (
        P(AXES, None, None),
        P(AXES, None, None),
        P(None, AXES),
        P(None, None, AXES),
        P(None, AXES),
        P(AXES, None),
        P(AXES, None),
        P(AXES, None, None),
        P(AXES, None),
        P(AXES, None),
    )
    return jax.shard_map(
        local,
        mesh=mesh,
        in_specs=placed,
        out_specs=(P(None, AXES), P(None, None, AXES)),
        check_vma=False,
    )
```

```python
import functools

import jax
import jax.numpy as jnp
from jax import lax
from jax.experimental import pallas as pl
from jax.experimental.pallas import tpu as pltpu
from jax.sharding import PartitionSpec as P

AXES = ("tile", "band")
ORDER = ("band", "tile")
SUB = 8
LANE = 128
MSG = 4 * SUB + 1
TARGET = 6 * SUB
SOURCE = 3 * SUB
ROWS = 32
GROUP = 16
VMEM_LIMIT = 16 * 1024 * 1024
PACK_LIMIT = 56 * 1024 * 1024
PEERS = 32


def iota(axis):
    return lax.broadcasted_iota(jnp.int32, (SUB, LANE), axis)


def pick(values, index):
    values = jnp.broadcast_to(values, (SUB, LANE))
    return jnp.take_along_axis(values, index, axis=1, mode="promise_in_bounds")


def shift_of(size):
    shift = size.bit_length() - 1
    assert 1 << shift == size
    return shift


def cross(left, right):
    return [
        left[1] * right[2] - left[2] * right[1],
        left[2] * right[0] - left[0] * right[2],
        left[0] * right[1] - left[1] * right[0],
    ]


def dot3(left, right):
    return left[0] * right[0] + left[1] * right[1] + left[2] * right[2]


def splat_rotation(poses, f):
    half = [jnp.full((SUB, LANE), poses[i, f] * 0.5, jnp.float32) for i in range(3)]
    w = 1.0 / jnp.sqrt(1.0 + half[0] * half[0] + half[1] * half[1] + half[2] * half[2])
    x, y, z = half[0] * w, half[1] * w, half[2] * w
    rotation = [
        [1.0 - 2.0 * (y * y + z * z), 2.0 * (x * y - w * z), 2.0 * (x * z + w * y)],
        [2.0 * (x * y + w * z), 1.0 - 2.0 * (x * x + z * z), 2.0 * (y * z - w * x)],
        [2.0 * (x * z - w * y), 2.0 * (y * z + w * x), 1.0 - 2.0 * (x * x + y * y)],
    ]
    return rotation, [jnp.full((SUB, LANE), poses[i, f], jnp.float32) for i in range(3, 6)]


def write_rotations(poses, turns):
    for f in range(poses.shape[1]):
        rotation, move = splat_rotation(poses, f)
        for i, tile in enumerate(rotation[0] + rotation[1] + rotation[2] + move):
            at = (12 * f + i) * SUB
            turns[at : at + SUB, :] = tile


def write_world(fields, turns, world, frags):
    blocks = fields[0].shape[1]
    total = turns.shape[0] // (12 * SUB)
    per_frag, stride = blocks // total, blocks + SUB
    for f in frags:
        tile = [turns[(12 * f + i) * SUB : (12 * f + i + 1) * SUB, :] for i in range(12)]
        for b in range(f * per_frag, (f + 1) * per_frag, SUB):
            for at, field in enumerate(fields):
                x = [field[j, b : b + SUB, :] for j in range(3)]
                for i in range(3):
                    row = dot3(tile[3 * i : 3 * i + 3], x)
                    if at == 0:
                        row = row + tile[9 + i]
                    world[pl.ds((3 * at + i) * stride + b, SUB), :] = row


def write_directions(directions, table):
    frags = directions.shape[2]
    for v in range(2):
        for j in range(6):
            table[6 * v + j : 6 * v + j + 1, 0:frags] = directions[j, v : v + 1, :]


def peer_at(place, sizes):
    n_tile, n_band = sizes
    if isinstance(place, int):
        return place % n_tile * n_band + place // n_tile
    tile = lax.bitwise_and(place, n_tile - 1)
    return tile * n_band + lax.shift_right_logical(place, shift_of(n_tile))


def entries(row_ref, index):
    out = jnp.zeros((SUB, LANE), row_ref.dtype)
    tile = lax.shift_right_logical(index, shift_of(LANE))
    for t in range(row_ref.shape[1] // LANE):
        hit = pick(row_ref[0:1, t * LANE : (t + 1) * LANE], lax.bitwise_and(index, LANE - 1))
        out = jnp.where(tile == t, hit, out)
    return out


def pack_kernel(
    points_h, poses_h, directions_h, src_h, maps_h, counts_h, out_h,
    points, poses, directions, src_s, src_v, maps, used, world, turns, table, out, sems, out_sems, *, sizes,
):
    devices = counts_h.shape[1]
    per_frag = points.shape[1] // poses.shape[1]
    stride = points.shape[1] + SUB
    frags = poses.shape[1]
    pairs = [(directions_h, directions), (src_h, src_v), (counts_h, used), (poses_h, poses)]
    pairs += [(points_h.at[j], points.at[j]) for j in range(3)]
    pairs += [(src_h, src_s), (maps_h, maps)]
    copies = [pltpu.make_async_copy(a, b, sems.at[i]) for i, (a, b) in enumerate(pairs)]
    for copy in copies:
        copy.start()
    for copy in copies[0:3]:
        copy.wait()
    write_directions(directions, table)
    limits = jnp.broadcast_to(used[0:1, :], (SUB, devices)).astype(jnp.float32)
    peers = lax.broadcasted_iota(jnp.int32, (SUB, devices), 1)
    row = lax.broadcasted_iota(jnp.int32, (SUB, devices), 0)
    slot = lax.shift_right_logical(iota(1), shift_of(GROUP))
    field = lax.bitwise_and(iota(1), GROUP - 1)
    for q in range(0, devices, SUB):
        block = entries(src_v, peer_at(iota(0) + q, sizes) * SUB + slot)
        frag = lax.shift_right_logical(block, shift_of(per_frag))
        hit = peers == peer_at(row + q, sizes)
        limit = jnp.sum(jnp.where(hit, limits, 0.0), axis=1, keepdims=True)
        extras = jnp.where(slot.astype(jnp.float32) < limit, 1.0, 0.0)
        for j in range(12):
            extras = jnp.where(field == j, pick(table[j : j + 1, :], frag), extras)
        extras = jnp.where(field == 13, frag.astype(jnp.float32), extras)
        out[pl.ds(q * MSG + MSG - 1, SUB, stride=MSG), :] = extras
    copies[3].wait()
    write_rotations(poses, turns)
    for copy in copies[4:7]:
        copy.wait()
    write_world([points], turns, world, range(frags))
    for copy in copies[7:]:
        copy.wait()

    def peer(q):
        p = peer_at(q, sizes)
        for s in range(SUB):
            block = src_s[0, p * SUB + s]
            out[pl.ds(q * MSG + s, 3, stride=SUB), :] = world[pl.ds(block, 3, stride=stride), :]
        rows = maps[p * SUB : (p + 1) * SUB, :]
        out[pl.ds(q * MSG + 3 * SUB, SUB), :] = rows.astype(jnp.float32)

    def piece(i):
        rows = pl.ds(i * SUB * MSG, SUB * MSG)
        return pltpu.make_async_copy(out.at[rows], out_h.at[rows], out_sems.at[i])

    for i in range(devices // SUB):
        for u in range(SUB):
            peer(i * SUB + u)
        piece(i).start()
    for i in range(devices // SUB):
        piece(i).wait()


def halves_of(values):
    high = values.astype(jnp.bfloat16)
    return high, (values - high.astype(jnp.float32)).astype(jnp.bfloat16)


def turn_steps(at, left, parts, i, t, put):
    first, second = i * 2 * LANE, i * 2 * LANE + LANE

    def split(u):
        high, low = halves_of(jnp.concatenate([at(u), at(u + 1)], axis=0))
        parts[u * SUB : (u + 2) * SUB, first : first + LANE] = high
        parts[u * SUB : (u + 2) * SUB, second : second + LANE] = low

    def multiply():
        put(
            lax.dot_general(
                left,
                parts[t : t + LANE, first : second + LANE],
                (((1,), (1,)), ((), ())),
                preferred_element_type=jnp.float32,
            )
        )

    tiles = range(t // SUB, (t + LANE) // SUB, 2)
    return [functools.partial(split, u) for u in tiles], multiply


def field_steps(source, target, index, same, parts, turned, t):
    def put(k, value):
        turned[k * LANE : (k + 1) * LANE, t : t + LANE] = value

    def turn_source(k):
        tiles = [source(u, k) for u in range(t // SUB, (t + LANE) // SUB)]
        put(6 + k, jnp.concatenate(tiles, axis=0).T)

    splits, products = [], []
    for k in range(6):

        def at(u, k=k):
            return pick(target(u, k), index(u))

        split, product = turn_steps(at, same, parts, k, t, functools.partial(put, k))
        splits.append(split)
        products.append(product)
    steps = [split[u] for u in range(len(splits[0])) for split in splits]
    return steps + products + [functools.partial(turn_source, k) for k in range(3)]


def run(steps):
    for step in steps:
        step()


def join_directions(side_a, side_b, joined, lanes, lanes_b):
    joined[0:12, lanes] = side_a[0:12, lanes]
    for v in range(2):
        turn_rows, move_rows = slice(6 * v, 6 * v + 3), slice(6 * v + 3, 6 * v + 6)
        joined[move_rows, lanes] = side_a[move_rows, lanes] - side_b[move_rows, lanes_b]
        joined[12 + 3 * v : 15 + 3 * v, lanes] = side_b[turn_rows, lanes_b]


def point_sums(turned, joined, partial, t, between=()):
    lanes = slice(t, t + LANE)
    first = t // LANE * ROWS * SUB
    zero = jnp.zeros((SUB, LANE), jnp.float32)
    totals = [zero] * 27
    rounds = LANE // SUB
    for i in range(rounds):
        field = [turned[i * SUB + k * LANE : (i + 1) * SUB + k * LANE, lanes] for k in range(9)]
        way = [joined[j : j + 1, lanes] for j in range(18)]
        y, n, x = field[0:3], field[3:6], field[6:9]
        p, q = cross(x, n), cross(y, n)
        scalars = [dot3(n, [x[k] - y[k] for k in range(3)])]
        for v in range(2):
            a, b = way[6 * v : 6 * v + 6], way[12 + 3 * v : 15 + 3 * v]
            scalars.append(dot3(p, a[0:3]) + dot3(n, a[3:6]) - dot3(q, b))
        terms = []
        for s in scalars:
            terms += [s * value for value in p + n]
        for s in scalars:
            terms += [s * value for value in q]
        totals = [total + term for total, term in zip(totals, terms)]
        run(between[i * len(between) // rounds : (i + 1) * len(between) // rounds])
    for j in range(ROWS):
        partial[first + j * SUB : first + (j + 1) * SUB, :] = totals[j] if j < 27 else zero
    total = partial[pl.ds(first, ROWS, stride=SUB), :]
    for s in range(1, SUB):
        total = total + partial[pl.ds(first + s, ROWS, stride=SUB), :]
    return total


def frag_of(row, per_frag):
    return lax.shift_right_logical(row, shift_of(per_frag))


def look_up(table, frag, out):
    for at in range(0, frag.shape[1], LANE):
        index = jnp.broadcast_to(frag[:, at : at + LANE], (SUB, LANE))
        for j in range(0, 2 * SUB, SUB):
            out[j : j + SUB, at : at + LANE] = pick(table[j : j + SUB, :], index)


def by_frag(sums, frag):
    pairs = sums.shape[1]
    hot = jnp.broadcast_to(frag, (SUB, pairs)) == lax.broadcasted_iota(jnp.int32, (SUB, pairs), 0)
    return lax.dot_general(
        sums,
        hot.astype(jnp.float32),
        (((1,), (1,)), ((), ())),
        precision=lax.Precision.HIGHEST,
        preferred_element_type=jnp.float32,
    )


def target_side(total):
    rows = []
    for k in range(3):
        rows += [total[18 + 3 * k : 21 + 3 * k, :], total[6 * k + 3 : 6 * k + 6, :]]
    return -jnp.concatenate(rows, axis=0)


def constants(same, gather, place, mine):
    def wide(ref, axis):
        return lax.broadcasted_iota(jnp.int32, ref.shape, axis)

    def put(ref, hit):
        ref[...] = hit.astype(jnp.float32).astype(jnp.bfloat16)

    put(same, lax.bitwise_and(wide(same, 1), LANE - 1) == wide(same, 0))
    put(gather, lax.bitwise_and(wide(gather, 1), GROUP - 1) == wide(gather, 0))
    entry = lax.bitwise_and(wide(place, 1), GROUP - 1) + GROUP * lax.shift_right_logical(
        wide(place, 1), shift_of(LANE)
    )
    put(place, lax.bitwise_and(wide(place, 0), ROWS - 1) == entry)
    put(mine, lax.shift_right_logical(wide(mine, 1), shift_of(SUB)) == wide(mine, 0))


def local_kernel(
    points, normals, poses, directions, pairs_s, pairs_v, maps, dst_s, dst_v,
    staged, remote_b, remote_frag, totals, same, gather, place, mine,
    world, turns, table, sources, targets, side_a, side_b, joined, parts, turned, partial, *, sizes,
):
    per_frag = points.shape[1] // poses.shape[1]
    stride = points.shape[1] + SUB
    constants(same, gather, place, mine)
    table[...] = jnp.zeros_like(table)
    write_directions(directions, table)
    for at in range(0, dst_v.shape[1], LANE):
        flat = iota(1) + at
        peer = peer_at(lax.shift_right_logical(flat, shift_of(SUB)), sizes)
        block = entries(dst_v, peer * SUB + lax.bitwise_and(flat, SUB - 1))
        remote_frag[0:1, at : at + LANE] = frag_of(block, per_frag)[0:1, :]
    look_up(table, remote_frag[...], remote_b)
    frag_a, frag_b = frag_of(pairs_v[0:1, :], per_frag), frag_of(pairs_v[1:2, :], per_frag)
    look_up(table, frag_a, side_a)
    look_up(table, frag_b, side_b)
    every = slice(0, pairs_s.shape[1])
    join_directions(side_a, side_b, joined, every, every)
    write_rotations(poses, turns)
    write_world([points, normals], turns, world, range(poses.shape[1]))

    def stage_remote(g, carry):
        for s in range(SUB):
            block = dst_s[0, peer_at(g, sizes) * SUB + s]
            staged[pl.ds(g * TARGET + s, 6, stride=SUB), :] = world[pl.ds(block, 6, stride=stride), :]
        return carry

    lax.fori_loop(0, dst_s.shape[1] // SUB, stage_remote, 0, unroll=4)

    def stage_local(g, carry):
        for s in range(SUB):
            a, b = pairs_s[0, g * SUB + s], pairs_s[1, g * SUB + s]
            targets[pl.ds(g * TARGET + s, 6, stride=SUB), :] = world[pl.ds(b, 6, stride=stride), :]
            sources[pl.ds(g * SOURCE + s, 3, stride=SUB), :] = world[pl.ds(a, 3, stride=stride), :]
        return carry

    lax.fori_loop(0, pairs_s.shape[1] // SUB, stage_local, 0, unroll=4)
    total = jnp.zeros(totals.shape, jnp.float32)
    tiles = range(0, pairs_s.shape[1], LANE)
    steps = [
        field_steps(
            lambda u, k: sources[u * SOURCE + k * SUB : u * SOURCE + (k + 1) * SUB, :],
            lambda u, k: targets[u * TARGET + k * SUB : u * TARGET + (k + 1) * SUB, :],
            lambda u: maps[u * SUB : (u + 1) * SUB, :],
            same[...],
            parts,
            turned,
            t,
        )
        for t in tiles
    ]
    run(steps[0])
    for i, t in enumerate(tiles):
        between = steps[i + 1] if i + 1 < len(steps) else ()
        sums = point_sums(turned, joined, partial, t, between)
        total = total + by_frag(sums, frag_a[:, t : t + LANE])[0:18, :]
        total = total + target_side(by_frag(sums, frag_b[:, t : t + LANE]))
    totals[...] = total


def fetch_local(*refs, inputs, outputs, sizes):
    far, outs, rest = refs[:inputs], refs[inputs : inputs + outputs], refs[inputs + outputs :]
    near, scratch, sems = rest[:inputs], rest[inputs:-1], rest[-1]
    copies = [pltpu.make_async_copy(a, b, sems.at[i]) for i, (a, b) in enumerate(zip(far, near))]
    for copy in copies:
        copy.start()
    for copy in copies:
        copy.wait()
    local_kernel(*near, *outs, *scratch, sizes=sizes)


def remote_kernel(
    arrived, staged, remote_b, remote_frag, local_totals, same, gather, place, mine,
    back, totals, side_a, joined, frags, index, parts, turned, partial,
):
    f32 = jnp.float32
    pairs = parts.shape[0]
    peers = pairs // SUB
    own = lax.shift_right_logical(iota(1), shift_of(GROUP)) == iota(0)
    slot = lax.shift_right_logical(iota(1), shift_of(GROUP)).astype(f32)[0:1, :]

    def block(c, total):
        first = c * peers
        start = c * pairs if isinstance(c, int) else pl.multiple_of(c * pairs, LANE)

        def row_at(u, size, row):
            at = (first + u) * size + row
            return at if isinstance(c, int) or size == MSG else pl.multiple_of(at, SUB)

        def extras(u):
            row = arrived[pl.ds(row_at(u, MSG, 4 * SUB), 1), :]
            frags[u * SUB : (u + 1) * SUB, :] = pick(row, iota(0) * GROUP + 13)
            return jnp.where(own, jnp.broadcast_to(row, (SUB, LANE)), 0.0)

        def front(t):
            lanes = slice(t, t + LANE)

            def indices():
                for u in range(t // SUB, (t + LANE) // SUB):
                    rows = arrived[pl.ds(row_at(u, MSG, 3 * SUB), SUB), :]
                    index[u * SUB : (u + 1) * SUB, :] = rows.astype(jnp.int32)

            def put(value):
                side_a[:, lanes] = value
                join_directions(side_a, remote_b, joined, lanes, pl.ds(start + t, LANE))

            split, product = turn_steps(extras, gather[...], parts, 6, t, put)
            return (
                [indices]
                + split
                + [product]
                + field_steps(
                    lambda u, k: arrived[pl.ds(row_at(u, MSG, SUB * k), SUB), :],
                    lambda u, k: staged[pl.ds(row_at(u, TARGET, SUB * k), SUB), :],
                    lambda u: index[u * SUB : (u + 1) * SUB, :],
                    same[...],
                    parts,
                    turned,
                    t,
                )
            )

        rows = [jnp.zeros((peers, LANE), f32) for half in range(2)]

        def back_steps(sums, t):
            lanes = slice(t, t + LANE)
            held = {}
            both = jnp.concatenate(halves_of(sums), axis=0)

            def scatter():
                held["placed"] = lax.dot_general(
                    both,
                    place[...],
                    (((0,), (0,)), ((), ())),
                    preferred_element_type=f32,
                )

            def add(half):
                hit = frags[lanes, :] == jnp.broadcast_to(slot, (LANE, LANE))
                part = jnp.where(hit, held["placed"][:, half * LANE : (half + 1) * LANE], 0.0)
                for piece in halves_of(part):
                    rows[half] = rows[half] + jnp.dot(
                        mine[:, lanes], piece, preferred_element_type=f32
                    )

            def own_side():
                frag = remote_frag[0:1, pl.ds(start + t, LANE)]
                hot = jnp.broadcast_to(frag, (SUB, LANE)) == iota(0)
                added = lax.dot_general(
                    both,
                    hot.astype(f32).astype(jnp.bfloat16),
                    (((1,), (1,)), ((), ())),
                    preferred_element_type=f32,
                )
                held["total"] = target_side(added[0:ROWS, :] + added[ROWS:, :])

            return [scatter, functools.partial(add, 0), functools.partial(add, 1), own_side], held

        tiles = range(0, pairs, LANE)
        steps = front(tiles[0])
        run(steps)
        behind, held = [], []
        for t in tiles:
            between = behind + (front(t + LANE) if t + LANE < pairs else [])
            sums = point_sums(turned, joined, partial, t, between)
            sums = sums * side_a[12:13, t : t + LANE]
            behind, kept = back_steps(sums, t)
            held.append(kept)
        run(behind)
        for kept in held:
            total = total + kept["total"]
        for half in range(2):
            back[pl.ds(2 * first + half, peers, stride=2), :] = rows[half]
        return total

    blocks = back.shape[0] // (2 * peers)
    total = local_totals[...]
    totals[...] = block(0, total) if blocks == 1 else lax.fori_loop(0, blocks, block, total)


def final_kernel(back, totals, gradient, hess, *, per_frag):
    devices = back.shape[0] // 2
    frags = gradient.shape[1]
    index = lax.bitwise_and(iota(1), frags - 1) * GROUP + iota(0)
    halves = []
    for half in range(2):
        tile = back[pl.ds(half, SUB, stride=2), :]
        for q in range(SUB, devices, SUB):
            tile = tile + back[pl.ds(2 * q + half, SUB, stride=2), :]
        halves.append(jnp.sum(tile, axis=0, keepdims=True))
    parts = [pick(halves[0], index), pick(halves[0], index + SUB), pick(halves[1], index)]
    total = jnp.concatenate(parts, axis=0)[0:18, 0:frags] + totals[...]
    gradient[...] = total[0:6, :] * (1.0 / LANE)
    for v in range(2):
        part = total[6 + 6 * v : 12 + 6 * v, :] * (1.0 / (LANE * per_frag))
        for j in range(6):
            hess[j, v : v + 1, :] = part[j : j + 1, :]


def call(kernel, outs, scratch, spaces, limit=VMEM_LIMIT, out_space="v", **more):
    kinds = {"v": pltpu.VMEM, "s": pltpu.SMEM, "h": pltpu.HBM}
    return pl.pallas_call(
        kernel,
        out_shape=outs,
        in_specs=[pl.BlockSpec(memory_space=kinds[s]) for s in spaces],
        out_specs=[pl.BlockSpec(memory_space=kinds[out_space])] * len(outs),
        scratch_shapes=scratch,
        compiler_params=pltpu.CompilerParams(vmem_limit_bytes=limit),
        **more,
    )


def in_hbm(values):
    return pltpu.with_memory_space_constraint(values, pltpu.HBM)


def exchange(rows, devices):
    sent = rows.reshape(devices, 1, -1)
    sent = lax.all_to_all(sent, ORDER, split_axis=0, concat_axis=0, tiled=True)
    return sent.reshape(rows.shape)


def local(
    points, normals, poses, directions, local_pairs, local_maps,
    remote_src, remote_maps, remote_dst, counts,
):
    sizes = lax.axis_size("tile"), lax.axis_size("band")
    devices = sizes[0] * sizes[1]
    blocks, _, count = points.shape
    frags = poses.shape[1]
    slots = remote_src.shape[1]
    pairs = local_pairs.shape[1]
    assert count == LANE and frags == SUB and slots == devices * SUB and devices % PEERS == 0
    per_frag = blocks // frags
    stride = blocks + SUB
    f32 = jnp.float32
    points = points.transpose(1, 0, 2)
    normals = normals.transpose(1, 0, 2)
    directions = directions.transpose(1, 0, 2)

    def array(*shape, dtype=f32):
        return jax.ShapeDtypeStruct(shape, dtype)

    def vmem(*shape, dtype=f32):
        return pltpu.VMEM(shape, dtype)

    i32, bf16 = jnp.int32, jnp.bfloat16
    part = PEERS * SUB
    (message,) = call(
        functools.partial(pack_kernel, sizes=sizes),
        [array(devices * MSG, LANE)],
        [
            vmem(3, blocks, LANE),
            pltpu.SMEM((6, frags), f32),
            vmem(6, 2, frags),
            pltpu.SMEM((1, slots), i32),
            vmem(1, slots, dtype=i32),
            vmem(slots, LANE, dtype=i32),
            vmem(1, devices, dtype=i32),
            vmem(3 * stride, LANE),
            vmem(12 * frags * SUB, LANE),
            vmem(2 * SUB, LANE),
            vmem(devices * MSG, LANE),
            pltpu.SemaphoreType.DMA((9,)),
            pltpu.SemaphoreType.DMA((devices // SUB,)),
        ],
        "hhhhhh",
        limit=PACK_LIMIT,
        out_space="h",
    )(*[in_hbm(x) for x in (points, poses, directions, remote_src, remote_maps[0], counts)])
    arrived = exchange(message, devices)
    staged, remote_b, remote_frag, totals, same, gather, place, mine = call(
        functools.partial(fetch_local, inputs=9, outputs=8, sizes=sizes),
        [
            array(devices * TARGET, LANE),
            array(2 * SUB, slots),
            array(1, slots, dtype=i32),
            array(18, frags),
            array(LANE, 2 * LANE, dtype=bf16),
            array(GROUP, 2 * LANE, dtype=bf16),
            array(2 * ROWS, 2 * LANE, dtype=bf16),
            array(PEERS, part, dtype=bf16),
        ],
        [
            vmem(3, blocks, LANE),
            vmem(3, blocks, LANE),
            pltpu.SMEM((6, frags), f32),
            vmem(6, 2, frags),
            pltpu.SMEM((2, pairs), i32),
            vmem(2, pairs, dtype=i32),
            vmem(pairs, LANE, dtype=i32),
            pltpu.SMEM((1, slots), i32),
            vmem(1, slots, dtype=i32),
            vmem(6 * stride, LANE),
            vmem(12 * frags * SUB, LANE),
            vmem(2 * SUB, LANE),
            vmem(pairs // SUB * SOURCE, LANE),
            vmem(pairs // SUB * TARGET, LANE),
            vmem(2 * SUB, pairs),
            vmem(2 * SUB, pairs),
            vmem(3 * SUB, pairs),
            vmem(pairs, 6 * 2 * LANE, dtype=bf16),
            vmem(9 * LANE, pairs),
            vmem(pairs // LANE * ROWS * SUB, LANE),
            pltpu.SemaphoreType.DMA((9,)),
        ],
        "hhhhhhhhh",
        cost_estimate=pl.CostEstimate(
            flops=200 * pairs * LANE, bytes_accessed=4_000_000, transcendentals=0
        ),
    )(
        *[
            in_hbm(x)
            for x in (
                points, normals, poses, directions, local_pairs, local_pairs, local_maps,
                remote_dst, remote_dst,
            )
        ]
    )
    back, totals = call(
        remote_kernel,
        [array(devices * 2, LANE), array(18, frags)],
        [
            vmem(2 * SUB, part),
            vmem(3 * SUB, part),
            vmem(part, LANE),
            vmem(part, LANE, dtype=i32),
            vmem(part, 7 * 2 * LANE, dtype=bf16),
            vmem(9 * LANE, part),
            vmem(part // LANE * ROWS * SUB, LANE),
        ],
        "vvvvvvvvv",
    )(arrived, staged, remote_b, remote_frag, totals, same, gather, place, mine)
    back = exchange(back, devices)
    gradient, hess = call(
        functools.partial(final_kernel, per_frag=per_frag),
        [array(6, frags), array(6, 2, frags)],
        [],
        "vv",
    )(back, totals)
    return (gradient, hess.transpose(1, 0, 2))


def solution(mesh):
    placed = (
        P(AXES, None, None),
        P(AXES, None, None),
        P(None, AXES),
        P(None, None, AXES),
        P(None, AXES),
        P(AXES, None),
        P(AXES, None),
        P(AXES, None, None),
        P(AXES, None),
        P(AXES, None),
    )
    return jax.shard_map(
        local,
        mesh=mesh,
        in_specs=placed,
        out_specs=(P(None, AXES), P(None, None, AXES)),
        check_vma=False,
    )
```

```python
import functools

import jax
import jax.numpy as jnp
from jax import lax
from jax.experimental import pallas as pl
from jax.experimental.pallas import tpu as pltpu
from jax.sharding import PartitionSpec as P

AXES = ("tile", "band")
ORDER = ("band", "tile")
SUB = 8
LANE = 128
MSG = 4 * SUB + 1
TARGET = 6 * SUB
SOURCE = 3 * SUB
ROWS = 32
GROUP = 16
VMEM_LIMIT = 16 * 1024 * 1024
PACK_LIMIT = 56 * 1024 * 1024
PEERS = 32


def iota(axis):
    return lax.broadcasted_iota(jnp.int32, (SUB, LANE), axis)


def pick(values, index):
    values = jnp.broadcast_to(values, (SUB, LANE))
    return jnp.take_along_axis(values, index, axis=1, mode="promise_in_bounds")


def shift_of(size):
    shift = size.bit_length() - 1
    assert 1 << shift == size
    return shift


def cross(left, right):
    return [
        left[1] * right[2] - left[2] * right[1],
        left[2] * right[0] - left[0] * right[2],
        left[0] * right[1] - left[1] * right[0],
    ]


def dot3(left, right):
    return left[0] * right[0] + left[1] * right[1] + left[2] * right[2]


def splat_rotation(poses, f):
    half = [jnp.full((SUB, LANE), poses[i, f] * 0.5, jnp.float32) for i in range(3)]
    w = 1.0 / jnp.sqrt(1.0 + half[0] * half[0] + half[1] * half[1] + half[2] * half[2])
    x, y, z = half[0] * w, half[1] * w, half[2] * w
    rotation = [
        [1.0 - 2.0 * (y * y + z * z), 2.0 * (x * y - w * z), 2.0 * (x * z + w * y)],
        [2.0 * (x * y + w * z), 1.0 - 2.0 * (x * x + z * z), 2.0 * (y * z - w * x)],
        [2.0 * (x * z - w * y), 2.0 * (y * z + w * x), 1.0 - 2.0 * (x * x + y * y)],
    ]
    return rotation, [jnp.full((SUB, LANE), poses[i, f], jnp.float32) for i in range(3, 6)]


def write_rotations(poses, turns):
    for f in range(poses.shape[1]):
        rotation, move = splat_rotation(poses, f)
        for i, tile in enumerate(rotation[0] + rotation[1] + rotation[2] + move):
            at = (12 * f + i) * SUB
            turns[at : at + SUB, :] = tile


def write_world(fields, turns, world, frags):
    blocks = fields[0].shape[1]
    total = turns.shape[0] // (12 * SUB)
    per_frag, stride = blocks // total, blocks + SUB
    for f in frags:
        tile = [turns[(12 * f + i) * SUB : (12 * f + i + 1) * SUB, :] for i in range(12)]
        for b in range(f * per_frag, (f + 1) * per_frag, SUB):
            for at, field in enumerate(fields):
                x = [field[j, b : b + SUB, :] for j in range(3)]
                for i in range(3):
                    row = dot3(tile[3 * i : 3 * i + 3], x)
                    if at == 0:
                        row = row + tile[9 + i]
                    world[pl.ds((3 * at + i) * stride + b, SUB), :] = row


def write_directions(directions, table):
    frags = directions.shape[2]
    for v in range(2):
        for j in range(6):
            table[6 * v + j : 6 * v + j + 1, 0:frags] = directions[j, v : v + 1, :]


def peer_at(place, sizes):
    n_tile, n_band = sizes
    if isinstance(place, int):
        return place % n_tile * n_band + place // n_tile
    tile = lax.bitwise_and(place, n_tile - 1)
    return tile * n_band + lax.shift_right_logical(place, shift_of(n_tile))


def entries(row_ref, index):
    out = jnp.zeros((SUB, LANE), row_ref.dtype)
    tile = lax.shift_right_logical(index, shift_of(LANE))
    for t in range(row_ref.shape[1] // LANE):
        hit = pick(row_ref[0:1, t * LANE : (t + 1) * LANE], lax.bitwise_and(index, LANE - 1))
        out = jnp.where(tile == t, hit, out)
    return out


def pack_kernel(
    points_h, poses_h, directions_h, src_h, maps_h, counts_h, out_h,
    points, poses, directions, src_s, src_v, maps, used, world, turns, table, out, sems, out_sems, *, sizes,
):
    devices = counts_h.shape[1]
    per_frag = points.shape[1] // poses.shape[1]
    stride = points.shape[1] + SUB
    frags = poses.shape[1]
    pairs = [(directions_h, directions), (src_h, src_v), (counts_h, used), (poses_h, poses)]
    pairs += [(points_h.at[j], points.at[j]) for j in range(3)]
    pairs += [(src_h, src_s), (maps_h, maps)]
    copies = [pltpu.make_async_copy(a, b, sems.at[i]) for i, (a, b) in enumerate(pairs)]
    for copy in copies:
        copy.start()
    for copy in copies[0:3]:
        copy.wait()
    write_directions(directions, table)
    limits = jnp.broadcast_to(used[0:1, :], (SUB, devices)).astype(jnp.float32)
    peers = lax.broadcasted_iota(jnp.int32, (SUB, devices), 1)
    row = lax.broadcasted_iota(jnp.int32, (SUB, devices), 0)
    slot = lax.shift_right_logical(iota(1), shift_of(GROUP))
    field = lax.bitwise_and(iota(1), GROUP - 1)
    for q in range(0, devices, SUB):
        block = entries(src_v, peer_at(iota(0) + q, sizes) * SUB + slot)
        frag = lax.shift_right_logical(block, shift_of(per_frag))
        hit = peers == peer_at(row + q, sizes)
        limit = jnp.sum(jnp.where(hit, limits, 0.0), axis=1, keepdims=True)
        extras = jnp.where(slot.astype(jnp.float32) < limit, 1.0, 0.0)
        for j in range(12):
            extras = jnp.where(field == j, pick(table[j : j + 1, :], frag), extras)
        extras = jnp.where(field == 13, frag.astype(jnp.float32), extras)
        out[pl.ds(q * MSG + MSG - 1, SUB, stride=MSG), :] = extras
    copies[3].wait()
    write_rotations(poses, turns)
    for copy in copies[4:7]:
        copy.wait()
    write_world([points], turns, world, range(frags))
    for copy in copies[7:]:
        copy.wait()

    def peer(q):
        p = peer_at(q, sizes)
        for s in range(SUB):
            block = src_s[0, p * SUB + s]
            out[pl.ds(q * MSG + s, 3, stride=SUB), :] = world[pl.ds(block, 3, stride=stride), :]
        rows = maps[p * SUB : (p + 1) * SUB, :]
        out[pl.ds(q * MSG + 3 * SUB, SUB), :] = rows.astype(jnp.float32)

    def piece(i):
        rows = pl.ds(i * SUB * MSG, SUB * MSG)
        return pltpu.make_async_copy(out.at[rows], out_h.at[rows], out_sems.at[i])

    for i in range(devices // SUB):
        for u in range(SUB):
            peer(i * SUB + u)
        piece(i).start()
    for i in range(devices // SUB):
        piece(i).wait()


def halves_of(values):
    high = values.astype(jnp.bfloat16)
    return high, (values - high.astype(jnp.float32)).astype(jnp.bfloat16)


def turn_steps(at, left, parts, i, t, put):
    first, second = i * 2 * LANE, i * 2 * LANE + LANE

    def split(u):
        high, low = halves_of(jnp.concatenate([at(u), at(u + 1)], axis=0))
        parts[u * SUB : (u + 2) * SUB, first : first + LANE] = high
        parts[u * SUB : (u + 2) * SUB, second : second + LANE] = low

    def multiply():
        put(
            lax.dot_general(
                left,
                parts[t : t + LANE, first : second + LANE],
                (((1,), (1,)), ((), ())),
                preferred_element_type=jnp.float32,
            )
        )

    tiles = range(t // SUB, (t + LANE) // SUB, 2)
    return [functools.partial(split, u) for u in tiles], multiply


def field_steps(source, target, index, same, parts, turned, t):
    def put(k, value):
        turned[k * LANE : (k + 1) * LANE, t : t + LANE] = value

    def turn_source(k):
        tiles = [source(u, k) for u in range(t // SUB, (t + LANE) // SUB)]
        put(6 + k, jnp.concatenate(tiles, axis=0).T)

    splits, products = [], []
    for k in range(6):

        def at(u, k=k):
            return pick(target(u, k), index(u))

        split, product = turn_steps(at, same, parts, k, t, functools.partial(put, k))
        splits.append(split)
        products.append(product)
    steps = [split[u] for u in range(len(splits[0])) for split in splits]
    return steps + products + [functools.partial(turn_source, k) for k in range(3)]


def run(steps):
    for step in steps:
        step()


def join_directions(side_a, side_b, joined, lanes, lanes_b):
    joined[0:12, lanes] = side_a[0:12, lanes]
    for v in range(2):
        turn_rows, move_rows = slice(6 * v, 6 * v + 3), slice(6 * v + 3, 6 * v + 6)
        joined[move_rows, lanes] = side_a[move_rows, lanes] - side_b[move_rows, lanes_b]
        joined[12 + 3 * v : 15 + 3 * v, lanes] = side_b[turn_rows, lanes_b]


def point_sums(turned, joined, partial, t, between=()):
    lanes = slice(t, t + LANE)
    first = t // LANE * ROWS * SUB
    zero = jnp.zeros((SUB, LANE), jnp.float32)
    totals = [zero] * 27
    rounds = LANE // SUB
    for i in range(rounds):
        field = [turned[i * SUB + k * LANE : (i + 1) * SUB + k * LANE, lanes] for k in range(9)]
        way = [joined[j : j + 1, lanes] for j in range(18)]
        y, n, x = field[0:3], field[3:6], field[6:9]
        p, q = cross(x, n), cross(y, n)
        scalars = [dot3(n, [x[k] - y[k] for k in range(3)])]
        for v in range(2):
            a, b = way[6 * v : 6 * v + 6], way[12 + 3 * v : 15 + 3 * v]
            scalars.append(dot3(p, a[0:3]) + dot3(n, a[3:6]) - dot3(q, b))
        terms = []
        for s in scalars:
            terms += [s * value for value in p + n]
        for s in scalars:
            terms += [s * value for value in q]
        totals = [total + term for total, term in zip(totals, terms)]
        run(between[i * len(between) // rounds : (i + 1) * len(between) // rounds])
    for j in range(ROWS):
        partial[first + j * SUB : first + (j + 1) * SUB, :] = totals[j] if j < 27 else zero
    total = partial[pl.ds(first, ROWS, stride=SUB), :]
    for s in range(1, SUB):
        total = total + partial[pl.ds(first + s, ROWS, stride=SUB), :]
    return total


def frag_of(row, per_frag):
    return lax.shift_right_logical(row, shift_of(per_frag))


def look_up(table, frag, out):
    for at in range(0, frag.shape[1], LANE):
        index = jnp.broadcast_to(frag[:, at : at + LANE], (SUB, LANE))
        for j in range(0, 2 * SUB, SUB):
            out[j : j + SUB, at : at + LANE] = pick(table[j : j + SUB, :], index)


def by_frag(sums, frag):
    pairs = sums.shape[1]
    hot = jnp.broadcast_to(frag, (SUB, pairs)) == lax.broadcasted_iota(jnp.int32, (SUB, pairs), 0)
    return lax.dot_general(
        sums,
        hot.astype(jnp.float32),
        (((1,), (1,)), ((), ())),
        precision=lax.Precision.HIGHEST,
        preferred_element_type=jnp.float32,
    )


def target_side(total):
    rows = []
    for k in range(3):
        rows += [total[18 + 3 * k : 21 + 3 * k, :], total[6 * k + 3 : 6 * k + 6, :]]
    return -jnp.concatenate(rows, axis=0)


def constants(same, gather, place, mine):
    def wide(ref, axis):
        return lax.broadcasted_iota(jnp.int32, ref.shape, axis)

    def put(ref, hit):
        ref[...] = hit.astype(jnp.float32).astype(jnp.bfloat16)

    put(same, lax.bitwise_and(wide(same, 1), LANE - 1) == wide(same, 0))
    put(gather, lax.bitwise_and(wide(gather, 1), GROUP - 1) == wide(gather, 0))
    entry = lax.bitwise_and(wide(place, 1), GROUP - 1) + GROUP * lax.shift_right_logical(
        wide(place, 1), shift_of(LANE)
    )
    put(place, lax.bitwise_and(wide(place, 0), ROWS - 1) == entry)
    put(mine, lax.shift_right_logical(wide(mine, 1), shift_of(SUB)) == wide(mine, 0))


def local_kernel(
    points, normals, poses, directions, pairs_s, pairs_v, maps, dst_s, dst_v,
    staged, remote_b, remote_frag, totals, same, gather, place, mine,
    world, turns, table, sources, targets, side_a, side_b, joined, parts, turned, partial, *, sizes,
):
    per_frag = points.shape[1] // poses.shape[1]
    stride = points.shape[1] + SUB
    constants(same, gather, place, mine)
    table[...] = jnp.zeros_like(table)
    write_directions(directions, table)
    for at in range(0, dst_v.shape[1], LANE):
        flat = iota(1) + at
        peer = peer_at(lax.shift_right_logical(flat, shift_of(SUB)), sizes)
        block = entries(dst_v, peer * SUB + lax.bitwise_and(flat, SUB - 1))
        remote_frag[0:1, at : at + LANE] = frag_of(block, per_frag)[0:1, :]
    look_up(table, remote_frag[...], remote_b)
    frag_a, frag_b = frag_of(pairs_v[0:1, :], per_frag), frag_of(pairs_v[1:2, :], per_frag)
    look_up(table, frag_a, side_a)
    look_up(table, frag_b, side_b)
    every = slice(0, pairs_s.shape[1])
    join_directions(side_a, side_b, joined, every, every)
    write_rotations(poses, turns)
    write_world([points, normals], turns, world, range(poses.shape[1]))

    def stage_remote(g, carry):
        for s in range(SUB):
            block = dst_s[0, peer_at(g, sizes) * SUB + s]
            staged[pl.ds(g * TARGET + s, 6, stride=SUB), :] = world[pl.ds(block, 6, stride=stride), :]
        return carry

    lax.fori_loop(0, dst_s.shape[1] // SUB, stage_remote, 0, unroll=4)

    def stage_local(g, carry):
        for s in range(SUB):
            a, b = pairs_s[0, g * SUB + s], pairs_s[1, g * SUB + s]
            targets[pl.ds(g * TARGET + s, 6, stride=SUB), :] = world[pl.ds(b, 6, stride=stride), :]
            sources[pl.ds(g * SOURCE + s, 3, stride=SUB), :] = world[pl.ds(a, 3, stride=stride), :]
        return carry

    lax.fori_loop(0, pairs_s.shape[1] // SUB, stage_local, 0, unroll=4)
    total = jnp.zeros(totals.shape, jnp.float32)
    tiles = range(0, pairs_s.shape[1], LANE)
    steps = [
        field_steps(
            lambda u, k: sources[u * SOURCE + k * SUB : u * SOURCE + (k + 1) * SUB, :],
            lambda u, k: targets[u * TARGET + k * SUB : u * TARGET + (k + 1) * SUB, :],
            lambda u: maps[u * SUB : (u + 1) * SUB, :],
            same[...],
            parts,
            turned,
            t,
        )
        for t in tiles
    ]
    run(steps[0])
    for i, t in enumerate(tiles):
        between = steps[i + 1] if i + 1 < len(steps) else ()
        sums = point_sums(turned, joined, partial, t, between)
        total = total + by_frag(sums, frag_a[:, t : t + LANE])[0:18, :]
        total = total + target_side(by_frag(sums, frag_b[:, t : t + LANE]))
    totals[...] = total


def fetch_local(*refs, inputs, outputs, sizes):
    far, outs, rest = refs[:inputs], refs[inputs : inputs + outputs], refs[inputs + outputs :]
    near, scratch, sems = rest[:inputs], rest[inputs:-1], rest[-1]
    copies = [pltpu.make_async_copy(a, b, sems.at[i]) for i, (a, b) in enumerate(zip(far, near))]
    for copy in copies:
        copy.start()
    for copy in copies:
        copy.wait()
    local_kernel(*near, *outs, *scratch, sizes=sizes)


def remote_kernel(
    arrived, staged, remote_b, remote_frag, local_totals, same, gather, place, mine,
    back, totals, side_a, joined, frags, index, parts, turned, partial,
):
    f32 = jnp.float32
    pairs = parts.shape[0]
    peers = pairs // SUB
    own = lax.shift_right_logical(iota(1), shift_of(GROUP)) == iota(0)
    slot = lax.shift_right_logical(iota(1), shift_of(GROUP)).astype(f32)[0:1, :]

    def block(c, total):
        first = c * peers
        start = c * pairs if isinstance(c, int) else pl.multiple_of(c * pairs, LANE)

        def row_at(u, size, row):
            at = (first + u) * size + row
            return at if isinstance(c, int) or size == MSG else pl.multiple_of(at, SUB)

        def extras(u):
            row = arrived[pl.ds(row_at(u, MSG, 4 * SUB), 1), :]
            frags[u * SUB : (u + 1) * SUB, :] = pick(row, iota(0) * GROUP + 13)
            return jnp.where(own, jnp.broadcast_to(row, (SUB, LANE)), 0.0)

        def front(t):
            lanes = slice(t, t + LANE)

            def indices():
                for u in range(t // SUB, (t + LANE) // SUB):
                    rows = arrived[pl.ds(row_at(u, MSG, 3 * SUB), SUB), :]
                    index[u * SUB : (u + 1) * SUB, :] = rows.astype(jnp.int32)

            def put(value):
                side_a[:, lanes] = value
                join_directions(side_a, remote_b, joined, lanes, pl.ds(start + t, LANE))

            split, product = turn_steps(extras, gather[...], parts, 6, t, put)
            return (
                [indices]
                + split
                + [product]
                + field_steps(
                    lambda u, k: arrived[pl.ds(row_at(u, MSG, SUB * k), SUB), :],
                    lambda u, k: staged[pl.ds(row_at(u, TARGET, SUB * k), SUB), :],
                    lambda u: index[u * SUB : (u + 1) * SUB, :],
                    same[...],
                    parts,
                    turned,
                    t,
                )
            )

        rows = [jnp.zeros((peers, LANE), f32) for half in range(2)]

        def back_steps(sums, t):
            lanes = slice(t, t + LANE)
            held = {}
            both = jnp.concatenate(halves_of(sums), axis=0)

            def scatter():
                held["placed"] = lax.dot_general(
                    both,
                    place[...],
                    (((0,), (0,)), ((), ())),
                    preferred_element_type=f32,
                )

            def add():
                hit = frags[lanes, :] == jnp.broadcast_to(slot, (LANE, LANE))
                part = [
                    jnp.where(hit, held["placed"][:, half * LANE : (half + 1) * LANE], 0.0)
                    for half in range(2)
                ]
                pieces = jnp.concatenate(halves_of(jnp.concatenate(part, axis=1)), axis=0)
                twice = jnp.concatenate([mine[:, lanes]] * 2, axis=1)
                sent = jnp.dot(twice, pieces, preferred_element_type=f32)
                for half in range(2):
                    rows[half] = rows[half] + sent[:, half * LANE : (half + 1) * LANE]

            def own_side():
                frag = remote_frag[0:1, pl.ds(start + t, LANE)]
                hot = jnp.broadcast_to(frag, (SUB, LANE)) == iota(0)
                added = lax.dot_general(
                    both,
                    hot.astype(f32).astype(jnp.bfloat16),
                    (((1,), (1,)), ((), ())),
                    preferred_element_type=f32,
                )
                held["total"] = target_side(added[0:ROWS, :] + added[ROWS:, :])

            return [scatter, add, own_side], held

        tiles = range(0, pairs, LANE)
        steps = front(tiles[0])
        run(steps)
        behind, held = [], []
        for t in tiles:
            between = behind + (front(t + LANE) if t + LANE < pairs else [])
            sums = point_sums(turned, joined, partial, t, between)
            sums = sums * side_a[12:13, t : t + LANE]
            behind, kept = back_steps(sums, t)
            held.append(kept)
        run(behind)
        for kept in held:
            total = total + kept["total"]
        for half in range(2):
            back[pl.ds(2 * first + half, peers, stride=2), :] = rows[half]
        return total

    blocks = back.shape[0] // (2 * peers)
    total = local_totals[...]
    totals[...] = block(0, total) if blocks == 1 else lax.fori_loop(0, blocks, block, total)


def final_kernel(back, totals, gradient, hess, *, per_frag):
    devices = back.shape[0] // 2
    frags = gradient.shape[1]
    index = lax.bitwise_and(iota(1), frags - 1) * GROUP + iota(0)
    halves = []
    for half in range(2):
        tile = back[pl.ds(half, SUB, stride=2), :]
        for q in range(SUB, devices, SUB):
            tile = tile + back[pl.ds(2 * q + half, SUB, stride=2), :]
        halves.append(jnp.sum(tile, axis=0, keepdims=True))
    parts = [pick(halves[0], index), pick(halves[0], index + SUB), pick(halves[1], index)]
    total = jnp.concatenate(parts, axis=0)[0:18, 0:frags] + totals[...]
    gradient[...] = total[0:6, :] * (1.0 / LANE)
    for v in range(2):
        part = total[6 + 6 * v : 12 + 6 * v, :] * (1.0 / (LANE * per_frag))
        for j in range(6):
            hess[j, v : v + 1, :] = part[j : j + 1, :]


def call(kernel, outs, scratch, spaces, limit=VMEM_LIMIT, out_space="v", **more):
    kinds = {"v": pltpu.VMEM, "s": pltpu.SMEM, "h": pltpu.HBM}
    return pl.pallas_call(
        kernel,
        out_shape=outs,
        in_specs=[pl.BlockSpec(memory_space=kinds[s]) for s in spaces],
        out_specs=[pl.BlockSpec(memory_space=kinds[out_space])] * len(outs),
        scratch_shapes=scratch,
        compiler_params=pltpu.CompilerParams(vmem_limit_bytes=limit),
        **more,
    )


def in_hbm(values):
    return pltpu.with_memory_space_constraint(values, pltpu.HBM)


def exchange(rows, devices):
    sent = rows.reshape(devices, 1, -1)
    sent = lax.all_to_all(sent, ORDER, split_axis=0, concat_axis=0, tiled=True)
    return sent.reshape(rows.shape)


def local(
    points, normals, poses, directions, local_pairs, local_maps,
    remote_src, remote_maps, remote_dst, counts,
):
    sizes = lax.axis_size("tile"), lax.axis_size("band")
    devices = sizes[0] * sizes[1]
    blocks, _, count = points.shape
    frags = poses.shape[1]
    slots = remote_src.shape[1]
    pairs = local_pairs.shape[1]
    assert count == LANE and frags == SUB and slots == devices * SUB and devices % PEERS == 0
    per_frag = blocks // frags
    stride = blocks + SUB
    f32 = jnp.float32
    points = points.transpose(1, 0, 2)
    normals = normals.transpose(1, 0, 2)
    directions = directions.transpose(1, 0, 2)

    def array(*shape, dtype=f32):
        return jax.ShapeDtypeStruct(shape, dtype)

    def vmem(*shape, dtype=f32):
        return pltpu.VMEM(shape, dtype)

    i32, bf16 = jnp.int32, jnp.bfloat16
    part = PEERS * SUB
    (message,) = call(
        functools.partial(pack_kernel, sizes=sizes),
        [array(devices * MSG, LANE)],
        [
            vmem(3, blocks, LANE),
            pltpu.SMEM((6, frags), f32),
            vmem(6, 2, frags),
            pltpu.SMEM((1, slots), i32),
            vmem(1, slots, dtype=i32),
            vmem(slots, LANE, dtype=i32),
            vmem(1, devices, dtype=i32),
            vmem(3 * stride, LANE),
            vmem(12 * frags * SUB, LANE),
            vmem(2 * SUB, LANE),
            vmem(devices * MSG, LANE),
            pltpu.SemaphoreType.DMA((9,)),
            pltpu.SemaphoreType.DMA((devices // SUB,)),
        ],
        "hhhhhh",
        limit=PACK_LIMIT,
        out_space="h",
    )(*[in_hbm(x) for x in (points, poses, directions, remote_src, remote_maps[0], counts)])
    arrived = exchange(message, devices)
    staged, remote_b, remote_frag, totals, same, gather, place, mine = call(
        functools.partial(fetch_local, inputs=9, outputs=8, sizes=sizes),
        [
            array(devices * TARGET, LANE),
            array(2 * SUB, slots),
            array(1, slots, dtype=i32),
            array(18, frags),
            array(LANE, 2 * LANE, dtype=bf16),
            array(GROUP, 2 * LANE, dtype=bf16),
            array(2 * ROWS, 2 * LANE, dtype=bf16),
            array(PEERS, part, dtype=bf16),
        ],
        [
            vmem(3, blocks, LANE),
            vmem(3, blocks, LANE),
            pltpu.SMEM((6, frags), f32),
            vmem(6, 2, frags),
            pltpu.SMEM((2, pairs), i32),
            vmem(2, pairs, dtype=i32),
            vmem(pairs, LANE, dtype=i32),
            pltpu.SMEM((1, slots), i32),
            vmem(1, slots, dtype=i32),
            vmem(6 * stride, LANE),
            vmem(12 * frags * SUB, LANE),
            vmem(2 * SUB, LANE),
            vmem(pairs // SUB * SOURCE, LANE),
            vmem(pairs // SUB * TARGET, LANE),
            vmem(2 * SUB, pairs),
            vmem(2 * SUB, pairs),
            vmem(3 * SUB, pairs),
            vmem(pairs, 6 * 2 * LANE, dtype=bf16),
            vmem(9 * LANE, pairs),
            vmem(pairs // LANE * ROWS * SUB, LANE),
            pltpu.SemaphoreType.DMA((9,)),
        ],
        "hhhhhhhhh",
        cost_estimate=pl.CostEstimate(
            flops=200 * pairs * LANE, bytes_accessed=4_000_000, transcendentals=0
        ),
    )(
        *[
            in_hbm(x)
            for x in (
                points, normals, poses, directions, local_pairs, local_pairs, local_maps,
                remote_dst, remote_dst,
            )
        ]
    )
    back, totals = call(
        remote_kernel,
        [array(devices * 2, LANE), array(18, frags)],
        [
            vmem(2 * SUB, part),
            vmem(3 * SUB, part),
            vmem(part, LANE),
            vmem(part, LANE, dtype=i32),
            vmem(part, 7 * 2 * LANE, dtype=bf16),
            vmem(9 * LANE, part),
            vmem(part // LANE * ROWS * SUB, LANE),
        ],
        "vvvvvvvvv",
    )(arrived, staged, remote_b, remote_frag, totals, same, gather, place, mine)
    back = exchange(back, devices)
    gradient, hess = call(
        functools.partial(final_kernel, per_frag=per_frag),
        [array(6, frags), array(6, 2, frags)],
        [],
        "vv",
    )(back, totals)
    return (gradient, hess.transpose(1, 0, 2))


def solution(mesh):
    placed = (
        P(AXES, None, None),
        P(AXES, None, None),
        P(None, AXES),
        P(None, None, AXES),
        P(None, AXES),
        P(AXES, None),
        P(AXES, None),
        P(AXES, None, None),
        P(AXES, None),
        P(AXES, None),
    )
    return jax.shard_map(
        local,
        mesh=mesh,
        in_specs=placed,
        out_specs=(P(None, AXES), P(None, None, AXES)),
        check_vma=False,
    )
```
